32 devices in a mesh: batch: 2 (over core), expert: 16 (over z, y, x).
Axes of the slice: x: 2, y: 2, z: 4, core: 2. Of those that a mesh axis runs over, the one named last changes fastest.
Arguments:
- patches: bfloat16 [43520, 384], P(('batch', 'expert')), may hold values from -6 to 6
- slot_len: int32 [32, 5], P(('batch', 'expert')), may hold values from 0 to 576, as said below
- attn_weight: float32 [384, 1536], P('expert')
- attn_first: float32 [384, 1536], P('expert'), may hold values from -0.005859375 to 0.005859375
- attn_second: float32 [384, 1536], P('expert'), may hold values from 1.0850695e-06 to 4.340278e-06
- phi_weight: float32 [384, 16], P('expert'), may hold values from -0.078125 to 0.078125
- phi_first: float32 [384, 16], P('expert'), may hold values from -0.005859375 to 0.005859375
- phi_second: float32 [384, 16], P('expert'), may hold values from 1.0850695e-06 to 4.340278e-06
- norm_params: float32 [4, 384], P(None, 'expert')
- norm_first: float32 [4, 384], P(None, 'expert'), may hold values from -0.0078125 to 0.0078125
- norm_second: float32 [4, 384], P(None, 'expert'), may hold values from 1.695421e-06 to 6.781684e-06
- expert_in: float32 [16, 384, 1536], P('expert', None, 'batch'), may hold values from -2.5 to 2.5
- in_first: float32 [16, 384, 1536], P('expert', None, 'batch'), may hold values from -1.5258789e-05 to 1.5258789e-05
- in_second: float32 [16, 384, 1536], P('expert', None, 'batch'), may hold values from 6.781684e-12 to 2.7126737e-11
- expert_out: float32 [16, 1536, 384], P('expert', 'batch'), may hold values from -2.5 to 2.5
- out_first: float32 [16, 1536, 384], P('expert', 'batch'), may hold values from -2.2888184e-05 to 2.2888184e-05
- out_second: float32 [16, 1536, 384], P('expert', 'batch'), may hold values from 1.5258789e-11 to 6.1035156e-11
- cotangent: bfloat16 [43520, 384], P(('batch', 'expert')), may hold values from -6 to 6
Outputs:
- block_output: bfloat16 [43520, 384], P(('batch', 'expert'))
- input_grad: bfloat16 [43520, 384], P(('batch', 'expert'))
- grad_norm: float32 [], replicated
- attn_new: float32 [384, 1536], P('expert')
- attn_first_new: float32 [384, 1536], P('expert')
- attn_second_new: float32 [384, 1536], P('expert')
- phi_new: float32 [384, 16], P('expert')
- phi_first_new: float32 [384, 16], P('expert')
- phi_second_new: float32 [384, 16], P('expert')
- norm_new: float32 [4, 384], P(None, 'expert')
- norm_first_new: float32 [4, 384], P(None, 'expert')
- norm_second_new: float32 [4, 384], P(None, 'expert')
- in_new: float32 [16, 384, 1536], P('expert', None, 'batch')
- in_first_new: float32 [16, 384, 1536], P('expert', None, 'batch')
- in_second_new: float32 [16, 384, 1536], P('expert', None, 'batch')
- out_new: float32 [16, 1536, 384], P('expert', 'batch')
- out_first_new: float32 [16, 1536, 384], P('expert', 'batch')
- out_second_new: float32 [16, 1536, 384], P('expert', 'batch')
The draws below stay inside these ranges and needn't reach their ends.
Inputs may be any that keep to these rules, and one draw needn't show every extreme that they name: `slot_len`: row r lists the images of device r (batch index times the size of expert plus expert index) in the order in which they lie in its buffer from its first row on; every length is 196 or 576, a row holds at most one of 576 and at least one image, unused slots are 0 and come last, and the buffer rows after the last image are padding. In every draw some row holds 5 images that fill all 1360 rows.
All inputs are finite; a program needn't handle non-finite values.
Results may differ from the reference program's by a relative error of at most 0.02.
The reference program's roundings to bfloat16 on the way count: a program that leaves them out, or rounds other values in their place, can miss the bound.
Values may be sent and summed in bfloat16 or wider, within the bound.
A program may use at most 256 MiB of HBM per device.

```python
import math
from functools import partial
import jax
import jax.numpy as jnp
from jax import lax

D = 384
HEADS = 6
HEAD_DIM = 64
FF = 1536
SHORT_LEN = 196
LONG_LEN = 576
IMG_DEV = 5
STEP = 3
EXPERTS = 16
TOK_DEV = 1360
NDEV = 32
TOKENS = 43520


def draw_slot_len(key, part):
    key_long = jax.random.fold_in(key, 11)
    key_short = jax.random.fold_in(key, 12)
    key_full = jax.random.fold_in(key, 13)
    key_order = jax.random.fold_in(key, 14)
    longs = jax.random.randint(key_long, (NDEV,), 0, 2).astype(jnp.int32)
    shorts = jax.random.randint(key_short, (NDEV,), 0, 5040).astype(jnp.int32)
    shorts = 1 + shorts % (IMG_DEV - longs)
    full_row = jax.random.randint(key_full, (), 0, NDEV).astype(jnp.int32)
    is_full = jnp.arange(NDEV, dtype=jnp.int32) == full_row
    longs = jnp.where(is_full, 1, longs)
    shorts = jnp.where(is_full, IMG_DEV - 1, shorts)
    counts = longs + shorts
    long_place = jax.random.randint(key_order, (NDEV,), 0, 5040).astype(jnp.int32) % counts
    slot_index = jnp.arange(IMG_DEV, dtype=jnp.int32)[None, :]
    lengths = jnp.where(slot_index < counts[:, None], SHORT_LEN, 0)
    lengths = jnp.where((longs[:, None] == 1) & (slot_index == long_place[:, None]), LONG_LEN, lengths)
    return lengths.astype(jnp.int32)


def draw_attn_weight(key, part):
    columns = jnp.arange(4 * D)
    scales = jnp.where(columns < 2 * D, 0.6, jnp.where(columns < 3 * D, 1.0, 2.5)) / math.sqrt(D)
    base = jnp.clip(jax.random.normal(key, (D, 4 * D), jnp.float32), -5.0, 5.0)
    return (base * scales[None, :].astype(jnp.float32)).astype(jnp.float32)


def draw_norm_params(key, part):
    ramp = jnp.arange(D, dtype=jnp.float32) / D
    noise = jax.random.uniform(jax.random.fold_in(key, 21), (4, D), jnp.float32, -1.0, 1.0)
    rising = 1.0 + 2.0 * ramp
    gain_one = rising * (1.0 + 0.15 * noise[0])
    bias_one = 0.15 * noise[1]
    gain_two = rising * (1.0 + 0.15 * noise[2])
    bias_two = 0.08 * noise[3]
    return jnp.stack([gain_one, bias_one, gain_two, bias_two], axis=0).astype(jnp.float32)


def shard_levels(own_key, shape, split, least, top_value):
    level = 1.0
    for axis_at, shards_of in split:
        steps = jax.random.uniform(jax.random.fold_in(jax.random.fold_in(own_key, 6), axis_at), (shards_of,), jnp.float32, least / len(split), top_value / len(split))
        level = level * jnp.repeat(jnp.exp(steps), shape[axis_at] // shards_of).reshape((-1,) + (1,) * (len(shape) - 1 - axis_at))
    return level


def bell_draw(rng, extent, width, reach, shards=(), kind=jnp.bfloat16):
    loudness = shard_levels(rng, extent, shards, -0.22, 0.18) if shards else 1.0
    drawn = jax.random.normal(rng, extent, jnp.float32) * width * loudness
    return jnp.minimum(jnp.maximum(drawn, -reach), reach).astype(kind)


def setup_inputs(seed: int = 0) -> dict:
    arg_keys = jax.random.split(jax.random.key(seed), 19)
    patches = bell_draw(arg_keys[0], (TOKENS, D), 1.0, 6.0, ((0, 32),))
    slot_len = draw_slot_len(jax.random.fold_in(arg_keys[18], 71), 0)
    attn_weight = draw_attn_weight(jax.random.fold_in(arg_keys[18], 71), 0)
    attn_first = bell_draw(arg_keys[3], (D, 4 * D), (0.4 / D), 0.005859375, ((0, 16),), jnp.float32)
    attn_second = jnp.clip(jnp.exp(math.log(4.340277882874943e-06) - 1.3862944 * jax.random.uniform(arg_keys[4], (D, 4 * D), jnp.float32) ** shard_levels(arg_keys[4], (D, 4 * D), ((0, 16),), -0.2, 0.2)), 1.0850694707187358e-06, 4.340277882874943e-06)
    phi_weight = bell_draw(arg_keys[5], (D, EXPERTS), (0.25 / D ** 0.5), 0.078125, ((0, 16),), jnp.float32)
    phi_first = bell_draw(arg_keys[6], (D, EXPERTS), (0.4 / D), 0.005859375, ((0, 16),), jnp.float32)
    phi_second = jnp.clip(jnp.exp(math.log(4.340277882874943e-06) - 1.3862944 * jax.random.uniform(arg_keys[7], (D, EXPERTS), jnp.float32) ** shard_levels(arg_keys[7], (D, EXPERTS), ((0, 16),), -0.2, 0.2)), 1.0850694707187358e-06, 4.340277882874943e-06)
    norm_params = draw_norm_params(jax.random.fold_in(arg_keys[18], 71), 0)
    norm_first = bell_draw(arg_keys[9], (4, D), (0.5 / D), 0.0078125, ((1, 16),), jnp.float32)
    norm_second = jnp.clip(jnp.exp(math.log(6.781684078305261e-06) - 1.3862944 * jax.random.uniform(arg_keys[10], (4, D), jnp.float32) ** shard_levels(arg_keys[10], (4, D), ((1, 16),), -0.2, 0.2)), 1.6954210195763153e-06, 6.781684078305261e-06)
    expert_in = bell_draw(arg_keys[11], (EXPERTS, D, FF), (8 / D ** 0.5), 2.5, ((0, 16), (2, 2)), jnp.float32)
    in_first = bell_draw(arg_keys[12], (EXPERTS, D, FF), (0.001 / D), 1.52587890625e-05, ((0, 16), (2, 2)), jnp.float32)
    in_second = jnp.clip(jnp.exp(math.log(2.7126736620863845e-11) - 1.3862944 * jax.random.uniform(arg_keys[13], (EXPERTS, D, FF), jnp.float32) ** shard_levels(arg_keys[13], (EXPERTS, D, FF), ((0, 16), (2, 2)), -0.2, 0.2)), 6.781684155215961e-12, 2.7126736620863845e-11)
    expert_out = bell_draw(arg_keys[14], (EXPERTS, FF, D), (16 / FF ** 0.5), 2.5, ((0, 16), (1, 2)), jnp.float32)
    out_first = bell_draw(arg_keys[15], (EXPERTS, FF, D), (0.0015 / D), 2.288818359375e-05, ((0, 16), (1, 2)), jnp.float32)
    out_second = jnp.clip(jnp.exp(math.log(6.103515609590104e-11) - 1.3862944 * jax.random.uniform(arg_keys[16], (EXPERTS, FF, D), jnp.float32) ** shard_levels(arg_keys[16], (EXPERTS, FF, D), ((0, 16), (1, 2)), -0.2, 0.2)), 1.525878902397526e-11, 6.103515609590104e-11)
    cotangent = bell_draw(arg_keys[17], (TOKENS, D), 1.0, 6.0, ((0, 32),))
    return {"patches": patches, "slot_len": slot_len, "attn_weight": attn_weight, "attn_first": attn_first, "attn_second": attn_second, "phi_weight": phi_weight, "phi_first": phi_first, "phi_second": phi_second, "norm_params": norm_params, "norm_first": norm_first, "norm_second": norm_second, "expert_in": expert_in, "in_first": in_first, "in_second": in_second, "expert_out": expert_out, "out_first": out_first, "out_second": out_second, "cotangent": cotangent}


@jax.custom_vjp
def low(v):
    return lax.optimization_barrier(v.astype(jnp.bfloat16)).astype(jnp.float32)

@jax.custom_vjp
def low_back(v):
    return v

def low_keep(v):
    return (low(v), None)

def low_pass(kept, grad):
    return (grad,)

def back_keep(v):
    return (v, None)

def back_low(kept, grad):
    return (low(grad),)
low.defvjp(low_keep, low_pass)
low_back.defvjp(back_keep, back_low)
NORM_EPS = 1e-06
CLIP_NORM = 1.0
BETA_FIRST = 0.5
BETA_SECOND = 0.5
ADAM_EPS = 1e-08
WEIGHT_DECAY = 0.05
MASKED = -1e+30

def matmul(left, right):
    return jnp.dot(left, right, precision=lax.Precision.HIGHEST, preferred_element_type=jnp.float32)

def layout(lengths, tokens_count):
    image_end = jnp.cumsum(lengths, dtype=jnp.int32)
    image_start = image_end - lengths
    position = jnp.arange(tokens_count, dtype=jnp.int32)
    inside = (position[None, :] >= image_start[:, None]) & (position[None, :] < image_end[:, None])
    member = inside.astype(jnp.float32)
    validity = lax.optimization_barrier(jnp.sum(member, axis=0))
    numbers = jnp.arange(lengths.shape[0], dtype=jnp.int32)
    inside_int = inside.astype(jnp.int32)
    segment = lax.optimization_barrier(jnp.sum(inside_int * numbers[:, None], axis=0, dtype=jnp.int32))
    segment = segment + lengths.shape[0] * (1 - lax.optimization_barrier(jnp.sum(inside_int, axis=0, dtype=jnp.int32)))
    return (member, validity, segment.astype(jnp.int32))

def normalize(values, scaling, offset):
    centred = values - lax.optimization_barrier(jnp.mean(values, axis=-1, keepdims=True))
    variance = lax.optimization_barrier(jnp.mean(centred * centred, axis=-1, keepdims=True))
    inverse = lax.rsqrt(variance + NORM_EPS)
    normed = centred * inverse
    return normed * scaling + offset

def row_softmax(scores):
    row_peak = lax.optimization_barrier(jnp.max(scores, axis=-1, keepdims=True))
    exponent = jnp.exp(scores - row_peak)
    return exponent / lax.optimization_barrier(jnp.sum(exponent, axis=-1, keepdims=True))

def dispatch_weights(logits, member):
    inside = member[:, :, None] > 0.5
    col_peak = lax.optimization_barrier(jnp.max(jnp.where(inside, logits[None, :, :], MASKED), axis=1, keepdims=True))
    present = lax.optimization_barrier(jnp.max(member, axis=1))[:, None, None]
    col_peak = jnp.where(present > 0.5, col_peak, 0.0)
    exponent = jnp.where(inside, jnp.exp(jnp.where(inside, logits[None, :, :] - col_peak, 0.0)), 0.0)
    col_total = lax.optimization_barrier(jnp.sum(exponent, axis=1, keepdims=True)) + (1.0 - present)
    return exponent / col_total

def adam_update(weight, first_moment, second_moment, gradient, factor, learning_rate, decay_rate):
    clipped = gradient * factor
    first_new = BETA_FIRST * first_moment + (1.0 - BETA_FIRST) * clipped
    second_new = BETA_SECOND * second_moment + (1.0 - BETA_SECOND) * clipped * clipped
    first_hat = first_new / (1.0 - BETA_FIRST ** STEP)
    second_hat = second_new / (1.0 - BETA_SECOND ** STEP)
    weight_new = weight - learning_rate * (first_hat / (jnp.sqrt(second_hat) + ADAM_EPS) + decay_rate * weight)
    return (weight_new, first_new, second_new)

def section_one(weights, items):
    w_qkv, w_proj, phi_low, norm_low = weights
    inputs, member, segment = items
    hidden_one = low(normalize(inputs, norm_low[0], norm_low[1]))
    qkv = matmul(hidden_one, w_qkv)
    query = low_back(low(qkv[:, :D])).reshape(TOK_DEV, HEADS, HEAD_DIM)
    keys = low_back(low(qkv[:, D:2 * D])).reshape(TOK_DEV, HEADS, HEAD_DIM)
    values = low_back(low(qkv[:, 2 * D:])).reshape(TOK_DEV, HEADS, HEAD_DIM)
    scores = jnp.einsum('qhd,khd->hqk', query, keys, precision=lax.Precision.HIGHEST) * HEAD_DIM ** (-0.5)
    scores = low_back(scores)
    same = segment[:, None] == segment[None, :]
    scores = jnp.where(same[None, :, :], scores, MASKED)
    attn_probs = row_softmax(scores)
    attended = jnp.einsum('hqk,khd->qhd', low(attn_probs), values, precision=lax.Precision.HIGHEST)
    attended = low_back(low(attended.reshape(TOK_DEV, D)))
    residual = inputs + low_back(matmul(attended, w_proj))
    hidden_two = low(normalize(residual, norm_low[2], norm_low[3]))
    logits = low_back(matmul(hidden_two, phi_low))
    dispatch = dispatch_weights(logits, member)
    slot_in = jnp.einsum('kte,td->ked', low(dispatch), hidden_two, precision=lax.Precision.HIGHEST)
    slot_in = low_back(low(slot_in))
    return (residual, logits, slot_in)

def expert_one(items):
    rows, in_low, out_low = items
    pre_act = low_back(matmul(rows, in_low))
    activated = low(jax.nn.gelu(pre_act))
    return low_back(low(matmul(activated, out_low)))

def section_two(items):
    residual, logits, returned, member, validity = items
    combine = row_softmax(logits)
    mix_weights = member[:, :, None] * low(combine)[None, :, :]
    mixture = low_back(jnp.einsum('kte,ked->td', mix_weights, returned, precision=lax.Precision.HIGHEST))
    return validity[:, None] * (residual + mixture)

def reference(patches, slot_len, attn_weight, attn_first, attn_second, phi_weight, phi_first, phi_second, norm_params, norm_first, norm_second, expert_in, in_first, in_second, expert_out, out_first, out_second, cotangent):
    member_all, validity_all, segment_all = jax.vmap(lambda lengths: layout(lengths, TOK_DEV))(slot_len)

    def forward(inputs, attn_master, phi_master, norm_master, in_master, out_master):
        attn_low = low(attn_master)
        weights = (attn_low[:, :3 * D], attn_low[:, 3 * D:], low(phi_master), low(norm_master))
        residual, logits, slot_in = lax.map(jax.checkpoint(partial(section_one, weights)), (inputs, member_all, segment_all))
        expert_rows = jnp.transpose(slot_in, (2, 0, 1, 3)).reshape(EXPERTS, NDEV * IMG_DEV, D)
        results = lax.map(jax.checkpoint(expert_one), (expert_rows, low(in_master), low(out_master)))
        returned = jnp.transpose(results.reshape(EXPERTS, NDEV, IMG_DEV, D), (1, 2, 0, 3))
        return lax.map(jax.checkpoint(section_two), (residual, logits, returned, member_all, validity_all))
    inputs = patches.astype(jnp.float32).reshape(NDEV, TOK_DEV, D)
    outputs, backward = jax.vjp(forward, inputs, attn_weight, phi_weight, norm_params, expert_in, expert_out)
    grad_inputs, grad_attn, grad_phi, grad_norms, grad_in, grad_out = backward(cotangent.astype(jnp.float32).reshape(NDEV, TOK_DEV, D))
    squares = jnp.sum(grad_attn * grad_attn) + jnp.sum(grad_phi * grad_phi) + jnp.sum(grad_norms * grad_norms) + jnp.sum(grad_in * grad_in) + jnp.sum(grad_out * grad_out)
    grad_norm = jnp.sqrt(squares)
    factor = CLIP_NORM / jnp.maximum(grad_norm, CLIP_NORM)
    attn_new, attn_first_new, attn_second_new = adam_update(attn_weight, attn_first, attn_second, grad_attn, factor, 1.0 / math.sqrt(D), WEIGHT_DECAY)
    phi_new, phi_first_new, phi_second_new = adam_update(phi_weight, phi_first, phi_second, grad_phi, factor, 0.25 / math.sqrt(D), WEIGHT_DECAY)
    norm_new, norm_first_new, norm_second_new = adam_update(norm_params, norm_first, norm_second, grad_norms, factor, 0.8, 0.0)
    in_new, in_first_new, in_second_new = adam_update(expert_in, in_first, in_second, grad_in, factor, 4.0 / math.sqrt(D), WEIGHT_DECAY)
    out_new, out_first_new, out_second_new = adam_update(expert_out, out_first, out_second, grad_out, factor, 8.0 / math.sqrt(FF), WEIGHT_DECAY)
    block_output = outputs.reshape(TOKENS, D).astype(jnp.bfloat16)
    input_grad = grad_inputs.reshape(TOKENS, D).astype(jnp.bfloat16)
    return (block_output, input_grad, grad_norm, attn_new, attn_first_new, attn_second_new, phi_new, phi_first_new, phi_second_new, norm_new, norm_first_new, norm_second_new, in_new, in_first_new, in_second_new, out_new, out_first_new, out_second_new)
```

```python
import functools
import math

import jax
import jax.numpy as jnp
from jax import lax
from jax.experimental import pallas as pl
from jax.experimental.pallas import tpu as pltpu
from jax.sharding import PartitionSpec as P

D = 384
HEADS = 6
HEAD_DIM = 64
FF = 1536
STEP = 3
SHORT_LEN = 196
LONG_LEN = 576
IMAGES = 5
SLOT_ROWS = 8
PAIRS = 3
GROUPS = 16
GROUP_ROWS = D // GROUPS

NORM_EPS = 1e-06
CLIP_NORM = 1.0
BETA_FIRST = 0.5
BETA_SECOND = 0.5
ADAM_EPS = 1e-08
WEIGHT_DECAY = 0.05
MASKED = -1e30
SCORE_SCALE = HEAD_DIM ** (-0.5)

MESH = pl.DeviceIdType.MESH
F32 = jnp.float32
BF16 = jnp.bfloat16
VMEM_BYTES = 58 * 1024 * 1024


def whole(count):
    return [pl.BlockSpec(memory_space=pltpu.VMEM)] * count


def round_up(value, unit):
    return -(-value // unit) * unit


def mm(left, right):
    return jnp.dot(left, right, preferred_element_type=F32)


def mm_nt(left, right):
    return lax.dot_general(left, right, (((1,), (1,)), ((), ())), preferred_element_type=F32)


def mm_tn(left, right):
    return lax.dot_general(left, right, (((0,), (0,)), ((), ())), preferred_element_type=F32)


def gather_kernel(experts, attn_ref, small_ref, main_out, small_out, stage, send_sem, recv_sem,
                  small_send, small_recv, pair_send, pair_recv):
    core = lax.axis_index("batch")
    me = lax.axis_index("expert")
    rows = attn_ref.shape[0]
    barrier = pltpu.get_barrier_semaphore()

    @pl.loop(1, experts)
    def _(j):
        peer = lax.rem(me + j, experts)
        pl.semaphore_signal(barrier, inc=1, device_id=(core, peer), device_id_type=MESH)

    pl.semaphore_signal(barrier, inc=1, device_id=(1 - core, me), device_id_type=MESH)
    if stage.shape[0] > 2 * rows:
        stage[...] = jnp.zeros_like(stage)
    first = pl.multiple_of(core * (2 * D), 128)
    stage[0:rows, :] = attn_ref[:, pl.ds(first, D)]
    stage[rows : 2 * rows, :] = attn_ref[:, pl.ds(first + D, D)]
    main_out[me, core] = stage[...].astype(BF16)
    small_out[me] = small_ref[...]
    pl.semaphore_wait(barrier, experts)

    def main_copy(j, block, peer):
        return pltpu.make_async_remote_copy(
            src_ref=main_out.at[block, core],
            dst_ref=main_out.at[block, core],
            send_sem=send_sem.at[j],
            recv_sem=recv_sem.at[j],
            device_id=(core, peer),
            device_id_type=MESH,
        )

    def small_copy(j, block, peer):
        return pltpu.make_async_remote_copy(
            src_ref=small_out.at[block],
            dst_ref=small_out.at[block],
            send_sem=small_send.at[j],
            recv_sem=small_recv.at[j],
            device_id=(core, peer),
            device_id_type=MESH,
        )

    def pair_copy(j, block, side):
        return pltpu.make_async_remote_copy(
            src_ref=main_out.at[block, side],
            dst_ref=main_out.at[block, side],
            send_sem=pair_send.at[j],
            recv_sem=pair_recv.at[j],
            device_id=(1 - core, me),
            device_id_type=MESH,
        )

    @pl.loop(1, experts)
    def _(j):
        peer = lax.rem(me + j, experts)
        main_copy(j, me, peer).start()
        small_copy(j, me, peer).start()

    pair_copy(0, me, core).start()

    @pl.loop(1, experts)
    def _(j):
        source = lax.rem(me - j + experts, experts)
        main_copy(j, source, source).wait_recv()
        pair_copy(j, source, core).start()

    @pl.loop(1, experts)
    def _(j):
        source = lax.rem(me - j + experts, experts)
        small_copy(j, source, source).wait_recv()
        main_copy(j, me, source).wait_send()
        small_copy(j, me, source).wait_send()

    @pl.loop(0, experts)
    def _(j):
        source = lax.rem(me - j + experts, experts)
        pair_copy(j, source, core).wait_send()
        pair_copy(j, source, 1 - core).wait_recv()


def gather_weights(attn_weight, small, experts):
    rows = attn_weight.shape[0]
    main_rows = round_up(2 * rows, 16)
    return pl.pallas_call(
        functools.partial(gather_kernel, experts),
        out_shape=(
            jax.ShapeDtypeStruct((experts, 2, main_rows, D), BF16),
            jax.ShapeDtypeStruct((experts,) + small.shape, BF16),
        ),
        in_specs=whole(2),
        out_specs=tuple(whole(2)),
        scratch_shapes=[pltpu.VMEM((main_rows, D), F32)]
        + [pltpu.SemaphoreType.DMA((experts,))] * 6,
        compiler_params=pltpu.CompilerParams(
            collective_id=0, has_side_effects=True, vmem_limit_bytes=VMEM_BYTES
        ),
        name="gather_weights",
    )(attn_weight, small)


def unpack_weight(main_ref, side, part):
    block = main_ref[:, side].astype(F32)[:, part * GROUP_ROWS : (part + 1) * GROUP_ROWS, :]
    return block.reshape(D, D).astype(BF16)


def unpack_small(small_ref, experts):
    lanes = small_ref.shape[2]
    columns = experts * SLOT_ROWS
    values = small_ref[...].astype(F32)[:, :GROUP_ROWS, :].reshape(D, lanes).astype(BF16)
    row = lax.broadcasted_iota(jnp.int32, (lanes, columns), 0)
    column = lax.broadcasted_iota(jnp.int32, (lanes, columns), 1)
    spread = jnp.where(row == column // SLOT_ROWS, 1.0, 0.0).astype(BF16)
    phi = mm(values, spread).astype(BF16)
    row = lax.broadcasted_iota(jnp.int32, (8, lanes), 0)
    column = lax.broadcasted_iota(jnp.int32, (8, lanes), 1)
    pick = jnp.where(column == row + experts, 1.0, 0.0).astype(BF16)
    return phi, mm_nt(pick, values)


def slot_bounds(len_ref, columns):
    image = lax.broadcasted_iota(jnp.int32, (1, columns), 1) % SLOT_ROWS
    starts = jnp.zeros((1, columns), jnp.int32)
    ends = jnp.zeros((1, columns), jnp.int32)
    start = jnp.int32(0)
    for k in range(IMAGES):
        end = start + len_ref[0, k]
        starts = jnp.where(image == k, start, starts)
        ends = jnp.where(image == k, end, ends)
        start = end
    return starts, ends, start


def normed(values):
    centred = values - jnp.mean(values, axis=-1, keepdims=True)
    variance = jnp.mean(centred * centred, axis=-1, keepdims=True)
    inverse = lax.rsqrt(variance + NORM_EPS)
    return centred * inverse, inverse


def norm_back(grad_shaped, normal, inverse, scaling):
    grad_normal = grad_shaped * scaling
    return inverse * (
        grad_normal
        - jnp.mean(grad_normal, axis=-1, keepdims=True)
        - normal * jnp.mean(grad_normal * normal, axis=-1, keepdims=True)
    )


def over_images(len_ref, tokens, body):
    def step(k, start):
        length = len_ref[0, k]
        for full in (SHORT_LEN, LONG_LEN):

            @pl.when(length == full)
            def _():
                window = round_up(full + 12, 16)
                first = jnp.minimum((start // 16) * 16, tokens - window)
                body(pl.multiple_of(first, 16), start - first, full, window)

        return start + length

    lax.fori_loop(0, IMAGES, step, jnp.int32(0))


def window_masks(shift, full, window):
    column = lax.broadcasted_iota(jnp.int32, (1, window), 1)
    row = lax.broadcasted_iota(jnp.int32, (window, 1), 0)
    bias = jnp.where((column >= shift) & (column < shift + full), 0.0, MASKED)
    inside = (row >= shift) & (row < shift + full)
    return bias, inside


def forward_kernel(experts, len_ref, patch_ref, main_ref, small_ref, cot_ref, qkv_ref, o_ref,
                   lse_ref, x1_ref, h2_ref, disp_ref, comb_ref, gy_ref, pack_ref, logit, packf):
    tokens = patch_ref.shape[0]
    columns = experts * SLOT_ROWS
    tile = tokens // 5
    phi, norms = unpack_small(small_ref, experts)
    starts, ends, total = slot_bounds(len_ref, columns)
    w_q, w_k = unpack_weight(main_ref, 0, 0), unpack_weight(main_ref, 0, 1)
    w_v = unpack_weight(main_ref, 1, 0)
    w_qkv = jnp.concatenate([w_q, w_k, w_v], axis=1)
    for t in range(5):
        rows = pl.ds(t * tile, tile)
        normal, _ = normed(patch_ref[rows, :].astype(F32))
        h1 = (normal * norms[0:1] + norms[1:2]).astype(BF16)
        qkv = mm(h1, w_qkv).astype(BF16)
        for c in range(9):
            qkv_ref[c, rows, :] = qkv[:, c * 128 : (c + 1) * 128]
    o_ref[...] = jnp.zeros_like(o_ref)
    lse_ref[...] = jnp.zeros_like(lse_ref)
    low_lane = lax.broadcasted_iota(jnp.int32, (1, 128), 1) < HEAD_DIM
    lane = lax.broadcasted_iota(jnp.int32, (1, 128), 1)

    def attend(first, shift, full, window):
        bias, inside = window_masks(shift, full, window)
        rows = pl.ds(first, window)

        @pl.loop(0, PAIRS)
        def _(p):
            query = qkv_ref[p, rows, :].astype(F32) * SCORE_SCALE
            keys = qkv_ref[PAIRS + p, rows, :]
            values = qkv_ref[2 * PAIRS + p, rows, :]
            outs = []
            sums = lse_ref[rows, :]
            for h in range(2):
                mine = low_lane if h == 0 else jnp.logical_not(low_lane)
                scores = mm_nt(jnp.where(mine, query, 0.0).astype(BF16), keys) + bias
                peak = jnp.max(scores, axis=-1, keepdims=True)
                exponent = jnp.exp(scores - peak)
                summed = jnp.sum(exponent, axis=-1, keepdims=True)
                probs = (exponent * (1.0 / summed)).astype(BF16)
                outs.append(mm(probs, values))
                sums = jnp.where(inside & (lane == 2 * p + h), peak + jnp.log(summed), sums)
            lse_ref[rows, :] = sums
            lanes = pl.ds(pl.multiple_of(p * 128, 128), 128)
            old = o_ref[rows, lanes].astype(F32)
            merged = jnp.where(inside, jnp.where(low_lane, outs[0], outs[1]), old)
            o_ref[rows, lanes] = merged.astype(BF16)

    over_images(len_ref, tokens, attend)

    w_o = unpack_weight(main_ref, 1, 1)
    for t in range(5):
        rows = pl.ds(t * tile, tile)
        x1 = patch_ref[rows, :].astype(F32) + mm(o_ref[rows, :], w_o)
        normal, _ = normed(x1)
        h2 = (normal * norms[2:3] + norms[3:4]).astype(BF16)
        h2_ref[rows, :] = h2
        logit[rows, :] = mm(h2, phi)
        position = t * tile + lax.broadcasted_iota(jnp.int32, (tile, 1), 0)
        valid = position < total
        x1_ref[rows, :] = jnp.where(valid, x1, 0.0)
        gy_ref[rows, :] = jnp.where(valid, cot_ref[rows, :].astype(F32), 0.0).astype(BF16)

    position = lax.broadcasted_iota(jnp.int32, (tokens, columns), 0)
    member = (position >= starts) & (position < ends)
    present = ends > starts
    logits = logit[...]
    peak = jnp.max(jnp.where(member, logits, MASKED), axis=0, keepdims=True)
    peak = jnp.where(present, peak, 0.0)
    exponent = jnp.where(member, jnp.exp(jnp.where(member, logits - peak, 0.0)), 0.0)
    summed = jnp.sum(exponent, axis=0, keepdims=True) + jnp.where(present, 0.0, 1.0)
    dispatch = exponent / summed
    disp_ref[...] = dispatch
    slots = mm_tn(dispatch.astype(BF16), h2_ref[...])
    row_peak = jnp.max(logits, axis=-1, keepdims=True)
    exponent = jnp.exp(logits - row_peak)
    summed = jnp.sum(exponent, axis=-1, keepdims=True) * (1.0 / SLOT_ROWS)
    combine = jnp.where(member, exponent / summed, 0.0)
    comb_ref[...] = combine
    grad_result = mm_tn(combine.astype(BF16), gy_ref[...])
    for part, matrix in enumerate((slots, grad_result)):
        pack_rows(packf, matrix.reshape(experts, SLOT_ROWS, D))
        pack_ref[:, part * 16 : (part + 1) * 16, :] = packf[...].astype(BF16)


def pack_rows(packf, blocks):
    packf[...] = jnp.zeros_like(packf)
    for c in range(3):
        packf[:, c * IMAGES : (c + 1) * IMAGES, :] = blocks[:, :IMAGES, c * 128 : (c + 1) * 128]


def unpack_rows(packf, wide):
    wide[...] = jnp.zeros_like(wide)
    for c in range(3):
        wide[:, 0:IMAGES, c * 128 : (c + 1) * 128] = packf[:, c * IMAGES : (c + 1) * IMAGES, :]


def forward_local(lengths, patches, main, small, cotangent, experts):
    tokens = patches.shape[0]
    columns = experts * SLOT_ROWS
    shape = jax.ShapeDtypeStruct
    return pl.pallas_call(
        functools.partial(forward_kernel, experts),
        out_shape=(
            shape((9, tokens, 128), BF16),
            shape((tokens, D), BF16),
            shape((tokens, 128), F32),
            shape((tokens, D), F32),
            shape((tokens, D), BF16),
            shape((tokens, columns), F32),
            shape((tokens, columns), F32),
            shape((tokens, D), BF16),
            shape((experts, 32, 128), BF16),
        ),
        in_specs=[pl.BlockSpec(memory_space=pltpu.SMEM)] + whole(4),
        out_specs=tuple(whole(9)),
        scratch_shapes=[pltpu.VMEM((tokens, columns), F32), pltpu.VMEM((experts, 16, 128), F32)],
        compiler_params=pltpu.CompilerParams(vmem_limit_bytes=VMEM_BYTES),
        name="forward_local",
    )(lengths, patches, main, small, cotangent)


def expert_kernel(experts, pack_ref, in_ref, out_ref, result_ref, gslot_ref, gin_ref, gout_ref,
                  square_ref, inbox, outbox, back, packf, wide, packe, widee, send_one, recv_one,
                  send_two, recv_two):
    core = lax.axis_index("batch")
    chip = lax.axis_index("expert")
    devices = 2 * experts
    me = core * experts + chip
    barrier = pltpu.get_barrier_semaphore()

    @pl.loop(1, devices)
    def _(j):
        peer = lax.rem(me + j, devices)
        pl.semaphore_signal(
            barrier, inc=1, device_id=(peer // experts, lax.rem(peer, experts)), device_id_type=MESH
        )

    w_in = in_ref[0].astype(BF16)
    w_out = out_ref[0].astype(BF16)
    inbox[me] = pack_ref[chip]
    pl.semaphore_wait(barrier, devices - 1)

    def first(j, peer):
        return pltpu.make_async_remote_copy(
            src_ref=pack_ref.at[lax.rem(peer, experts)],
            dst_ref=inbox.at[me],
            send_sem=send_one.at[j],
            recv_sem=recv_one.at[j],
            device_id=(peer // experts, lax.rem(peer, experts)),
            device_id_type=MESH,
        )

    def first_arrival(j, peer):
        return pltpu.make_async_remote_copy(
            src_ref=pack_ref.at[lax.rem(peer, experts)],
            dst_ref=inbox.at[peer],
            send_sem=send_one.at[j],
            recv_sem=recv_one.at[j],
            device_id=(peer // experts, lax.rem(peer, experts)),
            device_id_type=MESH,
        )

    def second(j, peer):
        return pltpu.make_async_remote_copy(
            src_ref=outbox.at[peer],
            dst_ref=back.at[me],
            send_sem=send_two.at[j],
            recv_sem=recv_two.at[j],
            device_id=(peer // experts, lax.rem(peer, experts)),
            device_id_type=MESH,
        )

    def second_arrival(j, peer):
        return pltpu.make_async_remote_copy(
            src_ref=outbox.at[peer],
            dst_ref=back.at[peer],
            send_sem=send_two.at[j],
            recv_sem=recv_two.at[j],
            device_id=(peer // experts, lax.rem(peer, experts)),
            device_id_type=MESH,
        )

    @pl.loop(1, devices)
    def _(j):
        first(j, lax.rem(me + j, devices)).start()

    @pl.loop(1, devices)
    def _(j):
        first_arrival(j, lax.rem(me - j + devices, devices)).wait_recv()

    rows = devices * SLOT_ROWS
    packf[...] = inbox[:, 0:16, :].astype(F32)
    unpack_rows(packf, wide)
    slots = wide[...].reshape(rows, D).astype(BF16)
    packf[...] = inbox[:, 16:32, :].astype(F32)
    unpack_rows(packf, wide)
    grads = wide[...].reshape(rows, D).astype(BF16)

    hidden = mm(slots, w_in)
    cubed = hidden * hidden * hidden
    root = math.sqrt(2.0 / math.pi)
    bent = jnp.tanh(root * (hidden + 0.044715 * cubed))
    half = 0.5 * (1.0 + bent)
    act = (hidden * half).astype(BF16)
    slope = half + 0.5 * hidden * (1.0 - bent * bent) * (
        root * (1.0 + 3.0 * 0.044715 * (hidden * hidden))
    )
    result = mm(act, w_out)
    pack_rows(packf, result.reshape(devices, SLOT_ROWS, D))
    outbox[:, 0:16, :] = packf[...].astype(BF16)
    grad_hidden = (mm_nt(grads, w_out) * slope).astype(BF16)
    grad_slots = mm_nt(grad_hidden, w_in)
    pack_rows(packf, grad_slots.reshape(devices, SLOT_ROWS, D))
    outbox[:, 16:32, :] = packf[...].astype(BF16)
    back[me] = outbox[me]

    @pl.loop(1, devices)
    def _(j):
        second(j, lax.rem(me + j, devices)).start()

    grad_out = mm_tn(act, grads)
    gout_ref[0] = grad_out
    grad_in = mm_tn(slots, grad_hidden)
    gin_ref[0] = grad_in
    squares = jnp.sum(grad_out * grad_out) + jnp.sum(grad_in * grad_in)
    square_ref[...] = jnp.full(square_ref.shape, squares, F32)

    @pl.loop(1, devices)
    def _(j):
        second_arrival(j, lax.rem(me - j + devices, devices)).wait_recv()

    for part, target in enumerate((result_ref, gslot_ref)):
        block = slice(part * 16, (part + 1) * 16)
        both = back[0:experts, block, :].astype(F32) + back[experts:devices, block, :].astype(F32)
        packe[...] = both.astype(BF16).astype(F32)
        unpack_rows(packe, widee)
        target[...] = widee[...].reshape(experts * SLOT_ROWS, D).astype(BF16)

    @pl.loop(1, devices)
    def _(j):
        peer = lax.rem(me + j, devices)
        first(j, peer).wait_send()
        second(j, peer).wait_send()


def run_experts(packed, expert_in, expert_out, experts):
    devices = 2 * experts
    shape = jax.ShapeDtypeStruct
    return pl.pallas_call(
        functools.partial(expert_kernel, experts),
        out_shape=(
            shape((experts * SLOT_ROWS, D), BF16),
            shape((experts * SLOT_ROWS, D), BF16),
            shape(expert_in.shape, F32),
            shape(expert_out.shape, F32),
            shape((8, 128), F32),
        ),
        in_specs=whole(3),
        out_specs=tuple(whole(5)),
        scratch_shapes=[
            pltpu.VMEM((devices, 32, 128), BF16),
            pltpu.VMEM((devices, 32, 128), BF16),
            pltpu.VMEM((devices, 32, 128), BF16),
            pltpu.VMEM((devices, 16, 128), F32),
            pltpu.VMEM((devices, SLOT_ROWS, D), F32),
            pltpu.VMEM((experts, 16, 128), F32),
            pltpu.VMEM((experts, SLOT_ROWS, D), F32),
        ]
        + [pltpu.SemaphoreType.DMA((devices,))] * 4,
        compiler_params=pltpu.CompilerParams(
            collective_id=1, has_side_effects=True, vmem_limit_bytes=VMEM_BYTES
        ),
        name="run_experts",
    )(packed, expert_in, expert_out)


def backward_kernel(experts, len_ref, patch_ref, main_ref, small_ref, qkv_ref, o_ref, lse_ref,
                    x1_ref, h2_ref, disp_ref, comb_ref, gy_ref, result_ref, gslot_ref, block_ref,
                    input_ref, gw_ref, gphi_ref, gnorm_ref, gdisp, glog, gx1, branch, go, gqkv,
                    h1_all):
    tokens = patch_ref.shape[0]
    columns = experts * SLOT_ROWS
    tile = tokens // 5
    phi, norms = unpack_small(small_ref, experts)
    result = result_ref[...]
    gslots = gslot_ref[...]

    inner = jnp.zeros((1, columns), F32)
    for t in range(5):
        rows = pl.ds(t * tile, tile)
        grad_dispatch = mm_nt(h2_ref[rows, :], gslots)
        gdisp[rows, :] = grad_dispatch
        inner = inner + jnp.sum(disp_ref[rows, :] * grad_dispatch, axis=0, keepdims=True)

    w_o = unpack_weight(main_ref, 1, 1)
    gain_two = jnp.zeros((1, D), F32)
    bias_two = jnp.zeros((1, D), F32)
    for t in range(5):
        rows = pl.ds(t * tile, tile)
        dispatch, combine, gy = disp_ref[rows, :], comb_ref[rows, :], gy_ref[rows, :]
        x1 = x1_ref[rows, :]
        mixed = mm(combine.astype(BF16), result)
        block_ref[rows, :] = (x1 + mixed).astype(BF16)
        weighted = combine * mm_nt(gy, result)
        grad_logits = (
            weighted
            - combine * jnp.sum(weighted, axis=-1, keepdims=True)
            + dispatch * (gdisp[rows, :] - inner)
        ).astype(BF16)
        glog[rows, :] = grad_logits
        grad_h2 = mm(dispatch.astype(BF16), gslots) + mm_nt(grad_logits, phi)
        normal, inverse = normed(x1)
        gain_two = gain_two + jnp.sum(grad_h2 * normal, axis=0, keepdims=True)
        bias_two = bias_two + jnp.sum(grad_h2, axis=0, keepdims=True)
        grad_x1 = gy.astype(F32) + norm_back(grad_h2, normal, inverse, norms[2:3])
        gx1[rows, :] = grad_x1
        grad_branch = grad_x1.astype(BF16)
        branch[rows, :] = grad_branch
        grad_o = mm_nt(grad_branch, w_o).astype(BF16)
        for c in range(PAIRS):
            go[c, rows, :] = grad_o[:, c * 128 : (c + 1) * 128]

    lanes = gphi_ref.shape[1]
    row = lax.broadcasted_iota(jnp.int32, (columns, lanes), 0)
    column = lax.broadcasted_iota(jnp.int32, (columns, lanes), 1)
    fold = jnp.where(column == row // SLOT_ROWS, 1.0, 0.0).astype(BF16)
    folded = mm(glog[...], fold).astype(BF16)
    gphi_ref[...] = mm_tn(h2_ref[...], folded)

    def put(side, part, value):
        gw_ref[side, :, part * GROUP_ROWS : (part + 1) * GROUP_ROWS, :] = value.reshape(
            GROUPS, GROUP_ROWS, D
        )

    put(1, 1, mm_tn(o_ref[...], branch[...]))

    gqkv[...] = jnp.zeros_like(gqkv)
    low_lane = lax.broadcasted_iota(jnp.int32, (1, 128), 1) < HEAD_DIM
    lane = lax.broadcasted_iota(jnp.int32, (1, 128), 1)

    def attend(first, shift, full, window):
        bias, inside = window_masks(shift, full, window)
        rows = pl.ds(first, window)
        sums = lse_ref[rows, :]

        @pl.loop(0, PAIRS)
        def _(p):
            query_low = qkv_ref[p, rows, :]
            query = query_low.astype(F32) * SCORE_SCALE
            keys = qkv_ref[PAIRS + p, rows, :]
            values = qkv_ref[2 * PAIRS + p, rows, :]
            grads_low = go[p, rows, :]
            grads = grads_low.astype(F32)
            parts = []
            for h in range(2):
                mine = low_lane if h == 0 else jnp.logical_not(low_lane)
                scores = mm_nt(jnp.where(mine, query, 0.0).astype(BF16), keys) + bias
                summed = jnp.sum(jnp.where(lane == 2 * p + h, sums, 0.0), axis=-1, keepdims=True)
                probs = jnp.exp(scores - jnp.where(inside, summed, 1e30))
                grad_probs = mm_nt(jnp.where(mine, grads, 0.0).astype(BF16), values)
                dot = jnp.sum(probs * grad_probs, axis=-1, keepdims=True)
                grad_scores = (probs * (grad_probs - dot)).astype(BF16)
                parts.append(
                    (
                        mm(grad_scores, keys) * SCORE_SCALE,
                        mm_tn(grad_scores, query_low) * SCORE_SCALE,
                        mm_tn(probs.astype(BF16), grads_low),
                    )
                )
            for c in range(3):
                old = gqkv[c * PAIRS + p, rows, :].astype(F32)
                new = jnp.where(low_lane, parts[0][c], parts[1][c])
                gqkv[c * PAIRS + p, rows, :] = jnp.where(inside, new, old).astype(BF16)

    over_images(len_ref, tokens, attend)

    w_q, w_k = unpack_weight(main_ref, 0, 0), unpack_weight(main_ref, 0, 1)
    w_v = unpack_weight(main_ref, 1, 0)
    w_qkv = jnp.concatenate([w_q, w_k, w_v], axis=1)
    gain_one = jnp.zeros((1, D), F32)
    bias_one = jnp.zeros((1, D), F32)
    for t in range(5):
        rows = pl.ds(t * tile, tile)
        grad_qkv = jnp.concatenate([gqkv[c, rows, :] for c in range(9)], axis=1)
        grad_h1 = mm_nt(grad_qkv, w_qkv)
        normal, inverse = normed(patch_ref[rows, :].astype(F32))
        h1_all[rows, :] = (normal * norms[0:1] + norms[1:2]).astype(BF16)
        gain_one = gain_one + jnp.sum(grad_h1 * normal, axis=0, keepdims=True)
        bias_one = bias_one + jnp.sum(grad_h1, axis=0, keepdims=True)
        grad_x = gx1[rows, :] + norm_back(grad_h1, normal, inverse, norms[0:1])
        input_ref[rows, :] = grad_x.astype(BF16)
    for c, (side, part) in enumerate(((0, 0), (0, 1), (1, 0))):
        grad = jnp.concatenate([gqkv[c * PAIRS + p] for p in range(PAIRS)], axis=1)
        put(side, part, mm_tn(h1_all[...], grad))
    gnorm_ref[...] = jnp.concatenate(
        [gain_one, bias_one, gain_two, bias_two, jnp.zeros((4, D), F32)], axis=0
    )


def backward_local(lengths, patches, main, small, saved, result, gslots, experts):
    tokens = patches.shape[0]
    columns = experts * SLOT_ROWS
    shape = jax.ShapeDtypeStruct
    return pl.pallas_call(
        functools.partial(backward_kernel, experts),
        out_shape=(
            shape((tokens, D), BF16),
            shape((tokens, D), BF16),
            shape((2, GROUPS, 2 * GROUP_ROWS, D), F32),
            shape((D, round_up(experts, 128)), F32),
            shape((8, D), F32),
        ),
        in_specs=[pl.BlockSpec(memory_space=pltpu.SMEM)] + whole(13),
        out_specs=tuple(whole(5)),
        scratch_shapes=[
            pltpu.VMEM((tokens, columns), F32),
            pltpu.VMEM((tokens, columns), BF16),
            pltpu.VMEM((tokens, D), F32),
            pltpu.VMEM((tokens, D), BF16),
            pltpu.VMEM((PAIRS, tokens, 128), BF16),
            pltpu.VMEM((9, tokens, 128), BF16),
            pltpu.VMEM((tokens, D), BF16),
        ],
        compiler_params=pltpu.CompilerParams(vmem_limit_bytes=VMEM_BYTES),
        name="backward_local",
    )(lengths, patches, main, small, *saved, result, gslots)


def reduce_kernel(experts, gw_ref, gs_ref, square_ref, main_out, small_out, norm_ref, pair_in,
                  pair_small, box, small_box, inbox, small_in, scalars, pair_send, pair_recv,
                  pair_small_send, pair_small_recv, send_sem, recv_sem, small_send, small_recv,
                  swap_sem, norm_send, norm_recv):
    core = lax.axis_index("batch")
    chip = lax.axis_index("expert")
    devices = 2 * experts
    me = core * experts + chip
    barrier = pltpu.get_barrier_semaphore()

    @pl.loop(1, devices)
    def _(j):
        peer = lax.rem(me + j, devices)
        pl.semaphore_signal(
            barrier, inc=1, device_id=(peer // experts, lax.rem(peer, experts)), device_id_type=MESH
        )

    pl.semaphore_wait(barrier, devices - 1)

    def pair_copy(target):
        return pltpu.make_async_remote_copy(
            src_ref=gw_ref.at[1 - core, target],
            dst_ref=pair_in.at[target],
            send_sem=pair_send.at[target],
            recv_sem=pair_recv.at[target],
            device_id=(1 - core, chip),
            device_id_type=MESH,
        )

    def pair_small_copy(target):
        return pltpu.make_async_remote_copy(
            src_ref=gs_ref.at[target],
            dst_ref=pair_small.at[target],
            send_sem=pair_small_send.at[target],
            recv_sem=pair_small_recv.at[target],
            device_id=(1 - core, chip),
            device_id_type=MESH,
        )

    def main_copy(j, block, peer):
        return pltpu.make_async_remote_copy(
            src_ref=box.at[peer],
            dst_ref=inbox.at[block],
            send_sem=send_sem.at[j],
            recv_sem=recv_sem.at[j],
            device_id=(core, peer),
            device_id_type=MESH,
        )

    def small_copy(j, block, peer):
        return pltpu.make_async_remote_copy(
            src_ref=small_box.at[peer],
            dst_ref=small_in.at[block],
            send_sem=small_send.at[j],
            recv_sem=small_recv.at[j],
            device_id=(core, peer),
            device_id_type=MESH,
        )

    @pl.loop(1, experts + 1)
    def _(j):
        target = lax.rem(chip + j, experts)
        pair_copy(target).start()
        pair_small_copy(target).start()

    @pl.loop(1, experts)
    def _(j):
        target = lax.rem(chip + j, experts)
        pair_copy(target).wait_recv()
        box[target] = (gw_ref[core, target] + pair_in[target]).astype(BF16)
        main_copy(j, chip, target).start()
        pair_small_copy(target).wait_recv()
        small_box[target] = (gs_ref[target] + pair_small[target]).astype(BF16)
        small_copy(j, chip, target).start()

    pair_copy(chip).wait_recv()
    pair_small_copy(chip).wait_recv()
    main_out[core] = gw_ref[core, chip] + pair_in[chip]
    small_out[...] = gs_ref[chip] + pair_small[chip]

    @pl.loop(1, experts)
    def _(j):
        source = lax.rem(chip - j + experts, experts)
        main_copy(j, source, source).wait_recv()
        main_out[core] += inbox[source].astype(F32)
        small_copy(j, source, source).wait_recv()
        small_out[...] += small_in[source].astype(F32)

    def swap(side):
        return pltpu.make_async_remote_copy(
            src_ref=main_out.at[side],
            dst_ref=main_out.at[side],
            send_sem=swap_sem.at[0],
            recv_sem=swap_sem.at[1],
            device_id=(1 - core, chip),
            device_id_type=MESH,
        )

    swap(core).start()
    own = main_out[core]
    shared = small_out[...]
    small_square = jnp.where(core == 0, jnp.sum(shared * shared), 0.0)
    squares = jnp.sum(own * own) + small_square
    scalars[me] = square_ref[...] + squares

    def norm_copy(j, block, peer):
        return pltpu.make_async_remote_copy(
            src_ref=scalars.at[block],
            dst_ref=scalars.at[block],
            send_sem=norm_send.at[j],
            recv_sem=norm_recv.at[j],
            device_id=(peer // experts, lax.rem(peer, experts)),
            device_id_type=MESH,
        )

    @pl.loop(1, devices)
    def _(j):
        norm_copy(j, me, lax.rem(me + j, devices)).start()

    @pl.loop(1, devices)
    def _(j):
        source = lax.rem(me - j + devices, devices)
        norm_copy(j, source, source).wait_recv()

    norm_ref[...] = jnp.sqrt(jnp.sum(scalars[...], axis=0))
    swap(1 - core).wait_recv()
    swap(core).wait_send()

    @pl.loop(1, experts + 1)
    def _(j):
        target = lax.rem(chip + j, experts)
        pair_copy(target).wait_send()
        pair_small_copy(target).wait_send()

    @pl.loop(1, experts)
    def _(j):
        target = lax.rem(chip + j, experts)
        main_copy(j, chip, target).wait_send()
        small_copy(j, chip, target).wait_send()

    @pl.loop(1, devices)
    def _(j):
        norm_copy(j, me, lax.rem(me + j, devices)).wait_send()


def reduce_grads(main, small, squares, experts):
    devices = 2 * experts
    block = main.shape[2:]
    part = small.shape[1:]
    shape = jax.ShapeDtypeStruct
    dma = pltpu.SemaphoreType.DMA
    return pl.pallas_call(
        functools.partial(reduce_kernel, experts),
        out_shape=(shape((2,) + block, F32), shape(part, F32), shape((8, 128), F32)),
        in_specs=whole(3),
        out_specs=tuple(whole(3)),
        scratch_shapes=[
            pltpu.VMEM((experts,) + block, F32),
            pltpu.VMEM((experts,) + part, F32),
            pltpu.VMEM((experts,) + block, BF16),
            pltpu.VMEM((experts,) + part, BF16),
            pltpu.VMEM((experts,) + block, BF16),
            pltpu.VMEM((experts,) + part, BF16),
            pltpu.VMEM((devices, 8, 128), F32),
        ]
        + [dma((experts,))] * 8
        + [dma((2,)), dma((devices,)), dma((devices,))],
        compiler_params=pltpu.CompilerParams(
            collective_id=2, has_side_effects=True, vmem_limit_bytes=VMEM_BYTES
        ),
        name="reduce_grads",
    )(main, small, squares)


def adam_update(weight, first_moment, second_moment, gradient, factor, learning_rate, decay_rate):
    clipped = gradient * factor
    first_new = BETA_FIRST * first_moment + (1.0 - BETA_FIRST) * clipped
    second_new = BETA_SECOND * second_moment + (1.0 - BETA_SECOND) * clipped * clipped
    first_hat = first_new / (1.0 - BETA_FIRST**STEP)
    second_hat = second_new / (1.0 - BETA_SECOND**STEP)
    weight_new = weight - learning_rate * (
        first_hat / (jnp.sqrt(second_hat) + ADAM_EPS) + decay_rate * weight
    )
    return (weight_new, first_new, second_new)


def pad_to(array, shape):
    return jnp.pad(array, [(0, full - size) for size, full in zip(array.shape, shape)])


def regroup_weights(main, small, experts):
    rows = D // experts
    if rows == GROUP_ROWS:
        return main, small
    lanes = small.shape[2]
    main = main[:, :, : 2 * rows].reshape(experts, 2, 2, rows, D).transpose(1, 2, 0, 3, 4)
    main = main.reshape(2, 2, GROUPS, GROUP_ROWS, D).transpose(2, 0, 1, 3, 4)
    small = small[:, :rows].reshape(GROUPS, GROUP_ROWS, lanes)
    return main.reshape(GROUPS, 2, 2 * GROUP_ROWS, D), pad_to(small, (GROUPS, 32, lanes))


def regroup_grads(main, small_rows, experts):
    rows = D // experts
    lanes = small_rows.shape[1]
    block_rows = round_up(rows, 16)
    small = pad_to(small_rows.reshape(experts, rows, lanes), (experts, block_rows, lanes))
    if rows == GROUP_ROWS:
        return main, small
    main = main.reshape(2, GROUPS, 2, GROUP_ROWS, D).transpose(0, 2, 1, 3, 4)
    main = main.reshape(2, 2, experts, rows, D).transpose(0, 2, 1, 3, 4)
    main = main.reshape(2, experts, 2 * rows, D)
    return pad_to(main, (2, experts, round_up(2 * rows, 16), D)), small


def local(
    patches,
    slot_len,
    attn_weight,
    attn_first,
    attn_second,
    phi_weight,
    phi_first,
    phi_second,
    norm_params,
    norm_first,
    norm_second,
    expert_in,
    in_first,
    in_second,
    expert_out,
    out_first,
    out_second,
    cotangent,
):
    experts = lax.axis_size("expert")
    rows = attn_weight.shape[0]
    lanes = round_up(experts + 4, 128)
    small = jnp.concatenate([phi_weight, norm_params.T], axis=1).astype(BF16)
    small = pad_to(small, (round_up(rows, 16), lanes))
    main, small = gather_weights(attn_weight, small, experts)
    main, small = regroup_weights(main, small, experts)
    *saved, packed = forward_local(slot_len, patches, main, small, cotangent, experts)
    result, gslots, grad_in, grad_out, squares = run_experts(packed, expert_in, expert_out, experts)
    block_output, input_grad, grad_main, grad_phi, grad_norms = backward_local(
        slot_len, patches, main, small, saved, result, gslots, experts
    )
    small_rows = jnp.concatenate([grad_phi[:, :experts], grad_norms[:4].T], axis=1)
    grad_main, grad_small = regroup_grads(grad_main, pad_to(small_rows, (D, lanes)), experts)
    main_part, small_part, norm_tile = reduce_grads(grad_main, grad_small, squares, experts)
    attn_part = main_part[:, : 2 * rows].reshape(2, 2, rows, D).transpose(2, 0, 1, 3)
    attn_part = attn_part.reshape(rows, 4 * D)
    phi_part = small_part[:rows, :experts]
    norm_part = small_part[:rows, experts : experts + 4].T
    grad_norm = norm_tile[0, 0]
    factor = CLIP_NORM / jnp.maximum(grad_norm, CLIP_NORM)
    attn_new, attn_first_new, attn_second_new = adam_update(
        attn_weight, attn_first, attn_second, attn_part, factor, 1.0 / math.sqrt(D), WEIGHT_DECAY
    )
    phi_new, phi_first_new, phi_second_new = adam_update(
        phi_weight, phi_first, phi_second, phi_part, factor, 0.25 / math.sqrt(D), WEIGHT_DECAY
    )
    norm_new, norm_first_new, norm_second_new = adam_update(
        norm_params, norm_first, norm_second, norm_part, factor, 0.8, 0.0
    )
    in_new, in_first_new, in_second_new = adam_update(
        expert_in, in_first, in_second, grad_in, factor, 4.0 / math.sqrt(D), WEIGHT_DECAY
    )
    out_new, out_first_new, out_second_new = adam_update(
        expert_out, out_first, out_second, grad_out, factor, 8.0 / math.sqrt(FF), WEIGHT_DECAY
    )
    return (
        block_output,
        input_grad,
        grad_norm,
        attn_new,
        attn_first_new,
        attn_second_new,
        phi_new,
        phi_first_new,
        phi_second_new,
        norm_new,
        norm_first_new,
        norm_second_new,
        in_new,
        in_first_new,
        in_second_new,
        out_new,
        out_first_new,
        out_second_new,
    )


def solution(mesh):
    in_specs = (
        P(("batch", "expert"), None),
        P(("batch", "expert"), None),
        P("expert", None),
        P("expert", None),
        P("expert", None),
        P("expert", None),
        P("expert", None),
        P("expert", None),
        P(None, "expert"),
        P(None, "expert"),
        P(None, "expert"),
        P("expert", None, "batch"),
        P("expert", None, "batch"),
        P("expert", None, "batch"),
        P("expert", "batch", None),
        P("expert", "batch", None),
        P("expert", "batch", None),
        P(("batch", "expert"), None),
    )
    out_specs = (
        P(("batch", "expert"), None),
        P(("batch", "expert"), None),
        P(),
        P("expert", None),
        P("expert", None),
        P("expert", None),
        P("expert", None),
        P("expert", None),
        P("expert", None),
        P(None, "expert"),
        P(None, "expert"),
        P(None, "expert"),
        P("expert", None, "batch"),
        P("expert", None, "batch"),
        P("expert", None, "batch"),
        P("expert", "batch", None),
        P("expert", "batch", None),
        P("expert", "batch", None),
    )
    return jax.shard_map(local, mesh=mesh, in_specs=in_specs, out_specs=out_specs, check_vma=False)
```

```python
import functools
import math

import jax
import jax.numpy as jnp
from jax import lax
from jax.experimental import pallas as pl
from jax.experimental.pallas import tpu as pltpu
from jax.sharding import PartitionSpec as P

D = 384
HEADS = 6
HEAD_DIM = 64
FF = 1536
STEP = 3
SHORT_LEN = 196
LONG_LEN = 576
IMAGES = 5
SLOT_ROWS = 8
PAIRS = 3
GROUPS = 16
GROUP_ROWS = D // GROUPS

NORM_EPS = 1e-06
CLIP_NORM = 1.0
BETA_FIRST = 0.5
BETA_SECOND = 0.5
ADAM_EPS = 1e-08
WEIGHT_DECAY = 0.05
MASKED = -1e30
SCORE_SCALE = HEAD_DIM ** (-0.5)

MESH = pl.DeviceIdType.MESH
F32 = jnp.float32
BF16 = jnp.bfloat16
VMEM_BYTES = 58 * 1024 * 1024


def whole(count):
    return [pl.BlockSpec(memory_space=pltpu.VMEM)] * count


def round_up(value, unit):
    return -(-value // unit) * unit


def mm(left, right):
    return jnp.dot(left, right, preferred_element_type=F32)


def mm_nt(left, right):
    return lax.dot_general(left, right, (((1,), (1,)), ((), ())), preferred_element_type=F32)


def mm_tn(left, right):
    return lax.dot_general(left, right, (((0,), (0,)), ((), ())), preferred_element_type=F32)


def block_rows(experts):
    rows = D // experts
    return round_up(6 * rows + max(experts, 4), 16)


def ring(experts):
    core = lax.axis_index("batch")
    chip = lax.axis_index("expert")
    first = chip ^ (1 + core)
    second = chip ^ (2 - core)
    return core, chip, first, second


def gather_kernel(experts, attn_ref, phi_ref, norm_ref, out, stage, send_z, send_first,
                  send_second, send_pair, recv, recv_pair):
    core, chip, first, second = ring(experts)
    rows = attn_ref.shape[0]
    column = lax.rem(chip, 4)
    layers = experts // 4
    layer = chip // 4
    barrier = pltpu.get_barrier_semaphore()

    @pl.loop(1, layers)
    def _(d):
        peer = lax.rem(layer + d, layers) * 4 + column
        pl.semaphore_signal(barrier, inc=1, device_id=(core, peer), device_id_type=MESH)

    pl.semaphore_signal(barrier, inc=1, device_id=(core, first), device_id_type=MESH)
    pl.semaphore_signal(barrier, inc=1, device_id=(core, second), device_id_type=MESH)
    pl.semaphore_signal(barrier, inc=1, device_id=(1 - core, chip), device_id_type=MESH)
    stage[...] = jnp.zeros_like(stage)
    for part in range(2):
        for g in range(3):
            lanes = pl.multiple_of(core * (2 * D) + (part * D + g * 128), 128)
            place = (2 * g + part) * rows
            stage[place : place + rows, :] = attn_ref[:, pl.ds(lanes, 128)]

    @pl.when(core == 0)
    def _():
        stage[6 * rows : 6 * rows + experts, 0:rows] = phi_ref[...]

    @pl.when(core == 1)
    def _():
        stage[6 * rows : 6 * rows + 4, 0:rows] = norm_ref[...]

    out[chip, core] = stage[...].astype(BF16)
    pl.semaphore_wait(barrier, layers + 2)

    def copy(block, side, sems, sem, arrivals, device):
        return pltpu.make_async_remote_copy(
            src_ref=out.at[block, side],
            dst_ref=out.at[block, side],
            send_sem=sems.at[sem],
            recv_sem=arrivals.at[block],
            device_id=device,
            device_id_type=MESH,
        )

    def along_z(d):
        peer = lax.rem(layer + d, layers) * 4 + column
        return copy(chip, core, send_z, d, recv, (core, peer))

    def to_first(block):
        return copy(block, core, send_first, block, recv, (core, first))

    def to_second(block):
        return copy(block, core, send_second, block, recv, (core, second))

    def to_pair(block):
        return copy(block, core, send_pair, block, recv_pair, (1 - core, chip))

    @pl.loop(1, layers)
    def _(d):
        along_z(d).start()

    to_first(chip).start()
    to_second(chip).start()
    to_pair(chip).start()

    @pl.loop(1, layers)
    def _(d):
        block = lax.rem(layer - d + layers, layers) * 4 + column
        to_first(block).wait_recv()
        to_first(block).start()
        to_second(block).start()
        to_pair(block).start()

    @pl.loop(0, layers)
    def _(d):
        block = lax.rem(layer - d + layers, layers) * 4 + lax.rem(first, 4)
        to_first(block).wait_recv()
        to_second(block).start()
        to_pair(block).start()

    @pl.loop(0, 2 * layers)
    def _(d):
        other = jnp.where(lax.rem(d, 2) == 0, lax.rem(second, 4), lax.rem(3 - column, 4))
        block = lax.rem(layer - d // 2 + layers, layers) * 4 + other
        to_first(block).wait_recv()
        to_pair(block).start()

    @pl.loop(1, layers)
    def _(d):
        along_z(d).wait_send()

    @pl.loop(0, layers)
    def _(d):
        block = d * 4 + column
        to_first(block).wait_send()
        to_second(block).wait_send()
        to_second(d * 4 + lax.rem(first, 4)).wait_send()

    @pl.loop(0, experts)
    def _(block):
        to_pair(block).wait_send()
        copy(block, 1 - core, send_pair, block, recv_pair, (1 - core, chip)).wait_recv()


def gather_weights(attn_weight, phi_turned, norm_params, experts):
    rows = block_rows(experts)
    dma = pltpu.SemaphoreType.DMA
    return pl.pallas_call(
        functools.partial(gather_kernel, experts),
        out_shape=jax.ShapeDtypeStruct((experts, 2, rows, 128), BF16),
        in_specs=whole(3),
        out_specs=whole(1)[0],
        scratch_shapes=[pltpu.VMEM((rows, 128), F32), dma((experts // 4,))]
        + [dma((experts,))] * 5,
        compiler_params=pltpu.CompilerParams(
            collective_id=0, has_side_effects=True, vmem_limit_bytes=16 * 1024 * 1024
        ),
        name="gather_weights",
    )(attn_weight, phi_turned, norm_params)


def unpack_weight(main_ref, side, part):
    blocks = main_ref[:, side].astype(F32)
    columns = []
    for g in range(3):
        place = (2 * g + part) * GROUP_ROWS
        columns.append(blocks[:, place : place + GROUP_ROWS, :].reshape(D, 128))
    return jnp.concatenate(columns, axis=1).astype(BF16)


def group_lanes():
    lane = lax.broadcasted_iota(jnp.int32, (128, D), 0)
    column = lax.broadcasted_iota(jnp.int32, (128, D), 1)
    return jnp.where(column % GROUP_ROWS == lane, 1.0, 0.0).astype(BF16)


def unpack_turned(main_ref, side, rows):
    first = 6 * GROUP_ROWS
    blocks = main_ref[:, side].astype(F32)[:, first : first + rows, :]
    spread = mm(blocks.reshape(GROUPS * rows, 128).astype(BF16), group_lanes())
    spread = spread.reshape(GROUPS, rows, D)
    group = lax.broadcasted_iota(jnp.int32, (GROUPS, 1, D), 0)
    column = lax.broadcasted_iota(jnp.int32, (GROUPS, 1, D), 2)
    return jnp.sum(jnp.where(column // GROUP_ROWS == group, spread, 0.0), axis=0)


def pack_turned(values):
    rows = values.shape[0]
    group = lax.broadcasted_iota(jnp.int32, (GROUPS, 1, D), 0)
    column = lax.broadcasted_iota(jnp.int32, (GROUPS, 1, D), 2)
    spread = jnp.where(column // GROUP_ROWS == group, values[None], 0.0)
    spread = spread.reshape(GROUPS * rows, D).astype(BF16)
    return mm_nt(spread, group_lanes()).reshape(GROUPS, rows, 128)


def unpack_small(main_ref, experts):
    turned = unpack_turned(main_ref, 0, max(experts, 16)).astype(BF16)
    row = lax.broadcasted_iota(jnp.int32, (experts * SLOT_ROWS, turned.shape[0]), 0)
    column = lax.broadcasted_iota(jnp.int32, (experts * SLOT_ROWS, turned.shape[0]), 1)
    spread = jnp.where(column == row // SLOT_ROWS, 1.0, 0.0).astype(BF16)
    return mm(spread, turned).astype(BF16), unpack_turned(main_ref, 1, 8)


def slot_bounds(len_ref, columns):
    image = lax.broadcasted_iota(jnp.int32, (1, columns), 1) % SLOT_ROWS
    starts = jnp.zeros((1, columns), jnp.int32)
    ends = jnp.zeros((1, columns), jnp.int32)
    start = jnp.int32(0)
    for k in range(IMAGES):
        end = start + len_ref[0, k]
        starts = jnp.where(image == k, start, starts)
        ends = jnp.where(image == k, end, ends)
        start = end
    return starts, ends, start


def normed(values):
    centred = values - jnp.mean(values, axis=-1, keepdims=True)
    variance = jnp.mean(centred * centred, axis=-1, keepdims=True)
    inverse = lax.rsqrt(variance + NORM_EPS)
    return centred * inverse, inverse


def norm_back(grad_shaped, normal, inverse, scaling):
    grad_normal = grad_shaped * scaling
    return inverse * (
        grad_normal
        - jnp.mean(grad_normal, axis=-1, keepdims=True)
        - normal * jnp.mean(grad_normal * normal, axis=-1, keepdims=True)
    )


def over_images(len_ref, tokens, body):
    def step(k, start):
        length = len_ref[0, k]
        for full in (SHORT_LEN, LONG_LEN):

            @pl.when(length == full)
            def _():
                window = round_up(full + 12, 16)
                first = jnp.minimum((start // 16) * 16, tokens - window)
                body(pl.multiple_of(first, 16), start - first, full, window)

        return start + length

    lax.fori_loop(0, IMAGES, step, jnp.int32(0))


def window_masks(shift, full, window):
    column = lax.broadcasted_iota(jnp.int32, (1, window), 1)
    row = lax.broadcasted_iota(jnp.int32, (window, 1), 0)
    bias = jnp.where((column >= shift) & (column < shift + full), 0.0, MASKED)
    inside = (row >= shift) & (row < shift + full)
    return bias, inside


def forward_kernel(experts, len_ref, patch_ref, main_ref, cot_ref, qkv_ref, o_ref, lse_ref, x1_ref,
                   h2_ref, disp_ref, comb_ref, gy_ref, pack_ref, logit, packf):
    tokens = patch_ref.shape[0]
    columns = experts * SLOT_ROWS
    tile = tokens // 5
    phi, norms = unpack_small(main_ref, experts)
    starts, ends, total = slot_bounds(len_ref, columns)
    w_q, w_k = unpack_weight(main_ref, 0, 0), unpack_weight(main_ref, 0, 1)
    w_v = unpack_weight(main_ref, 1, 0)
    w_qkv = jnp.concatenate([w_q, w_k, w_v], axis=1)
    for t in range(5):
        rows = pl.ds(t * tile, tile)
        normal, _ = normed(patch_ref[rows, :].astype(F32))
        h1 = (normal * norms[0:1] + norms[1:2]).astype(BF16)
        qkv = mm(h1, w_qkv).astype(BF16)
        for c in range(9):
            qkv_ref[c, rows, :] = qkv[:, c * 128 : (c + 1) * 128]
    o_ref[...] = jnp.zeros_like(o_ref)
    lse_ref[...] = jnp.zeros_like(lse_ref)
    low_lane = lax.broadcasted_iota(jnp.int32, (1, 128), 1) < HEAD_DIM
    lane = lax.broadcasted_iota(jnp.int32, (1, 128), 1)

    def attend(first, shift, full, window):
        bias, inside = window_masks(shift, full, window)
        rows = pl.ds(first, window)

        @pl.loop(0, PAIRS)
        def _(p):
            query = qkv_ref[p, rows, :].astype(F32) * SCORE_SCALE
            keys = qkv_ref[PAIRS + p, rows, :]
            values = qkv_ref[2 * PAIRS + p, rows, :]
            outs = []
            sums = lse_ref[rows, :]
            for h in range(2):
                mine = low_lane if h == 0 else jnp.logical_not(low_lane)
                scores = mm_nt(jnp.where(mine, query, 0.0).astype(BF16), keys) + bias
                peak = jnp.max(scores, axis=-1, keepdims=True)
                exponent = jnp.exp(scores - peak)
                summed = jnp.sum(exponent, axis=-1, keepdims=True)
                probs = (exponent * (1.0 / summed)).astype(BF16)
                outs.append(mm(probs, values))
                sums = jnp.where(inside & (lane == 2 * p + h), peak + jnp.log(summed), sums)
            lse_ref[rows, :] = sums
            lanes = pl.ds(pl.multiple_of(p * 128, 128), 128)
            old = o_ref[rows, lanes].astype(F32)
            merged = jnp.where(inside, jnp.where(low_lane, outs[0], outs[1]), old)
            o_ref[rows, lanes] = merged.astype(BF16)

    over_images(len_ref, tokens, attend)

    w_o = unpack_weight(main_ref, 1, 1)
    for t in range(5):
        rows = pl.ds(t * tile, tile)
        x1 = patch_ref[rows, :].astype(F32) + mm(o_ref[rows, :], w_o)
        normal, _ = normed(x1)
        h2 = (normal * norms[2:3] + norms[3:4]).astype(BF16)
        h2_ref[rows, :] = h2
        logit[rows, :] = mm_nt(h2, phi)
        position = t * tile + lax.broadcasted_iota(jnp.int32, (tile, 1), 0)
        valid = position < total
        x1_ref[rows, :] = jnp.where(valid, x1, 0.0)
        gy_ref[rows, :] = jnp.where(valid, cot_ref[rows, :].astype(F32), 0.0).astype(BF16)

    position = lax.broadcasted_iota(jnp.int32, (tokens, columns), 0)
    member = (position >= starts) & (position < ends)
    present = ends > starts
    logits = logit[...]
    peak = jnp.max(jnp.where(member, logits, MASKED), axis=0, keepdims=True)
    peak = jnp.where(present, peak, 0.0)
    exponent = jnp.where(member, jnp.exp(jnp.where(member, logits - peak, 0.0)), 0.0)
    summed = jnp.sum(exponent, axis=0, keepdims=True) + jnp.where(present, 0.0, 1.0)
    dispatch = exponent / summed
    disp_ref[...] = dispatch
    slots = mm_tn(dispatch.astype(BF16), h2_ref[...])
    row_peak = jnp.max(logits, axis=-1, keepdims=True)
    exponent = jnp.exp(logits - row_peak)
    summed = jnp.sum(exponent, axis=-1, keepdims=True) * (1.0 / SLOT_ROWS)
    combine = jnp.where(member, exponent / summed, 0.0)
    comb_ref[...] = combine
    grad_result = mm_tn(combine.astype(BF16), gy_ref[...])
    for part, matrix in enumerate((slots, grad_result)):
        pack_rows(packf, matrix.reshape(experts, SLOT_ROWS, D))
        pack_ref[:, part * 16 : (part + 1) * 16, :] = packf[...].astype(BF16)


def pack_rows(packf, blocks):
    packf[...] = jnp.zeros_like(packf)
    for c in range(3):
        packf[:, c * IMAGES : (c + 1) * IMAGES, :] = blocks[:, :IMAGES, c * 128 : (c + 1) * 128]


def unpack_rows(packf, wide):
    wide[...] = jnp.zeros_like(wide)
    for c in range(3):
        wide[:, 0:IMAGES, c * 128 : (c + 1) * 128] = packf[:, c * IMAGES : (c + 1) * IMAGES, :]


def forward_local(lengths, patches, main, cotangent, experts):
    tokens = patches.shape[0]
    columns = experts * SLOT_ROWS
    shape = jax.ShapeDtypeStruct
    return pl.pallas_call(
        functools.partial(forward_kernel, experts),
        out_shape=(
            shape((9, tokens, 128), BF16),
            shape((tokens, D), BF16),
            shape((tokens, 128), F32),
            shape((tokens, D), F32),
            shape((tokens, D), BF16),
            shape((tokens, columns), F32),
            shape((tokens, columns), F32),
            shape((tokens, D), BF16),
            shape((experts, 32, 128), BF16),
        ),
        in_specs=[pl.BlockSpec(memory_space=pltpu.SMEM)] + whole(3),
        out_specs=tuple(whole(9)),
        scratch_shapes=[pltpu.VMEM((tokens, columns), F32), pltpu.VMEM((experts, 16, 128), F32)],
        compiler_params=pltpu.CompilerParams(vmem_limit_bytes=VMEM_BYTES),
        name="forward_local",
    )(lengths, patches, main, cotangent)


def expert_kernel(experts, pack_ref, in_ref, out_ref, result_ref, gslot_ref, gin_ref, gout_ref,
                  square_ref, inbox, partial, given, outbox, back, packf, wide, packe, widee,
                  send_one, recv_one, pair_send, pair_recv, send_two, recv_two, sum_sem):
    core = lax.axis_index("batch")
    chip = lax.axis_index("expert")
    barrier = pltpu.get_barrier_semaphore()

    @pl.loop(1, experts)
    def _(j):
        peer = lax.rem(chip + j, experts)
        pl.semaphore_signal(barrier, inc=1, device_id=(core, peer), device_id_type=MESH)

    pl.semaphore_signal(barrier, inc=1, device_id=(1 - core, chip), device_id_type=MESH)
    w_in = in_ref[0].astype(BF16)
    w_out = out_ref[0].astype(BF16)
    inbox[core, chip] = pack_ref[chip]
    pl.semaphore_wait(barrier, experts)

    def first(j, block, peer):
        return pltpu.make_async_remote_copy(
            src_ref=pack_ref.at[peer],
            dst_ref=inbox.at[core, block],
            send_sem=send_one.at[j],
            recv_sem=recv_one.at[j],
            device_id=(core, peer),
            device_id_type=MESH,
        )

    def to_pair(side, block):
        return pltpu.make_async_remote_copy(
            src_ref=inbox.at[side, block],
            dst_ref=inbox.at[side, block],
            send_sem=pair_send.at[block],
            recv_sem=pair_recv.at[block],
            device_id=(1 - core, chip),
            device_id_type=MESH,
        )

    def second(j, block, peer):
        return pltpu.make_async_remote_copy(
            src_ref=outbox.at[peer],
            dst_ref=back.at[block],
            send_sem=send_two.at[j],
            recv_sem=recv_two.at[j],
            device_id=(core, peer),
            device_id_type=MESH,
        )

    @pl.loop(1, experts)
    def _(j):
        first(j, chip, lax.rem(chip + j, experts)).start()

    to_pair(core, chip).start()

    @pl.loop(1, experts)
    def _(j):
        source = lax.rem(chip - j + experts, experts)
        first(j, source, source).wait_recv()
        to_pair(core, source).start()

    @pl.loop(0, experts)
    def _(block):
        to_pair(1 - core, block).wait_recv()

    def spread(side, part):
        packe[...] = inbox[side, :, part * 16 : (part + 1) * 16, :].astype(F32)
        unpack_rows(packe, widee)
        return widee[...].reshape(experts * SLOT_ROWS, D).astype(BF16)

    def run(side):
        slots = spread(side, 0)
        grads = spread(side, 1)
        hidden = mm(slots, w_in)
        root = math.sqrt(2.0 / math.pi)
        bent = jnp.tanh(root * (hidden + 0.044715 * (hidden * hidden * hidden)))
        half = 0.5 * (1.0 + bent)
        act = (hidden * half).astype(BF16)
        slope = half + 0.5 * hidden * (1.0 - bent * bent) * (
            root * (1.0 + 3.0 * 0.044715 * (hidden * hidden))
        )
        result = mm(act, w_out)
        grad_hidden = (mm_nt(grads, w_out) * slope).astype(BF16)
        grad_slots = mm_nt(grad_hidden, w_in)
        return slots, grads, act, grad_hidden, result, grad_slots

    theirs = run(1 - core)
    for part in range(2):
        pack_rows(packf, theirs[4 + part].reshape(experts, SLOT_ROWS, D))
        partial[:, part * 16 : (part + 1) * 16, :] = packf[...].astype(BF16)
    halves = pltpu.make_async_remote_copy(
        src_ref=partial,
        dst_ref=given,
        send_sem=sum_sem.at[0],
        recv_sem=sum_sem.at[1],
        device_id=(1 - core, chip),
        device_id_type=MESH,
    )
    halves.start()
    ours = run(core)
    halves.wait_recv()
    for part in range(2):
        block = slice(part * 16, (part + 1) * 16)
        pack_rows(packf, ours[4 + part].reshape(experts, SLOT_ROWS, D))
        outbox[:, block, :] = (packf[...] + given[:, block, :].astype(F32)).astype(BF16)

    @pl.loop(1, experts)
    def _(j):
        second(j, chip, lax.rem(chip + j, experts)).start()

    back[chip] = outbox[chip]
    grad_out = mm_tn(ours[2], ours[1]) + mm_tn(theirs[2], theirs[1])
    gout_ref[0] = grad_out
    grad_in = mm_tn(ours[0], ours[3]) + mm_tn(theirs[0], theirs[3])
    gin_ref[0] = grad_in
    squares = jnp.sum(grad_out * grad_out) + jnp.sum(grad_in * grad_in)
    square_ref[...] = jnp.full(square_ref.shape, squares, F32)

    @pl.loop(1, experts)
    def _(j):
        source = lax.rem(chip - j + experts, experts)
        second(j, source, source).wait_recv()

    for part, target in enumerate((result_ref, gslot_ref)):
        packe[...] = back[:, part * 16 : (part + 1) * 16, :].astype(F32)
        unpack_rows(packe, widee)
        target[...] = widee[...].reshape(experts * SLOT_ROWS, D).astype(BF16)

    halves.wait_send()

    @pl.loop(1, experts)
    def _(j):
        peer = lax.rem(chip + j, experts)
        first(j, chip, peer).wait_send()
        second(j, chip, peer).wait_send()

    @pl.loop(0, experts)
    def _(block):
        to_pair(core, block).wait_send()


def run_experts(packed, expert_in, expert_out, experts):
    shape = jax.ShapeDtypeStruct
    dma = pltpu.SemaphoreType.DMA
    return pl.pallas_call(
        functools.partial(expert_kernel, experts),
        out_shape=(
            shape((experts * SLOT_ROWS, D), BF16),
            shape((experts * SLOT_ROWS, D), BF16),
            shape(expert_in.shape, F32),
            shape(expert_out.shape, F32),
            shape((1, 128), F32),
        ),
        in_specs=whole(3),
        out_specs=tuple(whole(5)),
        scratch_shapes=[
            pltpu.VMEM((2, experts, 32, 128), BF16),
            pltpu.VMEM((experts, 32, 128), BF16),
            pltpu.VMEM((experts, 32, 128), BF16),
            pltpu.VMEM((experts, 32, 128), BF16),
            pltpu.VMEM((experts, 32, 128), BF16),
            pltpu.VMEM((experts, 16, 128), F32),
            pltpu.VMEM((experts, SLOT_ROWS, D), F32),
            pltpu.VMEM((experts, 16, 128), F32),
            pltpu.VMEM((experts, SLOT_ROWS, D), F32),
        ]
        + [dma((experts,))] * 6
        + [dma((2,))],
        compiler_params=pltpu.CompilerParams(
            collective_id=1, has_side_effects=True, vmem_limit_bytes=VMEM_BYTES
        ),
        name="run_experts",
    )(packed, expert_in, expert_out)


def backward_kernel(experts, len_ref, patch_ref, main_ref, qkv_ref, o_ref, lse_ref,
                    x1_ref, h2_ref, disp_ref, comb_ref, gy_ref, result_ref, gslot_ref, block_ref,
                    input_ref, gw_ref, gdisp, glog, gx1, branch, go, gqkv,
                    h1_all):
    tokens = patch_ref.shape[0]
    columns = experts * SLOT_ROWS
    tile = tokens // 5
    phi, norms = unpack_small(main_ref, experts)
    result = result_ref[...]
    gslots = gslot_ref[...]

    inner = jnp.zeros((1, columns), F32)
    for t in range(5):
        rows = pl.ds(t * tile, tile)
        grad_dispatch = mm_nt(h2_ref[rows, :], gslots)
        gdisp[rows, :] = grad_dispatch
        inner = inner + jnp.sum(disp_ref[rows, :] * grad_dispatch, axis=0, keepdims=True)

    w_o = unpack_weight(main_ref, 1, 1)
    gain_two = jnp.zeros((1, D), F32)
    bias_two = jnp.zeros((1, D), F32)
    for t in range(5):
        rows = pl.ds(t * tile, tile)
        dispatch, combine, gy = disp_ref[rows, :], comb_ref[rows, :], gy_ref[rows, :]
        x1 = x1_ref[rows, :]
        mixed = mm(combine.astype(BF16), result)
        block_ref[rows, :] = (x1 + mixed).astype(BF16)
        weighted = combine * mm_nt(gy, result)
        grad_logits = (
            weighted
            - combine * jnp.sum(weighted, axis=-1, keepdims=True)
            + dispatch * (gdisp[rows, :] - inner)
        ).astype(BF16)
        glog[rows, :] = grad_logits
        grad_h2 = mm(dispatch.astype(BF16), gslots) + mm(grad_logits, phi)
        normal, inverse = normed(x1)
        gain_two = gain_two + jnp.sum(grad_h2 * normal, axis=0, keepdims=True)
        bias_two = bias_two + jnp.sum(grad_h2, axis=0, keepdims=True)
        grad_x1 = gy.astype(F32) + norm_back(grad_h2, normal, inverse, norms[2:3])
        gx1[rows, :] = grad_x1
        grad_branch = grad_x1.astype(BF16)
        branch[rows, :] = grad_branch
        grad_o = mm_nt(grad_branch, w_o).astype(BF16)
        for c in range(PAIRS):
            go[c, rows, :] = grad_o[:, c * 128 : (c + 1) * 128]

    small_rows = gw_ref.shape[2] - 6 * GROUP_ROWS
    row = lax.broadcasted_iota(jnp.int32, (columns, small_rows), 0)
    column = lax.broadcasted_iota(jnp.int32, (columns, small_rows), 1)
    fold = jnp.where(column == row // SLOT_ROWS, 1.0, 0.0).astype(BF16)
    folded = mm(glog[...], fold).astype(BF16)
    gw_ref[0, :, 6 * GROUP_ROWS :, :] = pack_turned(mm_tn(folded, h2_ref[...]))

    def put(side, part, value):
        for g in range(3):
            place = (2 * g + part) * GROUP_ROWS
            gw_ref[side, :, place : place + GROUP_ROWS, :] = value[
                :, g * 128 : (g + 1) * 128
            ].reshape(GROUPS, GROUP_ROWS, 128)

    put(1, 1, mm_tn(o_ref[...], branch[...]))

    gqkv[...] = jnp.zeros_like(gqkv)
    low_lane = lax.broadcasted_iota(jnp.int32, (1, 128), 1) < HEAD_DIM
    lane = lax.broadcasted_iota(jnp.int32, (1, 128), 1)

    def attend(first, shift, full, window):
        bias, inside = window_masks(shift, full, window)
        rows = pl.ds(first, window)
        sums = lse_ref[rows, :]

        @pl.loop(0, PAIRS)
        def _(p):
            query_low = qkv_ref[p, rows, :]
            query = query_low.astype(F32) * SCORE_SCALE
            keys = qkv_ref[PAIRS + p, rows, :]
            values = qkv_ref[2 * PAIRS + p, rows, :]
            grads_low = go[p, rows, :]
            grads = grads_low.astype(F32)
            parts = []
            for h in range(2):
                mine = low_lane if h == 0 else jnp.logical_not(low_lane)
                scores = mm_nt(jnp.where(mine, query, 0.0).astype(BF16), keys) + bias
                summed = jnp.sum(jnp.where(lane == 2 * p + h, sums, 0.0), axis=-1, keepdims=True)
                probs = jnp.exp(scores - jnp.where(inside, summed, 1e30))
                grad_probs = mm_nt(jnp.where(mine, grads, 0.0).astype(BF16), values)
                dot = jnp.sum(probs * grad_probs, axis=-1, keepdims=True)
                grad_scores = (probs * (grad_probs - dot)).astype(BF16)
                parts.append(
                    (
                        mm(grad_scores, keys) * SCORE_SCALE,
                        mm_tn(grad_scores, query_low) * SCORE_SCALE,
                        mm_tn(probs.astype(BF16), grads_low),
                    )
                )
            for c in range(3):
                old = gqkv[c * PAIRS + p, rows, :].astype(F32)
                new = jnp.where(low_lane, parts[0][c], parts[1][c])
                gqkv[c * PAIRS + p, rows, :] = jnp.where(inside, new, old).astype(BF16)

    over_images(len_ref, tokens, attend)

    w_q, w_k = unpack_weight(main_ref, 0, 0), unpack_weight(main_ref, 0, 1)
    w_v = unpack_weight(main_ref, 1, 0)
    w_qkv = jnp.concatenate([w_q, w_k, w_v], axis=1)
    gain_one = jnp.zeros((1, D), F32)
    bias_one = jnp.zeros((1, D), F32)
    for t in range(5):
        rows = pl.ds(t * tile, tile)
        grad_qkv = jnp.concatenate([gqkv[c, rows, :] for c in range(9)], axis=1)
        grad_h1 = mm_nt(grad_qkv, w_qkv)
        normal, inverse = normed(patch_ref[rows, :].astype(F32))
        h1_all[rows, :] = (normal * norms[0:1] + norms[1:2]).astype(BF16)
        gain_one = gain_one + jnp.sum(grad_h1 * normal, axis=0, keepdims=True)
        bias_one = bias_one + jnp.sum(grad_h1, axis=0, keepdims=True)
        grad_x = gx1[rows, :] + norm_back(grad_h1, normal, inverse, norms[0:1])
        input_ref[rows, :] = grad_x.astype(BF16)
    for c, (side, part) in enumerate(((0, 0), (0, 1), (1, 0))):
        grad = jnp.concatenate([gqkv[c * PAIRS + p] for p in range(PAIRS)], axis=1)
        put(side, part, mm_tn(h1_all[...], grad))
    zeros = jnp.zeros((small_rows - 4, D), F32)
    turned = jnp.concatenate([gain_one, bias_one, gain_two, bias_two, zeros], axis=0)
    gw_ref[1, :, 6 * GROUP_ROWS :, :] = pack_turned(turned)


def backward_local(lengths, patches, main, saved, result, gslots, experts):
    tokens = patches.shape[0]
    columns = experts * SLOT_ROWS
    shape = jax.ShapeDtypeStruct
    return pl.pallas_call(
        functools.partial(backward_kernel, experts),
        out_shape=(
            shape((tokens, D), BF16),
            shape((tokens, D), BF16),
            shape((2,) + (GROUPS,) + main.shape[2:], F32),
        ),
        in_specs=[pl.BlockSpec(memory_space=pltpu.SMEM)] + whole(12),
        out_specs=tuple(whole(3)),
        scratch_shapes=[
            pltpu.VMEM((tokens, columns), F32),
            pltpu.VMEM((tokens, columns), BF16),
            pltpu.VMEM((tokens, D), F32),
            pltpu.VMEM((tokens, D), BF16),
            pltpu.VMEM((PAIRS, tokens, 128), BF16),
            pltpu.VMEM((9, tokens, 128), BF16),
            pltpu.VMEM((tokens, D), BF16),
        ],
        compiler_params=pltpu.CompilerParams(vmem_limit_bytes=VMEM_BYTES),
        name="backward_local",
    )(lengths, patches, main, *saved, result, gslots)


def reduce_kernel(experts, gw_ref, square_ref, attn_out, phi_out, norm_out, total_ref, own, pair_in,
                  box_one, in_one, box_two, in_two, box_z, in_z, final, scalars, load_sem, pair_send,
                  pair_recv, send_one, recv_one, send_two, recv_two, send_z, recv_z, swap_sem,
                  norm_send, norm_recv):
    core, chip, first, second = ring(experts)
    rows = attn_out.shape[0]
    layers = experts // 4
    layer = chip // 4
    column = lax.rem(chip, 4)
    barrier = pltpu.get_barrier_semaphore()

    @pl.loop(1, experts)
    def _(j):
        peer = lax.rem(chip + j, experts)
        pl.semaphore_signal(barrier, inc=1, device_id=(core, peer), device_id_type=MESH)

    pl.semaphore_signal(barrier, inc=1, device_id=(1 - core, chip), device_id_type=MESH)
    load = pltpu.make_async_copy(gw_ref.at[core], own, load_sem.at[0])
    load.start()
    pl.semaphore_wait(barrier, experts)

    def pair_copy(block):
        return pltpu.make_async_remote_copy(
            src_ref=gw_ref.at[1 - core, block],
            dst_ref=pair_in.at[block],
            send_sem=pair_send.at[block],
            recv_sem=pair_recv.at[block],
            device_id=(1 - core, chip),
            device_id_type=MESH,
        )

    def copy(source, target, sends, arrivals, index, device):
        return pltpu.make_async_remote_copy(
            src_ref=source.at[index],
            dst_ref=target.at[index],
            send_sem=sends.at[index],
            recv_sem=arrivals.at[index],
            device_id=device,
            device_id_type=MESH,
        )

    def to_first(index):
        return copy(box_one, in_one, send_one, recv_one, index, (core, first))

    def to_second(index):
        return copy(box_two, in_two, send_two, recv_two, index, (core, second))

    def layer_at(d):
        return lax.rem(layer + 1 + d, layers)

    far = 3 - column

    def block_at(d, place):
        return layer_at(d) * 4 + place

    both, one, two = far, lax.rem(first, 4), lax.rem(second, 4)

    for place in (both, two, one, column):

        @pl.loop(0, layers)
        def _(d):
            pair_copy(block_at(d, place)).start()

    load.wait()

    def summed(block):
        pair_copy(block).wait_recv()
        return own[block] + pair_in[block]

    for batch, place in ((0, both), (1, one)):

        @pl.loop(0, layers)
        def _(d):
            index = batch * layers + layer_at(d)
            box_one[index] = summed(block_at(d, place)).astype(BF16)
            to_first(index).start()

    @pl.loop(0, layers)
    def _(d):
        index = layer_at(d)
        total = summed(block_at(d, two))
        to_first(index).wait_recv()
        box_two[index] = (total + in_one[index].astype(F32)).astype(BF16)
        to_second(index).start()

    def to_layer(index):
        return pltpu.make_async_remote_copy(
            src_ref=box_z.at[index],
            dst_ref=in_z.at[layer],
            send_sem=send_z.at[index],
            recv_sem=recv_z.at[layer],
            device_id=(core, index * 4 + column),
            device_id_type=MESH,
        )

    def column_sum(index):
        total = summed(index * 4 + column)
        to_first(layers + index).wait_recv()
        total = total + in_one[layers + index].astype(F32)
        to_second(index).wait_recv()
        return total + in_two[index].astype(F32)

    @pl.loop(0, layers - 1)
    def _(d):
        index = layer_at(d)
        box_z[index] = column_sum(index).astype(BF16)
        to_layer(index).start()

    final[core] = column_sum(layer)

    @pl.loop(1, layers)
    def _(d):
        index = lax.rem(layer - d + layers, layers)
        pltpu.make_async_remote_copy(
            src_ref=box_z.at[index],
            dst_ref=in_z.at[index],
            send_sem=send_z.at[index],
            recv_sem=recv_z.at[index],
            device_id=(core, index * 4 + column),
            device_id_type=MESH,
        ).wait_recv()
        final[core] += in_z[index].astype(F32)

    def swap(side):
        return pltpu.make_async_remote_copy(
            src_ref=final.at[side],
            dst_ref=final.at[side],
            send_sem=swap_sem.at[0],
            recv_sem=swap_sem.at[1],
            device_id=(1 - core, chip),
            device_id_type=MESH,
        )

    mine = final[core]
    swap(core).start()

    scalars[experts + core] = square_ref[...] + jnp.sum(mine * mine)

    def norm_pair(side):
        return pltpu.make_async_remote_copy(
            src_ref=scalars.at[experts + side],
            dst_ref=scalars.at[experts + side],
            send_sem=swap_sem.at[2],
            recv_sem=swap_sem.at[3],
            device_id=(1 - core, chip),
            device_id_type=MESH,
        )

    norm_pair(core).start()
    norm_pair(1 - core).wait_recv()
    scalars[chip] = scalars[experts] + scalars[experts + 1]

    def norm_copy(j, block, peer):
        return pltpu.make_async_remote_copy(
            src_ref=scalars.at[block],
            dst_ref=scalars.at[block],
            send_sem=norm_send.at[j],
            recv_sem=norm_recv.at[j],
            device_id=(core, peer),
            device_id_type=MESH,
        )

    @pl.loop(1, experts)
    def _(j):
        norm_copy(j, chip, lax.rem(chip + j, experts)).start()

    swap(1 - core).wait_recv()
    for side in range(2):
        for part in range(2):
            for g in range(3):
                lanes = (side * 2 + part) * D + g * 128
                place = (2 * g + part) * rows
                attn_out[:, lanes : lanes + 128] = final[side, place : place + rows, :]
    phi_out[...] = final[0, 6 * rows : 6 * rows + experts, 0:rows]
    norm_out[...] = final[1, 6 * rows : 6 * rows + 4, 0:rows]

    @pl.loop(1, experts)
    def _(j):
        source = lax.rem(chip - j + experts, experts)
        norm_copy(j, source, source).wait_recv()

    total_ref[...] = jnp.sqrt(jnp.sum(scalars[0:experts], axis=0))
    swap(core).wait_send()
    norm_pair(core).wait_send()

    @pl.loop(0, experts)
    def _(block):
        pair_copy(block).wait_send()

    @pl.loop(0, 2 * layers)
    def _(index):
        to_first(index).wait_send()

    @pl.loop(0, layers)
    def _(index):
        to_second(index).wait_send()

    @pl.loop(1, layers)
    def _(d):
        to_layer(lax.rem(layer + d, layers)).wait_send()

    @pl.loop(1, experts)
    def _(j):
        norm_copy(j, chip, lax.rem(chip + j, experts)).wait_send()


def reduce_grads(grads, squares, experts):
    rows = D // experts
    layers = experts // 4
    block = grads.shape[2:]
    shape = jax.ShapeDtypeStruct
    dma = pltpu.SemaphoreType.DMA
    return pl.pallas_call(
        functools.partial(reduce_kernel, experts),
        out_shape=(
            shape((rows, 4 * D), F32),
            shape((experts, rows), F32),
            shape((4, rows), F32),
            shape((1, 128), F32),
        ),
        in_specs=[pl.BlockSpec(memory_space=pl.ANY)] + whole(1),
        out_specs=tuple(whole(4)),
        scratch_shapes=[
            pltpu.VMEM((experts,) + block, F32),
            pltpu.VMEM((experts,) + block, F32),
            pltpu.VMEM((2 * layers,) + block, BF16),
            pltpu.VMEM((2 * layers,) + block, BF16),
            pltpu.VMEM((layers,) + block, BF16),
            pltpu.VMEM((layers,) + block, BF16),
            pltpu.VMEM((layers,) + block, BF16),
            pltpu.VMEM((layers,) + block, BF16),
            pltpu.VMEM((2,) + block, F32),
            pltpu.VMEM((experts + 2, 1, 128), F32),
            dma((1,)),
            dma((experts,)),
            dma((experts,)),
            dma((2 * layers,)),
            dma((2 * layers,)),
            dma((layers,)),
            dma((layers,)),
            dma((layers,)),
            dma((layers,)),
            dma((4,)),
            dma((experts,)),
            dma((experts,)),
        ],
        compiler_params=pltpu.CompilerParams(
            collective_id=2, has_side_effects=True, vmem_limit_bytes=VMEM_BYTES
        ),
        name="reduce_grads",
    )(grads, squares)


def adam_update(weight, first_moment, second_moment, gradient, factor, learning_rate, decay_rate):
    clipped = gradient * factor
    first_new = BETA_FIRST * first_moment + (1.0 - BETA_FIRST) * clipped
    second_new = BETA_SECOND * second_moment + (1.0 - BETA_SECOND) * clipped * clipped
    first_hat = first_new / (1.0 - BETA_FIRST**STEP)
    second_hat = second_new / (1.0 - BETA_SECOND**STEP)
    weight_new = weight - learning_rate * (
        first_hat / (jnp.sqrt(second_hat) + ADAM_EPS) + decay_rate * weight
    )
    return (weight_new, first_new, second_new)


def pad_to(array, shape):
    return jnp.pad(array, [(0, full - size) for size, full in zip(array.shape, shape)])


def regroup_weights(blocks, experts):
    rows = D // experts
    if rows == GROUP_ROWS:
        return blocks
    main = blocks[:, :, : 6 * rows].reshape(experts, 2, 3, 2, rows, 128).transpose(1, 2, 3, 0, 4, 5)
    main = main.reshape(2, 3, 2, GROUPS, GROUP_ROWS, 128).transpose(3, 0, 1, 2, 4, 5)
    main = main.reshape(GROUPS, 2, 6 * GROUP_ROWS, 128)
    small_rows = max(experts, 16)
    small = blocks[:, :, 6 * rows :, :rows]
    small = pad_to(small[:, :, :small_rows], (experts, 2, small_rows, rows))
    small = small.transpose(1, 2, 0, 3).reshape(2, small_rows, GROUPS, GROUP_ROWS)
    small = pad_to(small.transpose(2, 0, 1, 3), (GROUPS, 2, small_rows, 128))
    return jnp.concatenate([main, small], axis=2)


def regroup_grads(groups, experts):
    rows = D // experts
    if rows == GROUP_ROWS:
        return groups
    main = groups[:, :, : 6 * GROUP_ROWS].reshape(2, GROUPS, 3, 2, GROUP_ROWS, 128)
    main = main.transpose(0, 2, 3, 1, 4, 5).reshape(2, 3, 2, experts, rows, 128)
    main = main.transpose(0, 3, 1, 2, 4, 5).reshape(2, experts, 6 * rows, 128)
    small = groups[:, :, 6 * GROUP_ROWS :, :GROUP_ROWS]
    small_rows = min(small.shape[2], block_rows(experts) - 6 * rows)
    small = small[:, :, :small_rows].transpose(0, 2, 1, 3).reshape(2, small_rows, experts, rows)
    small = pad_to(small.transpose(0, 2, 1, 3), (2, experts, small_rows, 128))
    both = jnp.concatenate([main, small], axis=2)
    return pad_to(both, (2, experts, block_rows(experts), 128))


def local(
    patches,
    slot_len,
    attn_weight,
    attn_first,
    attn_second,
    phi_weight,
    phi_first,
    phi_second,
    norm_params,
    norm_first,
    norm_second,
    expert_in,
    in_first,
    in_second,
    expert_out,
    out_first,
    out_second,
    cotangent,
):
    experts = lax.axis_size("expert")
    weights = gather_weights(attn_weight, phi_weight.T, norm_params, experts)
    weights = regroup_weights(weights, experts)
    *saved, packed = forward_local(slot_len, patches, weights, cotangent, experts)
    result, gslots, grad_in, grad_out, squares = run_experts(packed, expert_in, expert_out, experts)
    block_output, input_grad, grads = backward_local(
        slot_len, patches, weights, saved, result, gslots, experts
    )
    grads = regroup_grads(grads, experts)
    attn_part, phi_part, norm_part, norm_tile = reduce_grads(grads, squares, experts)
    phi_part = phi_part.T
    grad_norm = norm_tile[0, 0]
    factor = CLIP_NORM / jnp.maximum(grad_norm, CLIP_NORM)
    attn_new, attn_first_new, attn_second_new = adam_update(
        attn_weight, attn_first, attn_second, attn_part, factor, 1.0 / math.sqrt(D), WEIGHT_DECAY
    )
    phi_new, phi_first_new, phi_second_new = adam_update(
        phi_weight, phi_first, phi_second, phi_part, factor, 0.25 / math.sqrt(D), WEIGHT_DECAY
    )
    norm_new, norm_first_new, norm_second_new = adam_update(
        norm_params, norm_first, norm_second, norm_part, factor, 0.8, 0.0
    )
    in_new, in_first_new, in_second_new = adam_update(
        expert_in, in_first, in_second, grad_in, factor, 4.0 / math.sqrt(D), WEIGHT_DECAY
    )
    out_new, out_first_new, out_second_new = adam_update(
        expert_out, out_first, out_second, grad_out, factor, 8.0 / math.sqrt(FF), WEIGHT_DECAY
    )
    return (
        block_output,
        input_grad,
        grad_norm,
        attn_new,
        attn_first_new,
        attn_second_new,
        phi_new,
        phi_first_new,
        phi_second_new,
        norm_new,
        norm_first_new,
        norm_second_new,
        in_new,
        in_first_new,
        in_second_new,
        out_new,
        out_first_new,
        out_second_new,
    )


def solution(mesh):
    in_specs = (
        P(("batch", "expert"), None),
        P(("batch", "expert"), None),
        P("expert", None),
        P("expert", None),
        P("expert", None),
        P("expert", None),
        P("expert", None),
        P("expert", None),
        P(None, "expert"),
        P(None, "expert"),
        P(None, "expert"),
        P("expert", None, "batch"),
        P("expert", None, "batch"),
        P("expert", None, "batch"),
        P("expert", "batch", None),
        P("expert", "batch", None),
        P("expert", "batch", None),
        P(("batch", "expert"), None),
    )
    out_specs = (
        P(("batch", "expert"), None),
        P(("batch", "expert"), None),
        P(),
        P("expert", None),
        P("expert", None),
        P("expert", None),
        P("expert", None),
        P("expert", None),
        P("expert", None),
        P(None, "expert"),
        P(None, "expert"),
        P(None, "expert"),
        P("expert", None, "batch"),
        P("expert", None, "batch"),
        P("expert", None, "batch"),
        P("expert", "batch", None),
        P("expert", "batch", None),
        P("expert", "batch", None),
    )
    return jax.shard_map(local, mesh=mesh, in_specs=in_specs, out_specs=out_specs, check_vma=False)
```

```python
import functools
import math

import jax
import jax.numpy as jnp
from jax import lax
from jax.experimental import pallas as pl
from jax.experimental.pallas import tpu as pltpu
from jax.sharding import PartitionSpec as P

D = 384
HEADS = 6
HEAD_DIM = 64
FF = 1536
STEP = 3
SHORT_LEN = 196
LONG_LEN = 576
IMAGES = 5
SLOT_ROWS = 8
PAIRS = 3
GROUPS = 16
GROUP_ROWS = D // GROUPS
LONG_WINDOW = 592
LONG_SPAN = 640
WINDOW_PAD = 48

NORM_EPS = 1e-06
CLIP_NORM = 1.0
BETA_FIRST = 0.5
BETA_SECOND = 0.5
ADAM_EPS = 1e-08
WEIGHT_DECAY = 0.05
MASKED = -1e30
SCORE_SCALE = HEAD_DIM ** (-0.5)

MESH = pl.DeviceIdType.MESH
F32 = jnp.float32
BF16 = jnp.bfloat16


def vmem_bytes(experts, mebibytes):
    return (mebibytes if experts <= 16 else 58) * 1024 * 1024


def whole(count):
    return [pl.BlockSpec(memory_space=pltpu.VMEM)] * count


def round_up(value, unit):
    return -(-value // unit) * unit


def mm(left, right):
    return jnp.dot(left, right, preferred_element_type=F32)


def mm_nt(left, right):
    return lax.dot_general(left, right, (((1,), (1,)), ((), ())), preferred_element_type=F32)


def mm_tn(left, right):
    return lax.dot_general(left, right, (((0,), (0,)), ((), ())), preferred_element_type=F32)


def block_rows(experts):
    rows = D // experts
    return round_up(6 * rows + max(experts, 4), 16)


def ring(experts):
    core = lax.axis_index("batch")
    chip = lax.axis_index("expert")
    first = chip ^ (1 + core)
    second = chip ^ (2 - core)
    return core, chip, first, second


def gather_kernel(experts, attn_hbm, phi_hbm, norm_hbm, out, stage, attn_ref, phi_ref, norm_ref, load_sem,
                  send_z, send_first, send_second, send_pair, recv, recv_pair):
    core, chip, first, second = ring(experts)
    rows = attn_ref.shape[0]
    half = pl.multiple_of(core * (2 * D), 128)
    loads = [
        pltpu.make_async_copy(attn_hbm.at[:, pl.ds(half, 2 * D)], attn_ref, load_sem.at[0]),
        pltpu.make_async_copy(phi_hbm, phi_ref, load_sem.at[1]),
        pltpu.make_async_copy(norm_hbm, norm_ref, load_sem.at[2]),
    ]
    for load in loads:
        load.start()
    column = lax.rem(chip, 4)
    layers = experts // 4
    layer = chip // 4
    barrier = pltpu.get_barrier_semaphore()

    @pl.loop(1, layers)
    def _(d):
        peer = lax.rem(layer + d, layers) * 4 + column
        pl.semaphore_signal(barrier, inc=1, device_id=(core, peer), device_id_type=MESH)

    pl.semaphore_signal(barrier, inc=1, device_id=(core, first), device_id_type=MESH)
    pl.semaphore_signal(barrier, inc=1, device_id=(core, second), device_id_type=MESH)
    pl.semaphore_signal(barrier, inc=1, device_id=(1 - core, chip), device_id_type=MESH)
    stage[...] = jnp.zeros_like(stage)
    for load in loads:
        load.wait()
    for part in range(2):
        for g in range(3):
            lanes = part * D + g * 128
            place = (2 * g + part) * rows
            stage[place : place + rows, :] = attn_ref[:, lanes : lanes + 128]

    @pl.when(core == 0)
    def _():
        stage[6 * rows : 6 * rows + experts, 0:rows] = phi_ref[...]

    @pl.when(core == 1)
    def _():
        stage[6 * rows : 6 * rows + 4, 0:rows] = norm_ref[...]

    out[chip, core] = stage[...].astype(BF16)
    pl.semaphore_wait(barrier, layers + 2)

    def copy(block, side, sems, sem, arrivals, device):
        return pltpu.make_async_remote_copy(
            src_ref=out.at[block, side],
            dst_ref=out.at[block, side],
            send_sem=sems.at[sem],
            recv_sem=arrivals.at[block],
            device_id=device,
            device_id_type=MESH,
        )

    def along_z(d):
        peer = lax.rem(layer + d, layers) * 4 + column
        return copy(chip, core, send_z, d, recv, (core, peer))

    def to_first(block):
        return copy(block, core, send_first, block, recv, (core, first))

    def to_second(block):
        return copy(block, core, send_second, block, recv, (core, second))

    def to_pair(block):
        return copy(block, core, send_pair, block, recv_pair, (1 - core, chip))

    @pl.loop(1, layers)
    def _(d):
        along_z(d).start()

    to_first(chip).start()
    to_second(chip).start()
    to_pair(chip).start()

    @pl.loop(1, layers)
    def _(d):
        block = lax.rem(layer - d + layers, layers) * 4 + column
        to_first(block).wait_recv()
        to_first(block).start()
        to_second(block).start()
        to_pair(block).start()

    @pl.loop(0, layers)
    def _(d):
        block = lax.rem(layer - d + layers, layers) * 4 + lax.rem(first, 4)
        to_first(block).wait_recv()
        to_second(block).start()
        to_pair(block).start()

    @pl.loop(0, 2 * layers)
    def _(d):
        other = jnp.where(lax.rem(d, 2) == 0, lax.rem(second, 4), lax.rem(3 - column, 4))
        block = lax.rem(layer - d // 2 + layers, layers) * 4 + other
        to_first(block).wait_recv()
        to_pair(block).start()

    @pl.loop(1, layers)
    def _(d):
        along_z(d).wait_send()

    @pl.loop(0, layers)
    def _(d):
        block = d * 4 + column
        to_first(block).wait_send()
        to_second(block).wait_send()
        to_second(d * 4 + lax.rem(first, 4)).wait_send()

    @pl.loop(0, experts)
    def _(block):
        to_pair(block).wait_send()
        copy(block, 1 - core, send_pair, block, recv_pair, (1 - core, chip)).wait_recv()


def gather_weights(attn_weight, phi_turned, norm_params, experts):
    rows = block_rows(experts)
    dma = pltpu.SemaphoreType.DMA
    return pl.pallas_call(
        functools.partial(gather_kernel, experts),
        out_shape=jax.ShapeDtypeStruct((experts, 2, rows, 128), BF16),
        in_specs=[pl.BlockSpec(memory_space=pltpu.HBM)] * 3,
        out_specs=whole(1)[0],
        scratch_shapes=[
            pltpu.VMEM((rows, 128), F32),
            pltpu.VMEM((attn_weight.shape[0], 2 * D), F32),
            pltpu.VMEM(phi_turned.shape, F32),
            pltpu.VMEM(norm_params.shape, F32),
            dma((3,)),
            dma((experts // 4,)),
        ]
        + [dma((experts,))] * 5,
        compiler_params=pltpu.CompilerParams(
            collective_id=0, has_side_effects=True, vmem_limit_bytes=vmem_bytes(experts, 3)
        ),
        name="gather_weights",
    )(attn_weight, phi_turned, norm_params)


def unpack_weight(main_ref, side, part):
    blocks = main_ref[:, side].astype(F32)
    columns = []
    for g in range(3):
        place = (2 * g + part) * GROUP_ROWS
        columns.append(blocks[:, place : place + GROUP_ROWS, :].reshape(D, 128))
    return jnp.concatenate(columns, axis=1).astype(BF16)


def group_lanes():
    lane = lax.broadcasted_iota(jnp.int32, (128, D), 0)
    column = lax.broadcasted_iota(jnp.int32, (128, D), 1)
    return jnp.where(column % GROUP_ROWS == lane, 1.0, 0.0).astype(BF16)


def unpack_turned(main_ref, side, rows):
    first = 6 * GROUP_ROWS
    blocks = main_ref[:, side].astype(F32)[:, first : first + rows, :]
    spread = mm(blocks.reshape(GROUPS * rows, 128).astype(BF16), group_lanes())
    spread = spread.reshape(GROUPS, rows, D)
    group = lax.broadcasted_iota(jnp.int32, (GROUPS, 1, D), 0)
    column = lax.broadcasted_iota(jnp.int32, (GROUPS, 1, D), 2)
    return jnp.sum(jnp.where(column // GROUP_ROWS == group, spread, 0.0), axis=0)


def pack_turned(values):
    rows = values.shape[0]
    group = lax.broadcasted_iota(jnp.int32, (GROUPS, 1, D), 0)
    column = lax.broadcasted_iota(jnp.int32, (GROUPS, 1, D), 2)
    spread = jnp.where(column // GROUP_ROWS == group, values[None], 0.0)
    spread = spread.reshape(GROUPS * rows, D).astype(BF16)
    return mm_nt(spread, group_lanes()).reshape(GROUPS, rows, 128)


def unpack_small(main_ref, experts):
    turned = unpack_turned(main_ref, 0, max(experts, 16)).astype(BF16)
    row = lax.broadcasted_iota(jnp.int32, (experts * SLOT_ROWS, turned.shape[0]), 0)
    column = lax.broadcasted_iota(jnp.int32, (experts * SLOT_ROWS, turned.shape[0]), 1)
    spread = jnp.where(column == row // SLOT_ROWS, 1.0, 0.0).astype(BF16)
    return mm(spread, turned).astype(BF16), unpack_turned(main_ref, 1, 8)


def slot_bounds(len_ref, columns):
    image = lax.broadcasted_iota(jnp.int32, (1, columns), 1) % SLOT_ROWS
    starts = jnp.zeros((1, columns), jnp.int32)
    ends = jnp.zeros((1, columns), jnp.int32)
    start = jnp.int32(0)
    for k in range(IMAGES):
        end = start + len_ref[0, k]
        starts = jnp.where(image == k, start, starts)
        ends = jnp.where(image == k, end, ends)
        start = end
    return starts, ends, start


def normed(values):
    centred = values - jnp.mean(values, axis=-1, keepdims=True)
    variance = jnp.mean(centred * centred, axis=-1, keepdims=True)
    inverse = lax.rsqrt(variance + NORM_EPS)
    return centred * inverse, inverse


def norm_back(grad_shaped, normal, inverse, scaling):
    grad_normal = grad_shaped * scaling
    return inverse * (
        grad_normal
        - jnp.mean(grad_normal, axis=-1, keepdims=True)
        - normal * jnp.mean(grad_normal * normal, axis=-1, keepdims=True)
    )


def over_images(len_ref, tokens, body):
    def step(k, start):
        length = len_ref[0, k]
        for full in (SHORT_LEN, LONG_LEN):

            @pl.when(length == full)
            def _():
                window = round_up(full + 12, 16)
                first = jnp.minimum((start // 16) * 16, tokens - window)
                body(pl.multiple_of(first, 16), start - first, full, window)

        return start + length

    lax.fori_loop(0, IMAGES, step, jnp.int32(0))


def rows_inside(shift, full, first, count):
    row = first + lax.broadcasted_iota(jnp.int32, (count, 1), 0)
    return (row >= shift) & (row < shift + full)


def columns_inside(shift, full, count):
    column = lax.broadcasted_iota(jnp.int32, (1, count), 1)
    return (column >= shift) & (column < shift + full)


def forward_kernel(experts, len_ref, patch_ref, main_ref, cot_hbm, qkv_ref, o_ref, lse_ref, x1_ref,
                   h2_ref, disp_ref, comb_ref, gy_ref, pack_ref, logit, packf, scores,
                   probs, peaks, cot_ref, load_sem):
    load = pltpu.make_async_copy(cot_hbm, cot_ref, load_sem.at[0])
    load.start()
    tokens = patch_ref.shape[0]
    columns = experts * SLOT_ROWS
    tile = tokens // 5
    phi, norms = unpack_small(main_ref, experts)
    starts, ends, total = slot_bounds(len_ref, columns)
    w_q, w_k = unpack_weight(main_ref, 0, 0), unpack_weight(main_ref, 0, 1)
    w_v = unpack_weight(main_ref, 1, 0)
    w_qkv = jnp.concatenate([w_q, w_k, w_v], axis=1)
    for t in range(5):
        rows = pl.ds(t * tile, tile)
        normal, _ = normed(patch_ref[rows, :].astype(F32))
        h1 = (normal * norms[0:1] + norms[1:2]).astype(BF16)
        qkv = mm(h1, w_qkv).astype(BF16)
        for c in range(9):
            qkv_ref[c, rows, :] = qkv[:, c * 128 : (c + 1) * 128]
    qkv_ref[:, tokens:, :] = jnp.zeros((9, WINDOW_PAD, 128), BF16)
    o_ref[...] = jnp.zeros_like(o_ref)
    lse_ref[...] = jnp.zeros_like(lse_ref)
    low_lane = lax.broadcasted_iota(jnp.int32, (1, 128), 1) < HEAD_DIM
    lane = lax.broadcasted_iota(jnp.int32, (1, 128), 1)

    def attend(first, shift, full, window):
        span = round_up(window, 128)
        bias = jnp.where(columns_inside(shift, full, span), 0.0, MASKED)
        inside = rows_inside(shift, full, 0, window)
        rows = pl.ds(first, window)
        wide = pl.ds(first, span)

        @pl.loop(0, PAIRS)
        def _(p):
            query = qkv_ref[p, rows, :].astype(F32) * SCORE_SCALE
            keys = qkv_ref[PAIRS + p, wide, :]
            ones = jnp.ones((span, 128), BF16)
            values = jnp.concatenate([qkv_ref[2 * PAIRS + p, wide, :], ones], axis=1)
            for h in range(2):
                mine = low_lane if h == 0 else jnp.logical_not(low_lane)
                scores[h, :window, :span] = mm_nt(jnp.where(mine, query, 0.0).astype(BF16), keys)
            for h in range(2):
                for r in range(0, window, 16):
                    part = scores[h, r : r + 16, :span] + bias
                    peak = jnp.max(part, axis=-1, keepdims=True)
                    probs[h, r : r + 16, :span] = jnp.exp(part - peak).astype(BF16)
                    peaks[h, r : r + 16, :] = jnp.broadcast_to(peak, (16, 128))
            outs = []
            sums = lse_ref[rows, :]
            for h in range(2):
                both = mm(probs[h, :window, :span], values)
                summed = both[:, 128:]
                outs.append(both[:, :128] * (1.0 / summed))
                logs = peaks[h, :window, :] + jnp.log(summed)
                sums = jnp.where(inside & (lane == 2 * p + h), logs, sums)
            lse_ref[rows, :] = sums
            lanes = pl.ds(pl.multiple_of(p * 128, 128), 128)
            old = o_ref[rows, lanes].astype(F32)
            merged = jnp.where(inside, jnp.where(low_lane, outs[0], outs[1]), old)
            o_ref[rows, lanes] = merged.astype(BF16)

    over_images(len_ref, tokens, attend)

    load.wait()
    w_o = unpack_weight(main_ref, 1, 1)
    for t in range(5):
        rows = pl.ds(t * tile, tile)
        x1 = patch_ref[rows, :].astype(F32) + mm(o_ref[rows, :], w_o)
        normal, _ = normed(x1)
        h2 = (normal * norms[2:3] + norms[3:4]).astype(BF16)
        h2_ref[rows, :] = h2
        logit[rows, :] = mm_nt(h2, phi)
        position = t * tile + lax.broadcasted_iota(jnp.int32, (tile, 1), 0)
        valid = position < total
        x1_ref[rows, :] = jnp.where(valid, x1, 0.0)
        gy_ref[rows, :] = jnp.where(valid, cot_ref[rows, :].astype(F32), 0.0).astype(BF16)

    position = lax.broadcasted_iota(jnp.int32, (tokens, columns), 0)
    member = (position >= starts) & (position < ends)
    present = ends > starts
    logits = logit[...]
    peak = jnp.max(jnp.where(member, logits, MASKED), axis=0, keepdims=True)
    peak = jnp.where(present, peak, 0.0)
    exponent = jnp.where(member, jnp.exp(jnp.where(member, logits - peak, 0.0)), 0.0)
    summed = jnp.sum(exponent, axis=0, keepdims=True) + jnp.where(present, 0.0, 1.0)
    dispatch = exponent / summed
    disp_ref[...] = dispatch
    slots = mm_tn(dispatch.astype(BF16), h2_ref[...])
    row_peak = jnp.max(logits, axis=-1, keepdims=True)
    exponent = jnp.exp(logits - row_peak)
    summed = jnp.sum(exponent, axis=-1, keepdims=True) * (1.0 / SLOT_ROWS)
    combine = jnp.where(member, exponent / summed, 0.0)
    comb_ref[...] = combine
    grad_result = mm_tn(combine.astype(BF16), gy_ref[...])
    for part, matrix in enumerate((slots, grad_result)):
        pack_rows(packf, matrix.reshape(experts, SLOT_ROWS, D))
        pack_ref[:, part * 16 : (part + 1) * 16, :] = packf[...].astype(BF16)


def pack_rows(packf, blocks):
    packf[...] = jnp.zeros_like(packf)
    for c in range(3):
        packf[:, c * IMAGES : (c + 1) * IMAGES, :] = blocks[:, :IMAGES, c * 128 : (c + 1) * 128]


def unpack_rows(packf, wide):
    wide[...] = jnp.zeros_like(wide)
    for c in range(3):
        wide[:, 0:IMAGES, c * 128 : (c + 1) * 128] = packf[:, c * IMAGES : (c + 1) * IMAGES, :]


def forward_local(lengths, patches, main, cotangent, experts):
    tokens = patches.shape[0]
    columns = experts * SLOT_ROWS
    shape = jax.ShapeDtypeStruct
    return pl.pallas_call(
        functools.partial(forward_kernel, experts),
        out_shape=(
            shape((9, tokens + WINDOW_PAD, 128), BF16),
            shape((tokens + WINDOW_PAD, D), BF16),
            shape((tokens + WINDOW_PAD, 128), F32),
            shape((tokens, D), F32),
            shape((tokens, D), BF16),
            shape((tokens, columns), F32),
            shape((tokens, columns), F32),
            shape((tokens, D), BF16),
            shape((experts, 32, 128), BF16),
        ),
        in_specs=[pl.BlockSpec(memory_space=pltpu.SMEM)]
        + whole(2)
        + [pl.BlockSpec(memory_space=pltpu.HBM)],
        out_specs=tuple(whole(9)),
        scratch_shapes=[
            pltpu.VMEM((tokens, columns), F32),
            pltpu.VMEM((experts, 16, 128), F32),
            pltpu.VMEM((2, LONG_WINDOW, LONG_SPAN), F32),
            pltpu.VMEM((2, LONG_WINDOW, LONG_SPAN), BF16),
            pltpu.VMEM((2, LONG_WINDOW, 128), F32),
            pltpu.VMEM((tokens, D), BF16),
            pltpu.SemaphoreType.DMA((1,)),
        ],
        compiler_params=pltpu.CompilerParams(vmem_limit_bytes=vmem_bytes(experts, 22)),
        name="forward_local",
    )(lengths, patches, main, cotangent)


def expert_kernel(experts, pack_ref, in_ref, out_ref, result_ref, gslot_ref, gin_ref, gout_ref,
                  square_ref, inbox, partial, given, outbox, back, packf, wide, packe, widee,
                  send_one, recv_one, pair_send, pair_recv, send_two, recv_two, sum_sem):
    core = lax.axis_index("batch")
    chip = lax.axis_index("expert")
    barrier = pltpu.get_barrier_semaphore()

    @pl.loop(1, experts)
    def _(j):
        peer = lax.rem(chip + j, experts)
        pl.semaphore_signal(barrier, inc=1, device_id=(core, peer), device_id_type=MESH)

    pl.semaphore_signal(barrier, inc=1, device_id=(1 - core, chip), device_id_type=MESH)
    w_in = in_ref[0].astype(BF16)
    w_out = out_ref[0].astype(BF16)
    inbox[core, chip] = pack_ref[chip]
    pl.semaphore_wait(barrier, experts)

    def first(j, block, peer):
        return pltpu.make_async_remote_copy(
            src_ref=pack_ref.at[peer],
            dst_ref=inbox.at[core, block],
            send_sem=send_one.at[j],
            recv_sem=recv_one.at[j],
            device_id=(core, peer),
            device_id_type=MESH,
        )

    def to_pair(side, block):
        return pltpu.make_async_remote_copy(
            src_ref=inbox.at[side, block],
            dst_ref=inbox.at[side, block],
            send_sem=pair_send.at[block],
            recv_sem=pair_recv.at[block],
            device_id=(1 - core, chip),
            device_id_type=MESH,
        )

    def second(j, block, peer):
        return pltpu.make_async_remote_copy(
            src_ref=outbox.at[peer],
            dst_ref=back.at[block],
            send_sem=send_two.at[j],
            recv_sem=recv_two.at[j],
            device_id=(core, peer),
            device_id_type=MESH,
        )

    @pl.loop(1, experts)
    def _(j):
        first(j, chip, lax.rem(chip + j, experts)).start()

    to_pair(core, chip).start()

    @pl.loop(1, experts)
    def _(j):
        source = lax.rem(chip - j + experts, experts)
        first(j, source, source).wait_recv()
        to_pair(core, source).start()

    @pl.loop(0, experts)
    def _(block):
        to_pair(1 - core, block).wait_recv()

    def spread(side, part):
        packe[...] = inbox[side, :, part * 16 : (part + 1) * 16, :].astype(F32)
        unpack_rows(packe, widee)
        return widee[...].reshape(experts * SLOT_ROWS, D).astype(BF16)

    def run(side):
        slots = spread(side, 0)
        grads = spread(side, 1)
        hidden = mm(slots, w_in)
        root = math.sqrt(2.0 / math.pi)
        bent = jnp.tanh(root * (hidden + 0.044715 * (hidden * hidden * hidden)))
        half = 0.5 * (1.0 + bent)
        act = (hidden * half).astype(BF16)
        slope = half + 0.5 * hidden * (1.0 - bent * bent) * (
            root * (1.0 + 3.0 * 0.044715 * (hidden * hidden))
        )
        result = mm(act, w_out)
        grad_hidden = (mm_nt(grads, w_out) * slope).astype(BF16)
        grad_slots = mm_nt(grad_hidden, w_in)
        return slots, grads, act, grad_hidden, result, grad_slots

    theirs = run(1 - core)
    for part in range(2):
        pack_rows(packf, theirs[4 + part].reshape(experts, SLOT_ROWS, D))
        partial[:, part * 16 : (part + 1) * 16, :] = packf[...].astype(BF16)
    halves = pltpu.make_async_remote_copy(
        src_ref=partial,
        dst_ref=given,
        send_sem=sum_sem.at[0],
        recv_sem=sum_sem.at[1],
        device_id=(1 - core, chip),
        device_id_type=MESH,
    )
    halves.start()
    ours = run(core)
    halves.wait_recv()
    for part in range(2):
        block = slice(part * 16, (part + 1) * 16)
        pack_rows(packf, ours[4 + part].reshape(experts, SLOT_ROWS, D))
        outbox[:, block, :] = (packf[...] + given[:, block, :].astype(F32)).astype(BF16)

    @pl.loop(1, experts)
    def _(j):
        second(j, chip, lax.rem(chip + j, experts)).start()

    back[chip] = outbox[chip]
    grad_out = mm_tn(ours[2], ours[1]) + mm_tn(theirs[2], theirs[1])
    gout_ref[0] = grad_out
    grad_in = mm_tn(ours[0], ours[3]) + mm_tn(theirs[0], theirs[3])
    gin_ref[0] = grad_in
    squares = jnp.sum(grad_out * grad_out) + jnp.sum(grad_in * grad_in)
    square_ref[...] = jnp.full(square_ref.shape, squares, F32)

    @pl.loop(1, experts)
    def _(j):
        source = lax.rem(chip - j + experts, experts)
        second(j, source, source).wait_recv()

    for part, target in enumerate((result_ref, gslot_ref)):
        packe[...] = back[:, part * 16 : (part + 1) * 16, :].astype(F32)
        unpack_rows(packe, widee)
        target[...] = widee[...].reshape(experts * SLOT_ROWS, D).astype(BF16)

    halves.wait_send()

    @pl.loop(1, experts)
    def _(j):
        peer = lax.rem(chip + j, experts)
        first(j, chip, peer).wait_send()
        second(j, chip, peer).wait_send()

    @pl.loop(0, experts)
    def _(block):
        to_pair(core, block).wait_send()


def run_experts(packed, expert_in, expert_out, experts):
    shape = jax.ShapeDtypeStruct
    dma = pltpu.SemaphoreType.DMA
    return pl.pallas_call(
        functools.partial(expert_kernel, experts),
        out_shape=(
            shape((experts * SLOT_ROWS, D), BF16),
            shape((experts * SLOT_ROWS, D), BF16),
            shape(expert_in.shape, F32),
            shape(expert_out.shape, F32),
            shape((1, 128), F32),
        ),
        in_specs=whole(3),
        out_specs=tuple(whole(5)),
        scratch_shapes=[
            pltpu.VMEM((2, experts, 32, 128), BF16),
            pltpu.VMEM((experts, 32, 128), BF16),
            pltpu.VMEM((experts, 32, 128), BF16),
            pltpu.VMEM((experts, 32, 128), BF16),
            pltpu.VMEM((experts, 32, 128), BF16),
            pltpu.VMEM((experts, 16, 128), F32),
            pltpu.VMEM((experts, SLOT_ROWS, D), F32),
            pltpu.VMEM((experts, 16, 128), F32),
            pltpu.VMEM((experts, SLOT_ROWS, D), F32),
        ]
        + [dma((experts,))] * 6
        + [dma((2,))],
        compiler_params=pltpu.CompilerParams(
            collective_id=1, has_side_effects=True, vmem_limit_bytes=vmem_bytes(experts, 8)
        ),
        name="run_experts",
    )(packed, expert_in, expert_out)


def backward_kernel(experts, len_ref, patch_ref, main_ref, qkv_ref, o_ref, lse_ref,
                    x1_ref, h2_ref, disp_ref, comb_ref, gy_ref, result_ref, gslot_ref, block_ref,
                    input_ref, gw_ref, gdisp, glog, gx1, branch, go, gqkv,
                    h1_all, scores, grad_probs, probs, grad_scores, sums):
    tokens = patch_ref.shape[0]
    columns = experts * SLOT_ROWS
    tile = tokens // 5
    phi, norms = unpack_small(main_ref, experts)
    result = result_ref[...]
    gslots = gslot_ref[...]

    inner = jnp.zeros((1, columns), F32)
    for t in range(5):
        rows = pl.ds(t * tile, tile)
        grad_dispatch = mm_nt(h2_ref[rows, :], gslots)
        gdisp[rows, :] = grad_dispatch
        inner = inner + jnp.sum(disp_ref[rows, :] * grad_dispatch, axis=0, keepdims=True)

    w_o = unpack_weight(main_ref, 1, 1)
    gain_two = jnp.zeros((1, D), F32)
    bias_two = jnp.zeros((1, D), F32)
    for t in range(5):
        rows = pl.ds(t * tile, tile)
        dispatch, combine, gy = disp_ref[rows, :], comb_ref[rows, :], gy_ref[rows, :]
        x1 = x1_ref[rows, :]
        mixed = mm(combine.astype(BF16), result)
        block_ref[rows, :] = (x1 + mixed).astype(BF16)
        weighted = combine * mm_nt(gy, result)
        grad_logits = (
            weighted
            - combine * jnp.sum(weighted, axis=-1, keepdims=True)
            + dispatch * (gdisp[rows, :] - inner)
        ).astype(BF16)
        glog[rows, :] = grad_logits
        grad_h2 = mm(dispatch.astype(BF16), gslots) + mm(grad_logits, phi)
        normal, inverse = normed(x1)
        gain_two = gain_two + jnp.sum(grad_h2 * normal, axis=0, keepdims=True)
        bias_two = bias_two + jnp.sum(grad_h2, axis=0, keepdims=True)
        grad_x1 = gy.astype(F32) + norm_back(grad_h2, normal, inverse, norms[2:3])
        gx1[rows, :] = grad_x1
        grad_branch = grad_x1.astype(BF16)
        branch[rows, :] = grad_branch
        grad_o = mm_nt(grad_branch, w_o).astype(BF16)
        for c in range(PAIRS):
            go[c, rows, :] = grad_o[:, c * 128 : (c + 1) * 128]

    small_rows = gw_ref.shape[2] - 6 * GROUP_ROWS
    row = lax.broadcasted_iota(jnp.int32, (columns, small_rows), 0)
    column = lax.broadcasted_iota(jnp.int32, (columns, small_rows), 1)
    fold = jnp.where(column == row // SLOT_ROWS, 1.0, 0.0).astype(BF16)
    folded = mm(glog[...], fold).astype(BF16)
    gw_ref[0, :, 6 * GROUP_ROWS :, :] = pack_turned(mm_tn(folded, h2_ref[...]))

    def put(side, part, value):
        for g in range(3):
            place = (2 * g + part) * GROUP_ROWS
            gw_ref[side, :, place : place + GROUP_ROWS, :] = value[
                :, g * 128 : (g + 1) * 128
            ].reshape(GROUPS, GROUP_ROWS, 128)

    put(1, 1, mm_tn(o_ref[0:tokens, :], branch[...]))

    gqkv[...] = jnp.zeros_like(gqkv)
    go[:, tokens:, :] = jnp.zeros((PAIRS, WINDOW_PAD, 128), BF16)
    low_lane = lax.broadcasted_iota(jnp.int32, (1, 128), 1) < HEAD_DIM

    head_row = lax.broadcasted_iota(jnp.int32, (8, 128), 0)
    head_lane = lax.broadcasted_iota(jnp.int32, (8, 128), 1)
    heads = jnp.where(head_row == head_lane // HEAD_DIM, 1.0, 0.0).astype(BF16)

    def attend(first, shift, full, window):
        span = round_up(window, 128)
        inside = rows_inside(shift, full, 0, window)
        queries_inside = columns_inside(shift, full, span)
        rows = pl.ds(first, window)
        wide = pl.ds(first, span)
        sums[:, :span] = jnp.transpose(lse_ref[wide, :])

        @pl.loop(0, PAIRS)
        def _(p):
            lanes = pl.ds(pl.multiple_of(p * 128, 128), 128)
            query = qkv_ref[p, wide, :]
            keys_low = qkv_ref[PAIRS + p, rows, :]
            keys = keys_low.astype(F32) * SCORE_SCALE
            values = qkv_ref[2 * PAIRS + p, rows, :].astype(F32)
            grads = go[p, wide, :]
            product = grads.astype(F32) * o_ref[wide, lanes].astype(F32)
            upper = product.astype(BF16)
            lower = (product - upper.astype(F32)).astype(BF16)
            inner_rows = mm_nt(heads, upper) + mm_nt(heads, lower)
            for h in range(2):
                mine = low_lane if h == 0 else jnp.logical_not(low_lane)
                scores[h, :window, :span] = mm_nt(jnp.where(mine, keys, 0.0).astype(BF16), query)
                grad_probs[h, :window, :span] = mm_nt(
                    jnp.where(mine, values, 0.0).astype(BF16), grads
                )
            for h in range(2):
                logs = jnp.where(queries_inside, sums[pl.ds(2 * p + h, 1), :span], 1e30)
                inner_row = inner_rows[h : h + 1]
                for r in range(0, window, 16):
                    part = jnp.exp(scores[h, r : r + 16, :span] - logs)
                    if r == 0 or r + 16 > full:
                        part = jnp.where(rows_inside(shift, full, r, 16), part, 0.0)
                    probs[h, r : r + 16, :span] = part.astype(BF16)
                    slope = part * (grad_probs[h, r : r + 16, :span] - inner_row)
                    grad_scores[h, r : r + 16, :span] = slope.astype(BF16)
            parts = []
            for h in range(2):
                slopes = grad_scores[h, :window, :span]
                parts.append(
                    (
                        mm_tn(slopes, keys_low)[:window] * SCORE_SCALE,
                        mm(slopes, query) * SCORE_SCALE,
                        mm(probs[h, :window, :span], grads),
                    )
                )
            for c in range(3):
                old = gqkv[c * PAIRS + p, rows, :].astype(F32)
                new = jnp.where(low_lane, parts[0][c], parts[1][c])
                gqkv[c * PAIRS + p, rows, :] = jnp.where(inside, new, old).astype(BF16)

    over_images(len_ref, tokens, attend)

    w_q, w_k = unpack_weight(main_ref, 0, 0), unpack_weight(main_ref, 0, 1)
    w_v = unpack_weight(main_ref, 1, 0)
    w_qkv = jnp.concatenate([w_q, w_k, w_v], axis=1)
    gain_one = jnp.zeros((1, D), F32)
    bias_one = jnp.zeros((1, D), F32)
    for t in range(5):
        rows = pl.ds(t * tile, tile)
        grad_qkv = jnp.concatenate([gqkv[c, rows, :] for c in range(9)], axis=1)
        grad_h1 = mm_nt(grad_qkv, w_qkv)
        normal, inverse = normed(patch_ref[rows, :].astype(F32))
        h1_all[rows, :] = (normal * norms[0:1] + norms[1:2]).astype(BF16)
        gain_one = gain_one + jnp.sum(grad_h1 * normal, axis=0, keepdims=True)
        bias_one = bias_one + jnp.sum(grad_h1, axis=0, keepdims=True)
        grad_x = gx1[rows, :] + norm_back(grad_h1, normal, inverse, norms[0:1])
        input_ref[rows, :] = grad_x.astype(BF16)
    for c, (side, part) in enumerate(((0, 0), (0, 1), (1, 0))):
        grad = jnp.concatenate([gqkv[c * PAIRS + p] for p in range(PAIRS)], axis=1)
        put(side, part, mm_tn(h1_all[...], grad))
    zeros = jnp.zeros((small_rows - 4, D), F32)
    turned = jnp.concatenate([gain_one, bias_one, gain_two, bias_two, zeros], axis=0)
    gw_ref[1, :, 6 * GROUP_ROWS :, :] = pack_turned(turned)


def backward_local(lengths, patches, main, saved, result, gslots, experts):
    tokens = patches.shape[0]
    columns = experts * SLOT_ROWS
    shape = jax.ShapeDtypeStruct
    return pl.pallas_call(
        functools.partial(backward_kernel, experts),
        out_shape=(
            shape((tokens, D), BF16),
            shape((tokens, D), BF16),
            shape((2,) + (GROUPS,) + main.shape[2:], F32),
        ),
        in_specs=[pl.BlockSpec(memory_space=pltpu.SMEM)] + whole(12),
        out_specs=tuple(whole(3)),
        scratch_shapes=[
            pltpu.VMEM((tokens, columns), F32),
            pltpu.VMEM((tokens, columns), BF16),
            pltpu.VMEM((tokens, D), F32),
            pltpu.VMEM((tokens, D), BF16),
            pltpu.VMEM((PAIRS, tokens + WINDOW_PAD, 128), BF16),
            pltpu.VMEM((9, tokens, 128), BF16),
            pltpu.VMEM((tokens, D), BF16),
            pltpu.VMEM((2, LONG_WINDOW, LONG_SPAN), F32),
            pltpu.VMEM((2, LONG_WINDOW, LONG_SPAN), F32),
            pltpu.VMEM((2, LONG_WINDOW, LONG_SPAN), BF16),
            pltpu.VMEM((2, LONG_WINDOW, LONG_SPAN), BF16),
            pltpu.VMEM((128, LONG_SPAN), F32),
        ],
        compiler_params=pltpu.CompilerParams(vmem_limit_bytes=vmem_bytes(experts, 28)),
        name="backward_local",
    )(lengths, patches, main, *saved, result, gslots)


def reduce_kernel(experts, gw_ref, square_ref, attn_out, phi_out, norm_out, total_ref, own, pair_in,
                  box_one, in_one, box_two, in_two, box_z, in_z, final, scalars, load_sem, pair_send,
                  pair_recv, send_one, recv_one, send_two, recv_two, send_z, recv_z, swap_sem,
                  norm_send, norm_recv):
    core, chip, first, second = ring(experts)
    rows = attn_out.shape[0]
    layers = experts // 4
    layer = chip // 4
    column = lax.rem(chip, 4)
    barrier = pltpu.get_barrier_semaphore()

    @pl.loop(1, experts)
    def _(j):
        peer = lax.rem(chip + j, experts)
        pl.semaphore_signal(barrier, inc=1, device_id=(core, peer), device_id_type=MESH)

    pl.semaphore_signal(barrier, inc=1, device_id=(1 - core, chip), device_id_type=MESH)
    load = pltpu.make_async_copy(gw_ref.at[core], own, load_sem.at[0])
    load.start()
    pl.semaphore_wait(barrier, experts)

    def pair_copy(block):
        return pltpu.make_async_remote_copy(
            src_ref=gw_ref.at[1 - core, block],
            dst_ref=pair_in.at[block],
            send_sem=pair_send.at[block],
            recv_sem=pair_recv.at[block],
            device_id=(1 - core, chip),
            device_id_type=MESH,
        )

    def copy(source, target, sends, arrivals, index, device):
        return pltpu.make_async_remote_copy(
            src_ref=source.at[index],
            dst_ref=target.at[index],
            send_sem=sends.at[index],
            recv_sem=arrivals.at[index],
            device_id=device,
            device_id_type=MESH,
        )

    def to_first(index):
        return copy(box_one, in_one, send_one, recv_one, index, (core, first))

    def to_second(index):
        return copy(box_two, in_two, send_two, recv_two, index, (core, second))

    def layer_at(d):
        return lax.rem(layer + 1 + d, layers)

    far = 3 - column

    def block_at(d, place):
        return layer_at(d) * 4 + place

    both, one, two = far, lax.rem(first, 4), lax.rem(second, 4)

    for place in (both, two, one, column):

        @pl.loop(0, layers)
        def _(d):
            pair_copy(block_at(d, place)).start()

    load.wait()

    def summed(block):
        pair_copy(block).wait_recv()
        return own[block] + pair_in[block]

    for batch, place in ((0, both), (1, one)):

        @pl.loop(0, layers)
        def _(d):
            index = batch * layers + layer_at(d)
            box_one[index] = summed(block_at(d, place)).astype(BF16)
            to_first(index).start()

    @pl.loop(0, layers)
    def _(d):
        index = layer_at(d)
        total = summed(block_at(d, two))
        to_first(index).wait_recv()
        box_two[index] = (total + in_one[index].astype(F32)).astype(BF16)
        to_second(index).start()

    def to_layer(index):
        return pltpu.make_async_remote_copy(
            src_ref=box_z.at[index],
            dst_ref=in_z.at[layer],
            send_sem=send_z.at[index],
            recv_sem=recv_z.at[layer],
            device_id=(core, index * 4 + column),
            device_id_type=MESH,
        )

    def column_sum(index):
        total = summed(index * 4 + column)
        to_first(layers + index).wait_recv()
        total = total + in_one[layers + index].astype(F32)
        to_second(index).wait_recv()
        return total + in_two[index].astype(F32)

    @pl.loop(0, layers - 1)
    def _(d):
        index = layer_at(d)
        box_z[index] = column_sum(index).astype(BF16)
        to_layer(index).start()

    final[core] = column_sum(layer)

    @pl.loop(1, layers)
    def _(d):
        index = lax.rem(layer - d + layers, layers)
        pltpu.make_async_remote_copy(
            src_ref=box_z.at[index],
            dst_ref=in_z.at[index],
            send_sem=send_z.at[index],
            recv_sem=recv_z.at[index],
            device_id=(core, index * 4 + column),
            device_id_type=MESH,
        ).wait_recv()
        final[core] += in_z[index].astype(F32)

    def swap(side):
        return pltpu.make_async_remote_copy(
            src_ref=final.at[side],
            dst_ref=final.at[side],
            send_sem=swap_sem.at[0],
            recv_sem=swap_sem.at[1],
            device_id=(1 - core, chip),
            device_id_type=MESH,
        )

    mine = final[core]
    swap(core).start()

    scalars[experts + core] = square_ref[...] + jnp.sum(mine * mine)

    def norm_pair(side):
        return pltpu.make_async_remote_copy(
            src_ref=scalars.at[experts + side],
            dst_ref=scalars.at[experts + side],
            send_sem=swap_sem.at[2],
            recv_sem=swap_sem.at[3],
            device_id=(1 - core, chip),
            device_id_type=MESH,
        )

    norm_pair(core).start()
    norm_pair(1 - core).wait_recv()
    scalars[chip] = scalars[experts] + scalars[experts + 1]

    def norm_copy(j, block, peer):
        return pltpu.make_async_remote_copy(
            src_ref=scalars.at[block],
            dst_ref=scalars.at[block],
            send_sem=norm_send.at[j],
            recv_sem=norm_recv.at[j],
            device_id=(core, peer),
            device_id_type=MESH,
        )

    @pl.loop(1, experts)
    def _(j):
        norm_copy(j, chip, lax.rem(chip + j, experts)).start()

    swap(1 - core).wait_recv()
    for side in range(2):
        for part in range(2):
            for g in range(3):
                lanes = (side * 2 + part) * D + g * 128
                place = (2 * g + part) * rows
                attn_out[:, lanes : lanes + 128] = final[side, place : place + rows, :]
    phi_out[...] = final[0, 6 * rows : 6 * rows + experts, 0:rows]
    norm_out[...] = final[1, 6 * rows : 6 * rows + 4, 0:rows]

    @pl.loop(1, experts)
    def _(j):
        source = lax.rem(chip - j + experts, experts)
        norm_copy(j, source, source).wait_recv()

    total_ref[...] = jnp.sqrt(jnp.sum(scalars[0:experts], axis=0))
    swap(core).wait_send()
    norm_pair(core).wait_send()

    @pl.loop(0, experts)
    def _(block):
        pair_copy(block).wait_send()

    @pl.loop(0, 2 * layers)
    def _(index):
        to_first(index).wait_send()

    @pl.loop(0, layers)
    def _(index):
        to_second(index).wait_send()

    @pl.loop(1, layers)
    def _(d):
        to_layer(lax.rem(layer + d, layers)).wait_send()

    @pl.loop(1, experts)
    def _(j):
        norm_copy(j, chip, lax.rem(chip + j, experts)).wait_send()


def reduce_grads(grads, squares, experts):
    rows = D // experts
    layers = experts // 4
    block = grads.shape[2:]
    shape = jax.ShapeDtypeStruct
    dma = pltpu.SemaphoreType.DMA
    return pl.pallas_call(
        functools.partial(reduce_kernel, experts),
        out_shape=(
            shape((rows, 4 * D), F32),
            shape((experts, rows), F32),
            shape((4, rows), F32),
            shape((1, 128), F32),
        ),
        in_specs=[pl.BlockSpec(memory_space=pl.ANY)] + whole(1),
        out_specs=tuple(whole(4)),
        scratch_shapes=[
            pltpu.VMEM((experts,) + block, F32),
            pltpu.VMEM((experts,) + block, F32),
            pltpu.VMEM((2 * layers,) + block, BF16),
            pltpu.VMEM((2 * layers,) + block, BF16),
            pltpu.VMEM((layers,) + block, BF16),
            pltpu.VMEM((layers,) + block, BF16),
            pltpu.VMEM((layers,) + block, BF16),
            pltpu.VMEM((layers,) + block, BF16),
            pltpu.VMEM((2,) + block, F32),
            pltpu.VMEM((experts + 2, 1, 128), F32),
            dma((1,)),
            dma((experts,)),
            dma((experts,)),
            dma((2 * layers,)),
            dma((2 * layers,)),
            dma((layers,)),
            dma((layers,)),
            dma((layers,)),
            dma((layers,)),
            dma((4,)),
            dma((experts,)),
            dma((experts,)),
        ],
        compiler_params=pltpu.CompilerParams(
            collective_id=2, has_side_effects=True, vmem_limit_bytes=vmem_bytes(experts, 8)
        ),
        name="reduce_grads",
    )(grads, squares)


def adam_update(weight, first_moment, second_moment, gradient, factor, learning_rate, decay_rate):
    clipped = gradient * factor
    first_new = BETA_FIRST * first_moment + (1.0 - BETA_FIRST) * clipped
    second_new = BETA_SECOND * second_moment + (1.0 - BETA_SECOND) * clipped * clipped
    first_hat = first_new / (1.0 - BETA_FIRST**STEP)
    second_hat = second_new / (1.0 - BETA_SECOND**STEP)
    weight_new = weight - learning_rate * (
        first_hat / (jnp.sqrt(second_hat) + ADAM_EPS) + decay_rate * weight
    )
    return (weight_new, first_new, second_new)


RATES = (
    (1.0 / math.sqrt(D), WEIGHT_DECAY),
    (0.25 / math.sqrt(D), WEIGHT_DECAY),
    (0.8, 0.0),
    (4.0 / math.sqrt(D), WEIGHT_DECAY),
    (8.0 / math.sqrt(FF), WEIGHT_DECAY),
)
UPDATE_STEPS = 4


def update_kernel(norm_ref, *refs):
    grad_norm = norm_ref[...]
    factor = CLIP_NORM / jnp.maximum(grad_norm, CLIP_NORM)
    factor = factor[0:1, 0:1]
    inputs, outputs = refs[:20], refs[20:]
    for k, (rate, decay) in enumerate(RATES):
        weight, first, second, grad = (ref[...] for ref in inputs[4 * k : 4 * k + 4])
        by = factor.reshape((1,) * grad.ndim)
        news = adam_update(weight, first, second, grad, by, rate, decay)
        for ref, new in zip(outputs[3 * k : 3 * k + 3], news):
            ref[...] = new


def update(norm_tile, groups):
    def spec(k, shape):
        if k == 0:
            return pl.BlockSpec((shape[0], shape[1] // UPDATE_STEPS), lambda i: (0, i))
        if k < 3:
            return pl.BlockSpec(shape, lambda i: (0, 0))
        return pl.BlockSpec((1, shape[1] // UPDATE_STEPS, shape[2]), lambda i: (0, i, 0))

    specs = [spec(k, group[0].shape) for k, group in enumerate(groups)]
    return pl.pallas_call(
        update_kernel,
        grid=(UPDATE_STEPS,),
        out_shape=tuple(
            jax.ShapeDtypeStruct(group[0].shape, F32) for group in groups for _ in range(3)
        ),
        in_specs=[pl.BlockSpec((1, 128), lambda i: (0, 0))]
        + [one for one in specs for _ in range(4)],
        out_specs=tuple(one for one in specs for _ in range(3)),
        compiler_params=pltpu.CompilerParams(vmem_limit_bytes=24 * 1024 * 1024),
        name="update",
    )(norm_tile, *[array for group in groups for array in group])


def in_hbm(array):
    return pltpu.with_memory_space_constraint(array, pltpu.HBM)


def pad_to(array, shape):
    return jnp.pad(array, [(0, full - size) for size, full in zip(array.shape, shape)])


def regroup_weights(blocks, experts):
    rows = D // experts
    if rows == GROUP_ROWS:
        return blocks
    main = blocks[:, :, : 6 * rows].reshape(experts, 2, 3, 2, rows, 128).transpose(1, 2, 3, 0, 4, 5)
    main = main.reshape(2, 3, 2, GROUPS, GROUP_ROWS, 128).transpose(3, 0, 1, 2, 4, 5)
    main = main.reshape(GROUPS, 2, 6 * GROUP_ROWS, 128)
    small_rows = max(experts, 16)
    small = blocks[:, :, 6 * rows :, :rows]
    small = pad_to(small[:, :, :small_rows], (experts, 2, small_rows, rows))
    small = small.transpose(1, 2, 0, 3).reshape(2, small_rows, GROUPS, GROUP_ROWS)
    small = pad_to(small.transpose(2, 0, 1, 3), (GROUPS, 2, small_rows, 128))
    return jnp.concatenate([main, small], axis=2)


def regroup_grads(groups, experts):
    rows = D // experts
    if rows == GROUP_ROWS:
        return groups
    main = groups[:, :, : 6 * GROUP_ROWS].reshape(2, GROUPS, 3, 2, GROUP_ROWS, 128)
    main = main.transpose(0, 2, 3, 1, 4, 5).reshape(2, 3, 2, experts, rows, 128)
    main = main.transpose(0, 3, 1, 2, 4, 5).reshape(2, experts, 6 * rows, 128)
    small = groups[:, :, 6 * GROUP_ROWS :, :GROUP_ROWS]
    small_rows = min(small.shape[2], block_rows(experts) - 6 * rows)
    small = small[:, :, :small_rows].transpose(0, 2, 1, 3).reshape(2, small_rows, experts, rows)
    small = pad_to(small.transpose(0, 2, 1, 3), (2, experts, small_rows, 128))
    both = jnp.concatenate([main, small], axis=2)
    return pad_to(both, (2, experts, block_rows(experts), 128))


def local(
    patches,
    slot_len,
    attn_weight,
    attn_first,
    attn_second,
    phi_weight,
    phi_first,
    phi_second,
    norm_params,
    norm_first,
    norm_second,
    expert_in,
    in_first,
    in_second,
    expert_out,
    out_first,
    out_second,
    cotangent,
):
    experts = lax.axis_size("expert")
    weights = gather_weights(
        in_hbm(attn_weight), in_hbm(phi_weight.T), in_hbm(norm_params), experts
    )
    weights = regroup_weights(weights, experts)
    *saved, packed = forward_local(
        slot_len, patches, weights, in_hbm(cotangent), experts
    )
    result, gslots, grad_in, grad_out, squares = run_experts(packed, expert_in, expert_out, experts)
    block_output, input_grad, grads = backward_local(
        slot_len, patches, weights, saved, result, gslots, experts
    )
    grads = regroup_grads(grads, experts)
    attn_part, phi_part, norm_part, norm_tile = reduce_grads(grads, squares, experts)
    news = update(
        norm_tile,
        (
            (attn_weight, attn_first, attn_second, attn_part),
            (phi_weight.T, phi_first.T, phi_second.T, phi_part),
            (norm_params, norm_first, norm_second, norm_part),
            (expert_in, in_first, in_second, grad_in),
            (expert_out, out_first, out_second, grad_out),
        ),
    )
    attn_new, attn_first_new, attn_second_new = news[0:3]
    phi_new, phi_first_new, phi_second_new = (new.T for new in news[3:6])
    norm_new, norm_first_new, norm_second_new = news[6:9]
    in_new, in_first_new, in_second_new = news[9:12]
    out_new, out_first_new, out_second_new = news[12:15]
    grad_norm = norm_tile[0, 0]
    return (
        block_output,
        input_grad,
        grad_norm,
        attn_new,
        attn_first_new,
        attn_second_new,
        phi_new,
        phi_first_new,
        phi_second_new,
        norm_new,
        norm_first_new,
        norm_second_new,
        in_new,
        in_first_new,
        in_second_new,
        out_new,
        out_first_new,
        out_second_new,
    )


def solution(mesh):
    in_specs = (
        P(("batch", "expert"), None),
        P(("batch", "expert"), None),
        P("expert", None),
        P("expert", None),
        P("expert", None),
        P("expert", None),
        P("expert", None),
        P("expert", None),
        P(None, "expert"),
        P(None, "expert"),
        P(None, "expert"),
        P("expert", None, "batch"),
        P("expert", None, "batch"),
        P("expert", None, "batch"),
        P("expert", "batch", None),
        P("expert", "batch", None),
        P("expert", "batch", None),
        P(("batch", "expert"), None),
    )
    out_specs = (
        P(("batch", "expert"), None),
        P(("batch", "expert"), None),
        P(),
        P("expert", None),
        P("expert", None),
        P("expert", None),
        P("expert", None),
        P("expert", None),
        P("expert", None),
        P(None, "expert"),
        P(None, "expert"),
        P(None, "expert"),
        P("expert", None, "batch"),
        P("expert", None, "batch"),
        P("expert", None, "batch"),
        P("expert", "batch", None),
        P("expert", "batch", None),
        P("expert", "batch", None),
    )
    return jax.shard_map(local, mesh=mesh, in_specs=in_specs, out_specs=out_specs, check_vma=False)
```

```python
import functools
import math

import jax
import jax.numpy as jnp
from jax import lax
from jax.experimental import pallas as pl
from jax.experimental.pallas import tpu as pltpu
from jax.sharding import PartitionSpec as P

D = 384
HEADS = 6
HEAD_DIM = 64
FF = 1536
STEP = 3
SHORT_LEN = 196
LONG_LEN = 576
IMAGES = 5
SLOT_ROWS = 8
PAIRS = 3
GROUPS = 16
GROUP_ROWS = D // GROUPS
CHUNK = 112
LONG_WINDOW = 592
LONG_SPAN = 640
WINDOW_PAD = 48

NORM_EPS = 1e-06
CLIP_NORM = 1.0
BETA_FIRST = 0.5
BETA_SECOND = 0.5
ADAM_EPS = 1e-08
WEIGHT_DECAY = 0.05
MASKED = -1e30
SCORE_SCALE = HEAD_DIM ** (-0.5)

MESH = pl.DeviceIdType.MESH
F32 = jnp.float32
BF16 = jnp.bfloat16


def vmem_bytes(experts, mebibytes):
    return (mebibytes if experts <= 16 else 60) * 1024 * 1024


def whole(count):
    return [pl.BlockSpec(memory_space=pltpu.VMEM)] * count


def round_up(value, unit):
    return -(-value // unit) * unit


def mm(left, right):
    return jnp.dot(left, right, preferred_element_type=F32)


def mm_nt(left, right):
    return lax.dot_general(left, right, (((1,), (1,)), ((), ())), preferred_element_type=F32)


def mm_tn(left, right):
    return lax.dot_general(left, right, (((0,), (0,)), ((), ())), preferred_element_type=F32)


def block_rows(experts):
    rows = D // experts
    return round_up(6 * rows + max(experts, 4), 16)


def ring(experts):
    core = lax.axis_index("batch")
    chip = lax.axis_index("expert")
    first = chip ^ (1 + core)
    second = chip ^ (2 - core)
    return core, chip, first, second


def gather_kernel(experts, attn_hbm, phi_hbm, norm_hbm, out, stage, attn_ref, phi_ref, norm_ref, load_sem,
                  sent, recv):
    core, chip, first, second = ring(experts)
    rows = attn_ref.shape[0]
    half = pl.multiple_of(core * (2 * D), 128)
    loads = [
        pltpu.make_async_copy(attn_hbm.at[:, pl.ds(half, 2 * D)], attn_ref, load_sem.at[0]),
        pltpu.make_async_copy(phi_hbm, phi_ref, load_sem.at[1]),
        pltpu.make_async_copy(norm_hbm, norm_ref, load_sem.at[2]),
    ]
    for load in loads:
        load.start()
    column = lax.rem(chip, 4)
    layers = experts // 4
    layer = chip // 4
    barrier = pltpu.get_barrier_semaphore()

    @pl.loop(1, layers)
    def _(d):
        peer = lax.rem(layer + d, layers) * 4 + column
        pl.semaphore_signal(barrier, inc=1, device_id=(core, peer), device_id_type=MESH)

    pl.semaphore_signal(barrier, inc=1, device_id=(core, first), device_id_type=MESH)
    pl.semaphore_signal(barrier, inc=1, device_id=(core, second), device_id_type=MESH)
    pl.semaphore_signal(barrier, inc=1, device_id=(1 - core, chip), device_id_type=MESH)
    stage[...] = jnp.zeros_like(stage)
    for load in loads:
        load.wait()
    for part in range(2):
        for g in range(3):
            lanes = part * D + g * 128
            place = (2 * g + part) * rows
            stage[place : place + rows, :] = attn_ref[:, lanes : lanes + 128]

    @pl.when(core == 0)
    def _():
        stage[6 * rows : 6 * rows + experts, 0:rows] = phi_ref[...]

    @pl.when(core == 1)
    def _():
        stage[6 * rows : 6 * rows + 4, 0:rows] = norm_ref[...]

    out[chip, core] = stage[...].astype(BF16)
    pl.semaphore_wait(barrier, layers + 2)

    def copy(source, target, send_sem, recv_sem, device):
        return pltpu.make_async_remote_copy(
            src_ref=source,
            dst_ref=target,
            send_sem=send_sem,
            recv_sem=recv_sem,
            device_id=device,
            device_id_type=MESH,
        )

    def along(block, peer):
        mine = out.at[block, core]
        return copy(mine, mine, sent.at[0], recv.at[block], (core, peer))

    def to_pair(block):
        mine = out.at[block, core]
        return copy(mine, mine, sent.at[1], sent.at[2], (1 - core, chip))

    @pl.loop(1, layers)
    def _(d):
        along(chip, lax.rem(layer + d, layers) * 4 + column).start()

    along(chip, first).start()
    along(chip, second).start()
    to_pair(chip).start()

    @pl.loop(1, layers)
    def _(d):
        block = lax.rem(layer - d + layers, layers) * 4 + column
        along(block, first).wait_recv()
        along(block, first).start()
        along(block, second).start()
        to_pair(block).start()

    @pl.loop(0, layers)
    def _(d):
        block = lax.rem(layer - d + layers, layers) * 4 + lax.rem(first, 4)
        along(block, first).wait_recv()
        along(block, second).start()
        to_pair(block).start()

    @pl.loop(0, 2 * layers)
    def _(d):
        other = jnp.where(lax.rem(d, 2) == 0, lax.rem(second, 4), lax.rem(3 - column, 4))
        block = lax.rem(layer - d // 2 + layers, layers) * 4 + other
        along(block, first).wait_recv()
        to_pair(block).start()

    sides = out.at[pl.ds(0, experts - 1), core]
    copy(sides, sides, sent.at[0], sent.at[0], (1 - core, chip)).wait_send()
    copy(out.at[:, core], out.at[:, 1 - core], sent.at[1], sent.at[2], (1 - core, chip)).wait()


def gather_weights(attn_weight, phi_turned, norm_params, experts):
    rows = block_rows(experts)
    dma = pltpu.SemaphoreType.DMA
    return pl.pallas_call(
        functools.partial(gather_kernel, experts),
        out_shape=jax.ShapeDtypeStruct((experts, 2, rows, 128), BF16),
        in_specs=[pl.BlockSpec(memory_space=pltpu.HBM)] * 3,
        out_specs=whole(1)[0],
        scratch_shapes=[
            pltpu.VMEM((rows, 128), F32),
            pltpu.VMEM((attn_weight.shape[0], 2 * D), F32),
            pltpu.VMEM(phi_turned.shape, F32),
            pltpu.VMEM(norm_params.shape, F32),
            dma((3,)),
            dma((3,)),
            dma((experts,)),
        ],
        compiler_params=pltpu.CompilerParams(
            collective_id=0, has_side_effects=True, vmem_limit_bytes=vmem_bytes(experts, 3)
        ),
        name="gather_weights",
    )(attn_weight, phi_turned, norm_params)


def unpack_weight(main_ref, side, part):
    blocks = main_ref[:, side].astype(F32)
    columns = []
    for g in range(3):
        place = (2 * g + part) * GROUP_ROWS
        columns.append(blocks[:, place : place + GROUP_ROWS, :].reshape(D, 128))
    return jnp.concatenate(columns, axis=1).astype(BF16)


def group_lanes():
    lane = lax.broadcasted_iota(jnp.int32, (128, D), 0)
    column = lax.broadcasted_iota(jnp.int32, (128, D), 1)
    return jnp.where(column % GROUP_ROWS == lane, 1.0, 0.0).astype(BF16)


def unpack_turned(main_ref, side, rows):
    first = 6 * GROUP_ROWS
    blocks = main_ref[:, side].astype(F32)[:, first : first + rows, :]
    spread = mm(blocks.reshape(GROUPS * rows, 128).astype(BF16), group_lanes())
    spread = spread.reshape(GROUPS, rows, D)
    group = lax.broadcasted_iota(jnp.int32, (GROUPS, 1, D), 0)
    column = lax.broadcasted_iota(jnp.int32, (GROUPS, 1, D), 2)
    return jnp.sum(jnp.where(column // GROUP_ROWS == group, spread, 0.0), axis=0)


def pack_turned(values):
    rows = values.shape[0]
    group = lax.broadcasted_iota(jnp.int32, (GROUPS, 1, D), 0)
    column = lax.broadcasted_iota(jnp.int32, (GROUPS, 1, D), 2)
    spread = jnp.where(column // GROUP_ROWS == group, values[None], 0.0)
    spread = spread.reshape(GROUPS * rows, D).astype(BF16)
    return mm_nt(spread, group_lanes()).reshape(GROUPS, rows, 128)


def unpack_small(main_ref, experts):
    turned = unpack_turned(main_ref, 0, max(experts, 16)).astype(BF16)
    row = lax.broadcasted_iota(jnp.int32, (experts * SLOT_ROWS, turned.shape[0]), 0)
    column = lax.broadcasted_iota(jnp.int32, (experts * SLOT_ROWS, turned.shape[0]), 1)
    spread = jnp.where(column == row // SLOT_ROWS, 1.0, 0.0).astype(BF16)
    return mm(spread, turned).astype(BF16), unpack_turned(main_ref, 1, 8)


def slot_bounds(len_ref, columns):
    image = lax.broadcasted_iota(jnp.int32, (1, columns), 1) % SLOT_ROWS
    starts = jnp.zeros((1, columns), jnp.int32)
    ends = jnp.zeros((1, columns), jnp.int32)
    start = jnp.int32(0)
    for k in range(IMAGES):
        end = start + len_ref[0, k]
        starts = jnp.where(image == k, start, starts)
        ends = jnp.where(image == k, end, ends)
        start = end
    return starts, ends, start


def normed(values):
    centred = values - jnp.mean(values, axis=-1, keepdims=True)
    variance = jnp.mean(centred * centred, axis=-1, keepdims=True)
    inverse = lax.rsqrt(variance + NORM_EPS)
    return centred * inverse, inverse


def norm_back(grad_shaped, normal, inverse, scaling):
    grad_normal = grad_shaped * scaling
    return inverse * (
        grad_normal
        - jnp.mean(grad_normal, axis=-1, keepdims=True)
        - normal * jnp.mean(grad_normal * normal, axis=-1, keepdims=True)
    )


def over_rows(start, stop, carry, body):
    for at in range(start, stop, CHUNK):
        carry = body(at, min(CHUNK, stop - at), carry)
    return carry


def fold_rows(values):
    return jnp.sum(values.reshape(values.shape[0] // 8, 8, values.shape[1]), axis=0)


def over_images(len_ref, tokens, body):
    def step(k, start):
        length = len_ref[0, k]
        for full in (SHORT_LEN, LONG_LEN):

            @pl.when(length == full)
            def _():
                window = round_up(full + 12, 16)
                first = jnp.minimum((start // 16) * 16, tokens - window)
                body(pl.multiple_of(first, 16), start - first, full, window)

        return start + length

    lax.fori_loop(0, IMAGES, step, jnp.int32(0))


def rows_inside(shift, full, first, count):
    row = first + lax.broadcasted_iota(jnp.int32, (count, 1), 0)
    return (row >= shift) & (row < shift + full)


def columns_inside(shift, full, count):
    column = lax.broadcasted_iota(jnp.int32, (1, count), 1)
    return (column >= shift) & (column < shift + full)


def forward_kernel(experts, len_ref, patch_ref, main_ref, cot_hbm, qkv_ref, o_ref, lse_ref, x1_ref,
                   h2_ref, disp_ref, comb_ref, gy_ref, pack_ref, logit, packf, scores,
                   probs, peaks, cot_ref, h1_all, load_sem):
    load = pltpu.make_async_copy(cot_hbm, cot_ref, load_sem.at[0])
    load.start()
    tokens = patch_ref.shape[0]
    columns = experts * SLOT_ROWS
    tile = tokens // 5
    phi, norms = unpack_small(main_ref, experts)
    starts, ends, total = slot_bounds(len_ref, columns)
    w_q, w_k = unpack_weight(main_ref, 0, 0), unpack_weight(main_ref, 0, 1)
    w_v = unpack_weight(main_ref, 1, 0)
    w_qkv = jnp.concatenate([w_q, w_k, w_v], axis=1)

    def first_norm(at, count, carry):
        rows = pl.ds(at, count)
        normal, _ = normed(patch_ref[rows, :].astype(F32))
        h1_all[rows, :] = (normal * norms[0:1] + norms[1:2]).astype(BF16)
        return carry

    over_rows(0, tokens, 0, first_norm)
    for t in range(5):
        rows = pl.ds(t * tile, tile)
        qkv = mm(h1_all[rows, :], w_qkv).astype(BF16)
        for c in range(9):
            qkv_ref[c, rows, :] = qkv[:, c * 128 : (c + 1) * 128]
    qkv_ref[:, tokens:, :] = jnp.zeros((9, WINDOW_PAD, 128), BF16)
    o_ref[...] = jnp.zeros_like(o_ref)
    lse_ref[...] = jnp.zeros_like(lse_ref)
    low_lane = lax.broadcasted_iota(jnp.int32, (1, 128), 1) < HEAD_DIM
    lane = lax.broadcasted_iota(jnp.int32, (1, 128), 1)

    def attend(first, shift, full, window):
        span = round_up(window, 128)
        bias = jnp.where(columns_inside(shift, full, span), 0.0, MASKED)
        inside = rows_inside(shift, full, 0, window)
        rows = pl.ds(first, window)
        wide = pl.ds(first, span)

        ones = jnp.ones((span, 128), BF16)

        def score(n):
            p, h = divmod(n, 2)
            mine = low_lane if h == 0 else jnp.logical_not(low_lane)
            query = jnp.where(mine, qkv_ref[p, rows, :].astype(F32) * SCORE_SCALE, 0.0)
            keys = qkv_ref[PAIRS + p, wide, :]
            scores[h, :window, :span] = mm_nt(query.astype(BF16), keys)

        score(0)
        outs = []
        for n in range(HEADS):
            p, h = divmod(n, 2)
            if n + 1 < HEADS:
                score(n + 1)
            for r in range(0, window, 16):
                part = scores[h, r : r + 16, :span] + bias
                peak = jnp.max(part, axis=-1, keepdims=True)
                probs[h, r : r + 16, :span] = jnp.exp(part - peak).astype(BF16)
                peaks[h, r : r + 16, :] = jnp.broadcast_to(peak, (16, 128))
            values = jnp.concatenate([qkv_ref[2 * PAIRS + p, wide, :], ones], axis=1)
            both = mm(probs[h, :window, :span], values)
            summed = both[:, 128:]
            outs.append(both[:, :128] * (1.0 / summed))
            logs = peaks[h, :window, :] + jnp.log(summed)
            lse_ref[rows, :] = jnp.where(inside & (lane == n), logs, lse_ref[rows, :])
            if h == 1:
                lanes = slice(p * 128, (p + 1) * 128)
                old = o_ref[rows, lanes].astype(F32)
                merged = jnp.where(inside, jnp.where(low_lane, outs[n - 1], outs[n]), old)
                o_ref[rows, lanes] = merged.astype(BF16)

    over_images(len_ref, tokens, attend)

    load.wait()
    w_o = unpack_weight(main_ref, 1, 1)
    for t in range(5):
        rows = pl.ds(t * tile, tile)
        x1_ref[rows, :] = mm(o_ref[rows, :], w_o)

    def second_norm(at, count, carry):
        rows = pl.ds(at, count)
        x1 = patch_ref[rows, :].astype(F32) + x1_ref[rows, :]
        normal, _ = normed(x1)
        h2_ref[rows, :] = (normal * norms[2:3] + norms[3:4]).astype(BF16)
        valid = at + lax.broadcasted_iota(jnp.int32, (count, 1), 0) < total
        x1_ref[rows, :] = jnp.where(valid, x1, 0.0)
        gy_ref[rows, :] = jnp.where(valid, cot_ref[rows, :].astype(F32), 0.0).astype(BF16)
        return carry

    over_rows(0, tokens, 0, second_norm)
    logit[...] = mm_nt(h2_ref[...], phi)

    def members(at, count):
        position = at + lax.broadcasted_iota(jnp.int32, (count, columns), 0)
        return (position >= starts) & (position < ends)

    def mixing(at, count, peak):
        rows = pl.ds(at, count)
        logits = logit[rows, :]
        member = members(at, count)
        exponent = jnp.exp(logits - jnp.max(logits, axis=-1, keepdims=True))
        summed = jnp.sum(exponent, axis=-1, keepdims=True) * (1.0 / SLOT_ROWS)
        comb_ref[rows, :] = jnp.where(member, exponent * (1.0 / summed), 0.0)
        inside = jnp.where(member, logits, MASKED)
        return jnp.maximum(peak, jnp.max(inside.reshape(count // 8, 8, columns), axis=0))

    peak = over_rows(0, tokens, jnp.full((8, columns), MASKED, F32), mixing)
    present = ends > starts
    peak = jnp.where(present, jnp.max(peak, axis=0, keepdims=True), 0.0)

    def exponents(at, count, summed):
        rows = pl.ds(at, count)
        member = members(at, count)
        exponent = jnp.exp(jnp.where(member, logit[rows, :] - peak, 0.0))
        exponent = jnp.where(member, exponent, 0.0)
        disp_ref[rows, :] = exponent
        return summed + fold_rows(exponent)

    summed = over_rows(0, tokens, jnp.zeros((8, columns), F32), exponents)
    summed = jnp.sum(summed, axis=0, keepdims=True) + jnp.where(present, 0.0, 1.0)
    dispatch = disp_ref[...] * (1.0 / summed)
    disp_ref[...] = dispatch
    slots = mm_tn(dispatch.astype(BF16), h2_ref[...])
    grad_result = mm_tn(comb_ref[...].astype(BF16), gy_ref[...])
    for part, matrix in enumerate((slots, grad_result)):
        pack_rows(packf, matrix.reshape(experts, SLOT_ROWS, D))
        pack_ref[:, part * 16 : (part + 1) * 16, :] = packf[...].astype(BF16)


def pack_rows(packf, blocks):
    packf[...] = jnp.zeros_like(packf)
    for c in range(3):
        packf[:, c * IMAGES : (c + 1) * IMAGES, :] = blocks[:, :IMAGES, c * 128 : (c + 1) * 128]


def unpack_rows(packf, wide):
    wide[...] = jnp.zeros_like(wide)
    for c in range(3):
        wide[:, 0:IMAGES, c * 128 : (c + 1) * 128] = packf[:, c * IMAGES : (c + 1) * IMAGES, :]


def forward_local(lengths, patches, main, cotangent, experts):
    tokens = patches.shape[0]
    columns = experts * SLOT_ROWS
    shape = jax.ShapeDtypeStruct
    return pl.pallas_call(
        functools.partial(forward_kernel, experts),
        out_shape=(
            shape((9, tokens + WINDOW_PAD, 128), BF16),
            shape((tokens + WINDOW_PAD, D), BF16),
            shape((tokens + WINDOW_PAD, 128), F32),
            shape((tokens, D), F32),
            shape((tokens, D), BF16),
            shape((tokens, columns), F32),
            shape((tokens, columns), F32),
            shape((tokens, D), BF16),
            shape((experts, 32, 128), BF16),
        ),
        in_specs=[pl.BlockSpec(memory_space=pltpu.SMEM)]
        + whole(2)
        + [pl.BlockSpec(memory_space=pltpu.HBM)],
        out_specs=tuple(whole(9)),
        scratch_shapes=[
            pltpu.VMEM((tokens, columns), F32),
            pltpu.VMEM((experts, 16, 128), F32),
            pltpu.VMEM((2, LONG_WINDOW, LONG_SPAN), F32),
            pltpu.VMEM((2, LONG_WINDOW, LONG_SPAN), BF16),
            pltpu.VMEM((2, LONG_WINDOW, 128), F32),
            pltpu.VMEM((tokens, D), BF16),
            pltpu.VMEM((tokens, D), BF16),
            pltpu.SemaphoreType.DMA((1,)),
        ],
        compiler_params=pltpu.CompilerParams(vmem_limit_bytes=vmem_bytes(experts, 24)),
        name="forward_local",
    )(lengths, patches, main, cotangent)


def expert_kernel(experts, pack_ref, in_ref, out_ref, result_ref, gslot_ref, gin_ref, gout_ref,
                  square_ref, inbox, partial, given, outbox, back, packf, wide, packe, widee,
                  sems):
    core = lax.axis_index("batch")
    chip = lax.axis_index("expert")
    barrier = pltpu.get_barrier_semaphore()

    @pl.loop(1, experts)
    def _(j):
        peer = lax.rem(chip + j, experts)
        pl.semaphore_signal(barrier, inc=1, device_id=(core, peer), device_id_type=MESH)

    pl.semaphore_signal(barrier, inc=1, device_id=(1 - core, chip), device_id_type=MESH)
    w_in = in_ref[0].astype(BF16)
    w_out = out_ref[0].astype(BF16)
    inbox[core, chip] = pack_ref[chip]
    pl.semaphore_wait(barrier, experts)

    def copy(source, target, sem, device):
        return pltpu.make_async_remote_copy(
            src_ref=source,
            dst_ref=target,
            send_sem=sems.at[sem],
            recv_sem=sems.at[sem + 1],
            device_id=device,
            device_id_type=MESH,
        )

    @pl.loop(1, experts)
    def _(j):
        peer = lax.rem(chip + j, experts)
        copy(pack_ref.at[peer], inbox.at[core, chip], 0, (core, peer)).start()

    others = pl.ds(0, experts - 1)
    first = copy(pack_ref.at[others], inbox.at[core, others], 0, (core, chip))
    first.wait_recv()
    pair = copy(inbox.at[core], inbox.at[core], 2, (1 - core, chip))
    pair.start()
    pair.wait_recv()

    def spread(side, part):
        packe[...] = inbox[side, :, part * 16 : (part + 1) * 16, :].astype(F32)
        unpack_rows(packe, widee)
        return widee[...].reshape(experts * SLOT_ROWS, D).astype(BF16)

    def run(side):
        slots = spread(side, 0)
        grads = spread(side, 1)
        hidden = mm(slots, w_in)
        root = math.sqrt(2.0 / math.pi)
        bent = jnp.tanh(root * (hidden + 0.044715 * (hidden * hidden * hidden)))
        half = 0.5 * (1.0 + bent)
        act = (hidden * half).astype(BF16)
        slope = half + 0.5 * hidden * (1.0 - bent * bent) * (
            root * (1.0 + 3.0 * 0.044715 * (hidden * hidden))
        )
        result = mm(act, w_out)
        grad_hidden = (mm_nt(grads, w_out) * slope).astype(BF16)
        grad_slots = mm_nt(grad_hidden, w_in)
        return slots, grads, act, grad_hidden, result, grad_slots

    theirs = run(1 - core)
    for part in range(2):
        pack_rows(packf, theirs[4 + part].reshape(experts, SLOT_ROWS, D))
        partial[:, part * 16 : (part + 1) * 16, :] = packf[...].astype(BF16)
    halves = copy(partial, given, 4, (1 - core, chip))
    halves.start()
    ours = run(core)
    halves.wait_recv()
    for part in range(2):
        block = slice(part * 16, (part + 1) * 16)
        pack_rows(packf, ours[4 + part].reshape(experts, SLOT_ROWS, D))
        outbox[:, block, :] = (packf[...] + given[:, block, :].astype(F32)).astype(BF16)

    @pl.loop(1, experts)
    def _(j):
        peer = lax.rem(chip + j, experts)
        copy(outbox.at[peer], back.at[chip], 6, (core, peer)).start()

    back[chip] = outbox[chip]
    grad_out = mm_tn(ours[2], ours[1]) + mm_tn(theirs[2], theirs[1])
    gout_ref[0] = grad_out
    grad_in = mm_tn(ours[0], ours[3]) + mm_tn(theirs[0], theirs[3])
    gin_ref[0] = grad_in
    squares = jnp.zeros((1, 128), F32)
    for grad in (grad_out, grad_in):
        columns = jnp.sum(grad * grad, axis=0, keepdims=True)
        for c in range(0, grad.shape[1], 128):
            squares = squares + columns[:, c : c + 128]
    square_ref[...] = squares

    second = copy(outbox.at[others], back.at[others], 6, (core, chip))
    second.wait_recv()
    for part, target in enumerate((result_ref, gslot_ref)):
        packe[...] = back[:, part * 16 : (part + 1) * 16, :].astype(F32)
        unpack_rows(packe, widee)
        target[...] = widee[...].reshape(experts * SLOT_ROWS, D).astype(BF16)

    first.wait_send()
    pair.wait_send()
    halves.wait_send()
    second.wait_send()


def run_experts(packed, expert_in, expert_out, experts):
    shape = jax.ShapeDtypeStruct
    return pl.pallas_call(
        functools.partial(expert_kernel, experts),
        out_shape=(
            shape((experts * SLOT_ROWS, D), BF16),
            shape((experts * SLOT_ROWS, D), BF16),
            shape(expert_in.shape, F32),
            shape(expert_out.shape, F32),
            shape((1, 128), F32),
        ),
        in_specs=whole(3),
        out_specs=tuple(whole(5)),
        scratch_shapes=[
            pltpu.VMEM((2, experts, 32, 128), BF16),
            pltpu.VMEM((experts, 32, 128), BF16),
            pltpu.VMEM((experts, 32, 128), BF16),
            pltpu.VMEM((experts, 32, 128), BF16),
            pltpu.VMEM((experts, 32, 128), BF16),
            pltpu.VMEM((experts, 16, 128), F32),
            pltpu.VMEM((experts, SLOT_ROWS, D), F32),
            pltpu.VMEM((experts, 16, 128), F32),
            pltpu.VMEM((experts, SLOT_ROWS, D), F32),
        ]
        + [pltpu.SemaphoreType.DMA((8,))],
        compiler_params=pltpu.CompilerParams(
            collective_id=1, has_side_effects=True, vmem_limit_bytes=vmem_bytes(experts, 8)
        ),
        name="run_experts",
    )(packed, expert_in, expert_out)


def backward_kernel(experts, len_ref, patch_ref, main_ref, qkv_ref, o_ref, lse_ref,
                    x1_ref, h2_ref, disp_ref, comb_ref, gy_ref, result_ref, gslot_ref, block_ref,
                    input_ref, gw_ref, gdisp, glog, gx1, branch, go, gqkv,
                    h1_all, scores, grad_probs, probs, grad_scores, sums, gcomb,
                    wide_rows):
    tokens = patch_ref.shape[0]
    columns = experts * SLOT_ROWS
    tile = tokens // 5
    phi, norms = unpack_small(main_ref, experts)
    result = result_ref[...]
    gslots = gslot_ref[...]

    kept = gdisp.shape[0] == tokens

    def place(at):
        return at if kept else at % tile

    inner = jnp.zeros((8, columns), F32)
    for t in range(5):
        rows = pl.ds(t * tile, tile)
        gdisp[pl.ds(place(t * tile), tile), :] = mm_nt(h2_ref[rows, :], gslots)

        def dispatch_inner(at, count, inner):
            products = disp_ref[pl.ds(at, count), :] * gdisp[pl.ds(place(at), count), :]
            return inner + fold_rows(products)

        inner = over_rows(t * tile, (t + 1) * tile, inner, dispatch_inner)
    inner = jnp.sum(inner, axis=0, keepdims=True)
    for t in range(5):
        rows = pl.ds(t * tile, tile)
        here = pl.ds(place(t * tile), tile)
        gx1[rows, :] = mm(comb_ref[rows, :].astype(BF16), result)
        gcomb[here, :] = mm_nt(gy_ref[rows, :], result)
        if not kept:
            gdisp[here, :] = mm_nt(h2_ref[rows, :], gslots)

        def logit_grads(at, count, carry):
            rows, here = pl.ds(at, count), pl.ds(place(at), count)
            block_ref[rows, :] = (x1_ref[rows, :] + gx1[rows, :]).astype(BF16)
            combine = comb_ref[rows, :]
            weighted = combine * gcomb[here, :]
            glog[rows, :] = (
                weighted
                - combine * jnp.sum(weighted, axis=-1, keepdims=True)
                + disp_ref[rows, :] * (gdisp[here, :] - inner)
            ).astype(BF16)
            return carry

        over_rows(t * tile, (t + 1) * tile, 0, logit_grads)
    for t in range(5):
        rows = pl.ds(t * tile, tile)
        gx1[rows, :] = mm(disp_ref[rows, :].astype(BF16), gslots) + mm(glog[rows, :], phi)

    def second_norm(at, count, carry):
        gain, bias = carry
        rows = pl.ds(at, count)
        grad_h2 = gx1[rows, :]
        normal, inverse = normed(x1_ref[rows, :])
        grad_x1 = gy_ref[rows, :].astype(F32) + norm_back(grad_h2, normal, inverse, norms[2:3])
        gx1[rows, :] = grad_x1
        branch[rows, :] = grad_x1.astype(BF16)
        return gain + fold_rows(grad_h2 * normal), bias + fold_rows(grad_h2)

    zero = jnp.zeros((8, D), F32)
    gain_two, bias_two = over_rows(0, tokens, (zero, zero), second_norm)
    w_o = unpack_weight(main_ref, 1, 1)
    for t in range(5):
        rows = pl.ds(t * tile, tile)
        grad_o = mm_nt(branch[rows, :], w_o).astype(BF16)
        for c in range(PAIRS):
            go[c, rows, :] = grad_o[:, c * 128 : (c + 1) * 128]

    small_rows = gw_ref.shape[2] - 6 * GROUP_ROWS
    row = lax.broadcasted_iota(jnp.int32, (columns, small_rows), 0)
    column = lax.broadcasted_iota(jnp.int32, (columns, small_rows), 1)
    fold = jnp.where(column == row // SLOT_ROWS, 1.0, 0.0).astype(BF16)
    folded = mm(glog[...], fold).astype(BF16)
    gw_ref[0, :, 6 * GROUP_ROWS :, :] = pack_turned(mm_tn(folded, h2_ref[...]))

    def put(side, part, value):
        for g in range(3):
            place = (2 * g + part) * GROUP_ROWS
            gw_ref[side, :, place : place + GROUP_ROWS, :] = value[
                :, g * 128 : (g + 1) * 128
            ].reshape(GROUPS, GROUP_ROWS, 128)

    put(1, 1, mm_tn(o_ref[0:tokens, :], branch[...]))

    gqkv[...] = jnp.zeros_like(gqkv)
    go[:, tokens:, :] = jnp.zeros((PAIRS, WINDOW_PAD, 128), BF16)
    low_lane = lax.broadcasted_iota(jnp.int32, (1, 128), 1) < HEAD_DIM

    head_row = lax.broadcasted_iota(jnp.int32, (8, 128), 0)
    head_lane = lax.broadcasted_iota(jnp.int32, (8, 128), 1)
    heads = jnp.where(head_row == head_lane // HEAD_DIM, 1.0, 0.0).astype(BF16)

    def attend(first, shift, full, window):
        span = round_up(window, 128)
        inside = rows_inside(shift, full, 0, window)
        queries_inside = columns_inside(shift, full, span)
        rows = pl.ds(first, window)
        wide = pl.ds(first, span)
        sums[:, :span] = jnp.transpose(lse_ref[wide, :])

        def score(n):
            p, h = divmod(n, 2)
            mine = low_lane if h == 0 else jnp.logical_not(low_lane)
            keys = jnp.where(mine, qkv_ref[PAIRS + p, rows, :].astype(F32) * SCORE_SCALE, 0.0)
            values = jnp.where(mine, qkv_ref[2 * PAIRS + p, rows, :].astype(F32), 0.0)
            scores[h, :window, :span] = mm_nt(keys.astype(BF16), qkv_ref[p, wide, :])
            grad_probs[h, :window, :span] = mm_nt(values.astype(BF16), go[p, wide, :])

        def split(values):
            low = values.astype(F32)
            halves = (jnp.where(low_lane, low, 0.0), jnp.where(low_lane, 0.0, low))
            return jnp.concatenate(halves, axis=0).astype(BF16)

        score(0)
        for n in range(HEADS):
            p, h = divmod(n, 2)
            if n + 1 < HEADS:
                score(n + 1)
            if h == 0:
                lanes = slice(p * 128, (p + 1) * 128)
                product = go[p, wide, :].astype(F32) * o_ref[wide, lanes].astype(F32)
                upper = product.astype(BF16)
                lower = (product - upper.astype(F32)).astype(BF16)
                inner_rows = mm_nt(heads, upper) + mm_nt(heads, lower)
            logs = jnp.where(queries_inside, sums[n : n + 1, :span], 1e30)
            inner_row = inner_rows[h : h + 1]
            for r in range(0, window, 16):
                part = jnp.exp(scores[h, r : r + 16, :span] - logs)
                if r == 0 or r + 16 > full:
                    part = jnp.where(rows_inside(shift, full, r, 16), part, 0.0)
                probs[h, r : r + 16, :span] = part.astype(BF16)
                slope = part * (grad_probs[h, r : r + 16, :span] - inner_row)
                grad_scores[h, r : r + 16, :span] = slope.astype(BF16)
            if h == 1:
                slopes = [grad_scores[g, :window, :span] for g in range(2)]
                weights = [probs[g, :window, :span] for g in range(2)]
                keys = split(qkv_ref[PAIRS + p, rows, :])
                news = (
                    jnp.transpose(mm_tn(keys, jnp.concatenate(slopes, axis=0)))[:window] * SCORE_SCALE,
                    mm(jnp.concatenate(slopes, axis=1), split(qkv_ref[p, wide, :])) * SCORE_SCALE,
                    mm(jnp.concatenate(weights, axis=1), split(go[p, wide, :])),
                )
                for c in range(3):
                    old = gqkv[c * PAIRS + p, rows, :].astype(F32)
                    gqkv[c * PAIRS + p, rows, :] = jnp.where(inside, news[c], old).astype(BF16)

    over_images(len_ref, tokens, attend)

    w_q, w_k = unpack_weight(main_ref, 0, 0), unpack_weight(main_ref, 0, 1)
    w_v = unpack_weight(main_ref, 1, 0)
    w_qkv = jnp.concatenate([w_q, w_k, w_v], axis=1)
    sums_one = (zero, zero)
    for t in range(5):
        rows = pl.ds(t * tile, tile)
        grad_qkv = jnp.concatenate([gqkv[c, rows, :] for c in range(9)], axis=1)
        wide_rows[pl.ds(place(t * tile), tile), :] = mm_nt(grad_qkv, w_qkv)

        def first_norm(at, count, carry):
            gain, bias = carry
            rows = pl.ds(at, count)
            grad_h1 = wide_rows[pl.ds(place(at), count), :]
            normal, inverse = normed(patch_ref[rows, :].astype(F32))
            h1_all[rows, :] = (normal * norms[0:1] + norms[1:2]).astype(BF16)
            grad_x = gx1[rows, :] + norm_back(grad_h1, normal, inverse, norms[0:1])
            input_ref[rows, :] = grad_x.astype(BF16)
            return gain + fold_rows(grad_h1 * normal), bias + fold_rows(grad_h1)

        sums_one = over_rows(t * tile, (t + 1) * tile, sums_one, first_norm)
    gain_one, bias_one = sums_one
    grad = mm_tn(h1_all[...], jnp.concatenate([gqkv[c] for c in range(9)], axis=1))
    for c, (side, part) in enumerate(((0, 0), (0, 1), (1, 0))):
        put(side, part, grad[:, c * D : (c + 1) * D])
    zeros = jnp.zeros((small_rows - 4, D), F32)
    turned = [jnp.sum(one, axis=0, keepdims=True) for one in (gain_one, bias_one, gain_two, bias_two)]
    turned = jnp.concatenate(turned + [zeros], axis=0)
    gw_ref[1, :, 6 * GROUP_ROWS :, :] = pack_turned(turned)


def backward_local(lengths, patches, main, saved, result, gslots, experts):
    tokens = patches.shape[0]
    columns = experts * SLOT_ROWS
    kept = tokens if experts <= 16 else tokens // 5
    shape = jax.ShapeDtypeStruct
    return pl.pallas_call(
        functools.partial(backward_kernel, experts),
        out_shape=(
            shape((tokens, D), BF16),
            shape((tokens, D), BF16),
            shape((2,) + (GROUPS,) + main.shape[2:], F32),
        ),
        in_specs=[pl.BlockSpec(memory_space=pltpu.SMEM)] + whole(12),
        out_specs=tuple(whole(3)),
        scratch_shapes=[
            pltpu.VMEM((kept, columns), F32),
            pltpu.VMEM((tokens, columns), BF16),
            pltpu.VMEM((tokens, D), F32),
            pltpu.VMEM((tokens, D), BF16),
            pltpu.VMEM((PAIRS, tokens + WINDOW_PAD, 128), BF16),
            pltpu.VMEM((9, tokens, 128), BF16),
            pltpu.VMEM((tokens, D), BF16),
            pltpu.VMEM((2, LONG_WINDOW, LONG_SPAN), F32),
            pltpu.VMEM((2, LONG_WINDOW, LONG_SPAN), F32),
            pltpu.VMEM((2, LONG_WINDOW, LONG_SPAN), BF16),
            pltpu.VMEM((2, LONG_WINDOW, LONG_SPAN), BF16),
            pltpu.VMEM((128, LONG_SPAN), F32),
            pltpu.VMEM((kept, columns), F32),
            pltpu.VMEM((kept, D), F32),
        ],
        compiler_params=pltpu.CompilerParams(vmem_limit_bytes=vmem_bytes(experts, 34)),
        name="backward_local",
    )(lengths, patches, main, *saved, result, gslots)


def reduce_kernel(experts, gw_ref, square_ref, attn_out, phi_out, norm_out, total_ref, own, pair_in,
                  box_one, in_one, box_two, in_two, box_z, in_z, final, scalars, load_sem, sent,
                  pair_recv, recv_one, recv_two, recv_z, swap_sem, norm_recv):
    core, chip, first, second = ring(experts)
    rows = attn_out.shape[0]
    layers = experts // 4
    layer = chip // 4
    column = lax.rem(chip, 4)
    barrier = pltpu.get_barrier_semaphore()

    @pl.loop(1, experts)
    def _(j):
        peer = lax.rem(chip + j, experts)
        pl.semaphore_signal(barrier, inc=1, device_id=(core, peer), device_id_type=MESH)

    pl.semaphore_signal(barrier, inc=1, device_id=(1 - core, chip), device_id_type=MESH)
    load = pltpu.make_async_copy(gw_ref.at[core], own, load_sem.at[0])
    load.start()
    pl.semaphore_wait(barrier, experts)

    def send(source, target, send_sem, recv_sem, device):
        return pltpu.make_async_remote_copy(
            src_ref=source,
            dst_ref=target,
            send_sem=send_sem,
            recv_sem=recv_sem,
            device_id=device,
            device_id_type=MESH,
        )

    def pair_copy(place):
        return send(
            gw_ref.at[1 - core, :, place],
            pair_in.at[:, place],
            sent.at[0],
            pair_recv.at[place],
            (1 - core, chip),
        )

    def to_first(index):
        return send(box_one.at[index], in_one.at[index], sent.at[1], recv_one.at[index], (core, first))

    def to_second(index):
        return send(box_two.at[index], in_two.at[index], sent.at[2], recv_two.at[index], (core, second))

    def layer_at(d):
        return lax.rem(layer + 1 + d, layers)

    far = 3 - column

    both, one, two = far, lax.rem(first, 4), lax.rem(second, 4)

    for place in (both, two, one, column):
        pair_copy(place).start()

    load.wait()

    for batch, place in ((0, both), (1, one)):
        pair_copy(place).wait_recv()

        @pl.loop(0, layers)
        def _(d):
            index = batch * layers + layer_at(d)
            total = own[layer_at(d), place] + pair_in[layer_at(d), place]
            box_one[index] = total.astype(BF16)
            to_first(index).start()

    pair_copy(two).wait_recv()

    @pl.loop(0, layers)
    def _(d):
        index = layer_at(d)
        total = own[index, two] + pair_in[index, two]
        to_first(index).wait_recv()
        box_two[index] = (total + in_one[index].astype(F32)).astype(BF16)
        to_second(index).start()

    pair_copy(column).wait_recv()

    def to_layer(index):
        return send(
            box_z.at[index], in_z.at[layer], sent.at[3], recv_z.at[layer], (core, index * 4 + column)
        )

    def column_sum(index):
        total = own[index, column] + pair_in[index, column]
        to_first(layers + index).wait_recv()
        total = total + in_one[layers + index].astype(F32)
        to_second(index).wait_recv()
        return total + in_two[index].astype(F32)

    @pl.loop(0, layers - 1)
    def _(d):
        index = layer_at(d)
        box_z[index] = column_sum(index).astype(BF16)
        to_layer(index).start()

    final[core] = column_sum(layer)

    @pl.loop(1, layers)
    def _(d):
        index = lax.rem(layer - d + layers, layers)
        send(
            box_z.at[index], in_z.at[index], sent.at[3], recv_z.at[index], (core, index * 4 + column)
        ).wait_recv()
        final[core] += in_z[index].astype(F32)

    def swap(side):
        return send(final.at[side], final.at[side], swap_sem.at[0], swap_sem.at[1], (1 - core, chip))

    mine = final[core]
    swap(core).start()

    scalars[experts + core] = square_ref[...] + jnp.sum(mine * mine, axis=0, keepdims=True)

    def norm_pair(side):
        mine = scalars.at[experts + side]
        return send(mine, mine, swap_sem.at[2], swap_sem.at[3], (1 - core, chip))

    norm_pair(core).start()
    norm_pair(1 - core).wait_recv()
    scalars[chip] = scalars[experts] + scalars[experts + 1]

    @pl.loop(1, experts)
    def _(j):
        mine = scalars.at[chip]
        send(mine, mine, sent.at[4], norm_recv.at[0], (core, lax.rem(chip + j, experts))).start()

    swap(1 - core).wait_recv()
    for side in range(2):
        for part in range(2):
            for g in range(3):
                lanes = (side * 2 + part) * D + g * 128
                place = (2 * g + part) * rows
                attn_out[:, lanes : lanes + 128] = final[side, place : place + rows, :]
    phi_out[...] = final[0, 6 * rows : 6 * rows + experts, 0:rows]
    norm_out[...] = final[1, 6 * rows : 6 * rows + 4, 0:rows]

    others = scalars.at[pl.ds(0, experts - 1)]
    norms = send(others, others, sent.at[4], norm_recv.at[0], (1 - core, chip))
    norms.wait_recv()
    lanes = jnp.sum(scalars[0:experts], axis=0)
    total = jnp.sqrt(jnp.sum(lanes, axis=-1, keepdims=True))
    total_ref[...] = jnp.broadcast_to(total, (1, 128))
    swap(core).wait_send()
    norm_pair(core).wait_send()

    for source, sem in (
        (gw_ref.at[1 - core], 0),
        (box_one, 1),
        (box_two, 2),
        (box_z.at[pl.ds(0, layers - 1)], 3),
    ):
        send(source, source, sent.at[sem], sent.at[sem], (1 - core, chip)).wait_send()
    norms.wait_send()


def reduce_grads(grads, squares, experts):
    rows = D // experts
    layers = experts // 4
    block = grads.shape[2:]
    shape = jax.ShapeDtypeStruct
    dma = pltpu.SemaphoreType.DMA
    return pl.pallas_call(
        functools.partial(reduce_kernel, experts),
        out_shape=(
            shape((rows, 4 * D), F32),
            shape((experts, rows), F32),
            shape((4, rows), F32),
            shape((1, 128), F32),
        ),
        in_specs=[pl.BlockSpec(memory_space=pl.ANY)] + whole(1),
        out_specs=tuple(whole(4)),
        scratch_shapes=[
            pltpu.VMEM((layers, 4) + block, F32),
            pltpu.VMEM((layers, 4) + block, F32),
            pltpu.VMEM((2 * layers,) + block, BF16),
            pltpu.VMEM((2 * layers,) + block, BF16),
            pltpu.VMEM((layers,) + block, BF16),
            pltpu.VMEM((layers,) + block, BF16),
            pltpu.VMEM((layers,) + block, BF16),
            pltpu.VMEM((layers,) + block, BF16),
            pltpu.VMEM((2,) + block, F32),
            pltpu.VMEM((experts + 2, 1, 128), F32),
            dma((1,)),
            dma((5,)),
            dma((4,)),
            dma((2 * layers,)),
            dma((layers,)),
            dma((layers,)),
            dma((4,)),
            dma((1,)),
        ],
        compiler_params=pltpu.CompilerParams(
            collective_id=2, has_side_effects=True, vmem_limit_bytes=vmem_bytes(experts, 8)
        ),
        name="reduce_grads",
    )(grads.reshape((2, layers, 4) + block), squares)


def adam_update(weight, first_moment, second_moment, gradient, factor, learning_rate, decay_rate):
    clipped = gradient * factor
    first_new = BETA_FIRST * first_moment + (1.0 - BETA_FIRST) * clipped
    second_new = BETA_SECOND * second_moment + (1.0 - BETA_SECOND) * clipped * clipped
    step_rate = learning_rate / (1.0 - BETA_FIRST**STEP)
    root = jnp.sqrt(second_new * (1.0 / (1.0 - BETA_SECOND**STEP)))
    weight_new = weight * (1.0 - learning_rate * decay_rate) - step_rate * (
        first_new / (root + ADAM_EPS)
    )
    return (weight_new, first_new, second_new)


RATES = (
    (1.0 / math.sqrt(D), WEIGHT_DECAY),
    (0.25 / math.sqrt(D), WEIGHT_DECAY),
    (0.8, 0.0),
    (4.0 / math.sqrt(D), WEIGHT_DECAY),
    (8.0 / math.sqrt(FF), WEIGHT_DECAY),
)
UPDATE_STEPS = 4


def update_kernel(norm_ref, *refs):
    grad_norm = norm_ref[...]
    factor = CLIP_NORM / jnp.maximum(grad_norm, CLIP_NORM)
    factor = factor[0:1, 0:1]
    inputs, outputs = refs[:20], refs[20:]
    for k, (rate, decay) in enumerate(RATES):
        weight, first, second, grad = (ref[...] for ref in inputs[4 * k : 4 * k + 4])
        by = factor.reshape((1,) * grad.ndim)
        news = adam_update(weight, first, second, grad, by, rate, decay)
        for ref, new in zip(outputs[3 * k : 3 * k + 3], news):
            ref[...] = new


def update(norm_tile, groups):
    def spec(k, shape):
        if k == 0:
            return pl.BlockSpec((shape[0], shape[1] // UPDATE_STEPS), lambda i: (0, i))
        if k < 3:
            return pl.BlockSpec(shape, lambda i: (0, 0))
        return pl.BlockSpec((1, shape[1] // UPDATE_STEPS, shape[2]), lambda i: (0, i, 0))

    specs = [spec(k, group[0].shape) for k, group in enumerate(groups)]
    return pl.pallas_call(
        update_kernel,
        grid=(UPDATE_STEPS,),
        out_shape=tuple(
            jax.ShapeDtypeStruct(group[0].shape, F32) for group in groups for _ in range(3)
        ),
        in_specs=[pl.BlockSpec((1, 128), lambda i: (0, 0))]
        + [one for one in specs for _ in range(4)],
        out_specs=tuple(one for one in specs for _ in range(3)),
        compiler_params=pltpu.CompilerParams(vmem_limit_bytes=24 * 1024 * 1024),
        name="update",
    )(norm_tile, *[array for group in groups for array in group])


def in_hbm(array):
    return pltpu.with_memory_space_constraint(array, pltpu.HBM)


def pad_to(array, shape):
    return jnp.pad(array, [(0, full - size) for size, full in zip(array.shape, shape)])


def regroup_weights(blocks, experts):
    rows = D // experts
    if rows == GROUP_ROWS:
        return blocks
    main = blocks[:, :, : 6 * rows].reshape(experts, 2, 3, 2, rows, 128).transpose(1, 2, 3, 0, 4, 5)
    main = main.reshape(2, 3, 2, GROUPS, GROUP_ROWS, 128).transpose(3, 0, 1, 2, 4, 5)
    main = main.reshape(GROUPS, 2, 6 * GROUP_ROWS, 128)
    small_rows = max(experts, 16)
    small = blocks[:, :, 6 * rows :, :rows]
    small = pad_to(small[:, :, :small_rows], (experts, 2, small_rows, rows))
    small = small.transpose(1, 2, 0, 3).reshape(2, small_rows, GROUPS, GROUP_ROWS)
    small = pad_to(small.transpose(2, 0, 1, 3), (GROUPS, 2, small_rows, 128))
    return jnp.concatenate([main, small], axis=2)


def regroup_grads(groups, experts):
    rows = D // experts
    if rows == GROUP_ROWS:
        return groups
    main = groups[:, :, : 6 * GROUP_ROWS].reshape(2, GROUPS, 3, 2, GROUP_ROWS, 128)
    main = main.transpose(0, 2, 3, 1, 4, 5).reshape(2, 3, 2, experts, rows, 128)
    main = main.transpose(0, 3, 1, 2, 4, 5).reshape(2, experts, 6 * rows, 128)
    small = groups[:, :, 6 * GROUP_ROWS :, :GROUP_ROWS]
    small_rows = min(small.shape[2], block_rows(experts) - 6 * rows)
    small = small[:, :, :small_rows].transpose(0, 2, 1, 3).reshape(2, small_rows, experts, rows)
    small = pad_to(small.transpose(0, 2, 1, 3), (2, experts, small_rows, 128))
    both = jnp.concatenate([main, small], axis=2)
    return pad_to(both, (2, experts, block_rows(experts), 128))


def local(
    patches,
    slot_len,
    attn_weight,
    attn_first,
    attn_second,
    phi_weight,
    phi_first,
    phi_second,
    norm_params,
    norm_first,
    norm_second,
    expert_in,
    in_first,
    in_second,
    expert_out,
    out_first,
    out_second,
    cotangent,
):
    experts = lax.axis_size("expert")
    weights = gather_weights(
        in_hbm(attn_weight), in_hbm(phi_weight.T), in_hbm(norm_params), experts
    )
    weights = regroup_weights(weights, experts)
    *saved, packed = forward_local(
        slot_len, patches, weights, in_hbm(cotangent), experts
    )
    result, gslots, grad_in, grad_out, squares = run_experts(packed, expert_in, expert_out, experts)
    block_output, input_grad, grads = backward_local(
        slot_len, patches, weights, saved, result, gslots, experts
    )
    grads = regroup_grads(grads, experts)
    attn_part, phi_part, norm_part, norm_tile = reduce_grads(grads, squares, experts)
    news = update(
        norm_tile,
        (
            (attn_weight, attn_first, attn_second, attn_part),
            (phi_weight.T, phi_first.T, phi_second.T, phi_part),
            (norm_params, norm_first, norm_second, norm_part),
            (expert_in, in_first, in_second, grad_in),
            (expert_out, out_first, out_second, grad_out),
        ),
    )
    attn_new, attn_first_new, attn_second_new = news[0:3]
    phi_new, phi_first_new, phi_second_new = (new.T for new in news[3:6])
    norm_new, norm_first_new, norm_second_new = news[6:9]
    in_new, in_first_new, in_second_new = news[9:12]
    out_new, out_first_new, out_second_new = news[12:15]
    grad_norm = norm_tile[0, 0]
    return (
        block_output,
        input_grad,
        grad_norm,
        attn_new,
        attn_first_new,
        attn_second_new,
        phi_new,
        phi_first_new,
        phi_second_new,
        norm_new,
        norm_first_new,
        norm_second_new,
        in_new,
        in_first_new,
        in_second_new,
        out_new,
        out_first_new,
        out_second_new,
    )


def solution(mesh):
    in_specs = (
        P(("batch", "expert"), None),
        P(("batch", "expert"), None),
        P("expert", None),
        P("expert", None),
        P("expert", None),
        P("expert", None),
        P("expert", None),
        P("expert", None),
        P(None, "expert"),
        P(None, "expert"),
        P(None, "expert"),
        P("expert", None, "batch"),
        P("expert", None, "batch"),
        P("expert", None, "batch"),
        P("expert", "batch", None),
        P("expert", "batch", None),
        P("expert", "batch", None),
        P(("batch", "expert"), None),
    )
    out_specs = (
        P(("batch", "expert"), None),
        P(("batch", "expert"), None),
        P(),
        P("expert", None),
        P("expert", None),
        P("expert", None),
        P("expert", None),
        P("expert", None),
        P("expert", None),
        P(None, "expert"),
        P(None, "expert"),
        P(None, "expert"),
        P("expert", None, "batch"),
        P("expert", None, "batch"),
        P("expert", None, "batch"),
        P("expert", "batch", None),
        P("expert", "batch", None),
        P("expert", "batch", None),
    )
    return jax.shard_map(local, mesh=mesh, in_specs=in_specs, out_specs=out_specs, check_vma=False)
```

```python
import functools
import math

import jax
import jax.numpy as jnp
from jax import lax
from jax.experimental import pallas as pl
from jax.experimental.pallas import tpu as pltpu
from jax.sharding import PartitionSpec as P

D = 384
HEADS = 6
HEAD_DIM = 64
FF = 1536
STEP = 3
SHORT_LEN = 196
LONG_LEN = 576
IMAGES = 5
SLOT_ROWS = 8
PAIRS = 3
GROUPS = 16
GROUP_ROWS = D // GROUPS
CHUNK = 112
LONG_WINDOW = 592
LONG_SPAN = 640
WINDOW_PAD = 48

NORM_EPS = 1e-06
CLIP_NORM = 1.0
BETA_FIRST = 0.5
BETA_SECOND = 0.5
ADAM_EPS = 1e-08
WEIGHT_DECAY = 0.05
MASKED = -1e30
SCORE_SCALE = HEAD_DIM ** (-0.5)

MESH = pl.DeviceIdType.MESH
F32 = jnp.float32
BF16 = jnp.bfloat16


def vmem_bytes(experts, mebibytes):
    return (mebibytes if experts <= 16 else 60) * 1024 * 1024


def whole(count):
    return [pl.BlockSpec(memory_space=pltpu.VMEM)] * count


def round_up(value, unit):
    return -(-value // unit) * unit


def mm(left, right):
    return jnp.dot(left, right, preferred_element_type=F32)


def mm_nt(left, right):
    return lax.dot_general(left, right, (((1,), (1,)), ((), ())), preferred_element_type=F32)


def mm_tn(left, right):
    return lax.dot_general(left, right, (((0,), (0,)), ((), ())), preferred_element_type=F32)


def block_rows(experts):
    rows = D // experts
    return round_up(6 * rows + max(experts, 4), 16)


def ring(experts):
    core = lax.axis_index("batch")
    chip = lax.axis_index("expert")
    first = chip ^ (1 + core)
    second = chip ^ (2 - core)
    return core, chip, first, second


def gather_kernel(experts, attn_hbm, phi_hbm, norm_hbm, patch_hbm, out, normal_ref, inverse_ref, patch_ref, stage, attn_ref, phi_ref, norm_ref, load_sem,
                  sent, recv):
    core, chip, first, second = ring(experts)
    rows = attn_ref.shape[0]
    half = pl.multiple_of(core * (2 * D), 128)
    loads = [
        pltpu.make_async_copy(attn_hbm.at[:, pl.ds(half, 2 * D)], attn_ref, load_sem.at[0]),
        pltpu.make_async_copy(phi_hbm, phi_ref, load_sem.at[1]),
        pltpu.make_async_copy(norm_hbm, norm_ref, load_sem.at[2]),
    ]
    for load in loads:
        load.start()
    load_patches = pltpu.make_async_copy(patch_hbm, patch_ref, load_sem.at[3])
    load_patches.start()
    column = lax.rem(chip, 4)
    layers = experts // 4
    layer = chip // 4
    barrier = pltpu.get_barrier_semaphore()

    @pl.loop(1, layers)
    def _(d):
        peer = lax.rem(layer + d, layers) * 4 + column
        pl.semaphore_signal(barrier, inc=1, device_id=(core, peer), device_id_type=MESH)

    pl.semaphore_signal(barrier, inc=1, device_id=(core, first), device_id_type=MESH)
    pl.semaphore_signal(barrier, inc=1, device_id=(core, second), device_id_type=MESH)
    pl.semaphore_signal(barrier, inc=1, device_id=(1 - core, chip), device_id_type=MESH)
    stage[...] = jnp.zeros_like(stage)
    for load in loads:
        load.wait()
    for part in range(2):
        for g in range(3):
            lanes = part * D + g * 128
            place = (2 * g + part) * rows
            stage[place : place + rows, :] = attn_ref[:, lanes : lanes + 128]

    @pl.when(core == 0)
    def _():
        stage[6 * rows : 6 * rows + experts, 0:rows] = phi_ref[...]

    @pl.when(core == 1)
    def _():
        stage[6 * rows : 6 * rows + 4, 0:rows] = norm_ref[...]

    out[chip, core] = stage[...].astype(BF16)
    pl.semaphore_wait(barrier, layers + 2)

    def copy(source, target, send_sem, recv_sem, device):
        return pltpu.make_async_remote_copy(
            src_ref=source,
            dst_ref=target,
            send_sem=send_sem,
            recv_sem=recv_sem,
            device_id=device,
            device_id_type=MESH,
        )

    def along(block, peer):
        mine = out.at[block, core]
        return copy(mine, mine, sent.at[0], recv.at[block], (core, peer))

    def to_pair(block):
        mine = out.at[block, core]
        return copy(mine, mine, sent.at[1], sent.at[2], (1 - core, chip))

    @pl.loop(1, layers)
    def _(d):
        along(chip, lax.rem(layer + d, layers) * 4 + column).start()

    along(chip, first).start()
    along(chip, second).start()
    to_pair(chip).start()

    load_patches.wait()

    def statistics(at, count, carry):
        rows = pl.ds(at, count)
        normal, inverse = normed(patch_ref[rows, :].astype(F32))
        normal_ref[rows, :] = normal
        inverse_ref[rows, :] = jnp.broadcast_to(inverse, (count, 128))
        return carry

    over_rows(0, patch_ref.shape[0], 0, statistics)

    @pl.loop(1, layers)
    def _(d):
        block = lax.rem(layer - d + layers, layers) * 4 + column
        along(block, first).wait_recv()
        along(block, first).start()
        along(block, second).start()
        to_pair(block).start()

    @pl.loop(0, layers)
    def _(d):
        block = lax.rem(layer - d + layers, layers) * 4 + lax.rem(first, 4)
        along(block, first).wait_recv()
        along(block, second).start()
        to_pair(block).start()

    @pl.loop(0, 2 * layers)
    def _(d):
        other = jnp.where(lax.rem(d, 2) == 0, lax.rem(second, 4), lax.rem(3 - column, 4))
        block = lax.rem(layer - d // 2 + layers, layers) * 4 + other
        along(block, first).wait_recv()
        to_pair(block).start()

    sides = out.at[pl.ds(0, experts - 1), core]
    copy(sides, sides, sent.at[0], sent.at[0], (1 - core, chip)).wait_send()
    copy(out.at[:, core], out.at[:, 1 - core], sent.at[1], sent.at[2], (1 - core, chip)).wait()


def gather_weights(attn_weight, phi_turned, norm_params, patches, experts):
    rows = block_rows(experts)
    tokens = patches.shape[0]
    dma = pltpu.SemaphoreType.DMA
    return pl.pallas_call(
        functools.partial(gather_kernel, experts),
        out_shape=(
            jax.ShapeDtypeStruct((experts, 2, rows, 128), BF16),
            jax.ShapeDtypeStruct((tokens, D), F32),
            jax.ShapeDtypeStruct((tokens, 128), F32),
        ),
        in_specs=[pl.BlockSpec(memory_space=pltpu.HBM)] * 4,
        out_specs=tuple(whole(3)),
        scratch_shapes=[
            pltpu.VMEM((tokens, D), BF16),
            pltpu.VMEM((rows, 128), F32),
            pltpu.VMEM((attn_weight.shape[0], 2 * D), F32),
            pltpu.VMEM(phi_turned.shape, F32),
            pltpu.VMEM(norm_params.shape, F32),
            dma((4,)),
            dma((3,)),
            dma((experts,)),
        ],
        compiler_params=pltpu.CompilerParams(
            collective_id=0, has_side_effects=True, vmem_limit_bytes=vmem_bytes(experts, 10)
        ),
        name="gather_weights",
    )(attn_weight, phi_turned, norm_params, patches)


def unpack_weight(main_ref, side, part):
    blocks = main_ref[:, side].astype(F32)
    columns = []
    for g in range(3):
        place = (2 * g + part) * GROUP_ROWS
        columns.append(blocks[:, place : place + GROUP_ROWS, :].reshape(D, 128))
    return jnp.concatenate(columns, axis=1).astype(BF16)


def group_lanes():
    lane = lax.broadcasted_iota(jnp.int32, (128, D), 0)
    column = lax.broadcasted_iota(jnp.int32, (128, D), 1)
    return jnp.where(column % GROUP_ROWS == lane, 1.0, 0.0).astype(BF16)


def unpack_turned(main_ref, side, rows):
    first = 6 * GROUP_ROWS
    blocks = main_ref[:, side].astype(F32)[:, first : first + rows, :]
    spread = mm(blocks.reshape(GROUPS * rows, 128).astype(BF16), group_lanes())
    spread = spread.reshape(GROUPS, rows, D)
    group = lax.broadcasted_iota(jnp.int32, (GROUPS, 1, D), 0)
    column = lax.broadcasted_iota(jnp.int32, (GROUPS, 1, D), 2)
    return jnp.sum(jnp.where(column // GROUP_ROWS == group, spread, 0.0), axis=0)


def pack_turned(values):
    rows = values.shape[0]
    group = lax.broadcasted_iota(jnp.int32, (GROUPS, 1, D), 0)
    column = lax.broadcasted_iota(jnp.int32, (GROUPS, 1, D), 2)
    spread = jnp.where(column // GROUP_ROWS == group, values[None], 0.0)
    spread = spread.reshape(GROUPS * rows, D).astype(BF16)
    return mm_nt(spread, group_lanes()).reshape(GROUPS, rows, 128)


def unpack_small(main_ref, experts):
    turned = unpack_turned(main_ref, 0, max(experts, 16)).astype(BF16)
    row = lax.broadcasted_iota(jnp.int32, (experts * SLOT_ROWS, turned.shape[0]), 0)
    column = lax.broadcasted_iota(jnp.int32, (experts * SLOT_ROWS, turned.shape[0]), 1)
    spread = jnp.where(column == row // SLOT_ROWS, 1.0, 0.0).astype(BF16)
    return mm(spread, turned).astype(BF16), unpack_turned(main_ref, 1, 8)


def slot_bounds(len_ref, columns):
    image = lax.broadcasted_iota(jnp.int32, (1, columns), 1) % SLOT_ROWS
    starts = jnp.zeros((1, columns), jnp.int32)
    ends = jnp.zeros((1, columns), jnp.int32)
    start = jnp.int32(0)
    for k in range(IMAGES):
        end = start + len_ref[0, k]
        starts = jnp.where(image == k, start, starts)
        ends = jnp.where(image == k, end, ends)
        start = end
    return starts, ends, start


def normed(values):
    centred = values - jnp.mean(values, axis=-1, keepdims=True)
    variance = jnp.mean(centred * centred, axis=-1, keepdims=True)
    inverse = lax.rsqrt(variance + NORM_EPS)
    return centred * inverse, inverse


def norm_back(grad_shaped, normal, inverse, scaling):
    grad_normal = grad_shaped * scaling
    return inverse * (
        grad_normal
        - jnp.mean(grad_normal, axis=-1, keepdims=True)
        - normal * jnp.mean(grad_normal * normal, axis=-1, keepdims=True)
    )


def over_rows(start, stop, carry, body):
    for at in range(start, stop, CHUNK):
        carry = body(at, min(CHUNK, stop - at), carry)
    return carry


def thrice(values):
    return jnp.concatenate([values] * 3, axis=1)


def fold_rows(values):
    return jnp.sum(values.reshape(values.shape[0] // 8, 8, values.shape[1]), axis=0)


def over_images(len_ref, tokens, body):
    def step(k, start):
        length = len_ref[0, k]
        for full in (SHORT_LEN, LONG_LEN):

            @pl.when(length == full)
            def _():
                window = round_up(full + 12, 16)
                first = jnp.minimum((start // 16) * 16, tokens - window)
                body(pl.multiple_of(first, 16), start - first, full, window)

        return start + length

    lax.fori_loop(0, IMAGES, step, jnp.int32(0))


def rows_inside(shift, full, first, count):
    row = first + lax.broadcasted_iota(jnp.int32, (count, 1), 0)
    return (row >= shift) & (row < shift + full)


def columns_inside(shift, full, count):
    column = lax.broadcasted_iota(jnp.int32, (1, count), 1)
    return (column >= shift) & (column < shift + full)


def forward_kernel(experts, len_ref, patch_ref, main_ref, norm_ref, cot_hbm, w_ref, phi_ref, norms_ref,
                   normal_ref, inverse_ref, h1_all, qkv_ref, o_ref, lse_ref, x1_ref, h2_ref, disp_ref,
                   comb_ref, gy_ref, pack_ref, logit, packf, scores,
                   probs, peaks, cot_ref, load_sem):
    load = pltpu.make_async_copy(cot_hbm, cot_ref, load_sem.at[0])
    load.start()
    tokens = patch_ref.shape[0]
    columns = experts * SLOT_ROWS
    tile = tokens // 5
    phi, norms = unpack_small(main_ref, experts)
    starts, ends, total = slot_bounds(len_ref, columns)
    norms_ref[...] = norms
    phi_ref[...] = phi
    for k in range(4):
        w_ref[:, k * D : (k + 1) * D] = unpack_weight(main_ref, k // 2, k % 2)
    w_qkv = w_ref[:, : 3 * D]

    def first_norm(at, count, carry):
        rows = pl.ds(at, count)
        h1_all[rows, :] = (norm_ref[rows, :] * norms[0:1] + norms[1:2]).astype(BF16)
        return carry

    over_rows(0, tokens, 0, first_norm)
    for t in range(5):
        rows = pl.ds(t * tile, tile)
        qkv = mm(h1_all[rows, :], w_qkv).astype(BF16)
        for c in range(9):
            qkv_ref[c, rows, :] = qkv[:, c * 128 : (c + 1) * 128]
    qkv_ref[:, tokens:, :] = jnp.zeros((9, WINDOW_PAD, 128), BF16)
    o_ref[...] = jnp.zeros_like(o_ref)
    lse_ref[...] = jnp.zeros_like(lse_ref)
    low_lane = lax.broadcasted_iota(jnp.int32, (1, 128), 1) < HEAD_DIM
    lane = lax.broadcasted_iota(jnp.int32, (1, 128), 1)

    def attend(first, shift, full, window):
        span = round_up(window, 128)
        bias = jnp.where(columns_inside(shift, full, span), 0.0, MASKED)
        inside = rows_inside(shift, full, 0, window)
        rows = pl.ds(first, window)
        wide = pl.ds(first, span)

        ones = jnp.ones((span, 128), BF16)

        def score(n):
            p, h = divmod(n, 2)
            mine = low_lane if h == 0 else jnp.logical_not(low_lane)
            query = jnp.where(mine, qkv_ref[p, rows, :].astype(F32) * SCORE_SCALE, 0.0)
            keys = qkv_ref[PAIRS + p, wide, :]
            scores[h, :window, :span] = mm_nt(query.astype(BF16), keys)

        score(0)
        outs = []
        for n in range(HEADS):
            p, h = divmod(n, 2)
            if n + 1 < HEADS:
                score(n + 1)
            for r in range(0, window, 16):
                part = scores[h, r : r + 16, :span] + bias
                peak = jnp.max(part, axis=-1, keepdims=True)
                probs[h, r : r + 16, :span] = jnp.exp(part - peak).astype(BF16)
                peaks[h, r : r + 16, :] = jnp.broadcast_to(peak, (16, 128))
            values = jnp.concatenate([qkv_ref[2 * PAIRS + p, wide, :], ones], axis=1)
            both = mm(probs[h, :window, :span], values)
            summed = both[:, 128:]
            outs.append(both[:, :128] * (1.0 / summed))
            logs = peaks[h, :window, :] + jnp.log(summed)
            lse_ref[rows, :] = jnp.where(inside & (lane == n), logs, lse_ref[rows, :])
            if h == 1:
                lanes = slice(p * 128, (p + 1) * 128)
                old = o_ref[rows, lanes].astype(F32)
                merged = jnp.where(inside, jnp.where(low_lane, outs[n - 1], outs[n]), old)
                o_ref[rows, lanes] = merged.astype(BF16)

    over_images(len_ref, tokens, attend)

    load.wait()
    w_o = w_ref[:, 3 * D :]
    for t in range(5):
        rows = pl.ds(t * tile, tile)
        x1_ref[rows, :] = mm(o_ref[rows, :], w_o)

    def second_norm(at, count, carry):
        rows = pl.ds(at, count)
        x1 = patch_ref[rows, :].astype(F32) + x1_ref[rows, :]
        normal, inverse = normed(x1)
        normal_ref[rows, :] = normal
        inverse_ref[rows, :] = jnp.broadcast_to(inverse, (count, 128))
        h2_ref[rows, :] = (normal * norms[2:3] + norms[3:4]).astype(BF16)
        valid = at + lax.broadcasted_iota(jnp.int32, (count, 1), 0) < total
        x1_ref[rows, :] = jnp.where(valid, x1, 0.0)
        gy_ref[rows, :] = jnp.where(valid, cot_ref[rows, :].astype(F32), 0.0).astype(BF16)
        return carry

    over_rows(0, tokens, 0, second_norm)
    logit[...] = mm_nt(h2_ref[...], phi)

    def members(at, count):
        position = at + lax.broadcasted_iota(jnp.int32, (count, columns), 0)
        return (position >= starts) & (position < ends)

    def mixing(at, count, peak):
        rows = pl.ds(at, count)
        logits = logit[rows, :]
        member = members(at, count)
        exponent = jnp.exp(logits - jnp.max(logits, axis=-1, keepdims=True))
        summed = jnp.sum(exponent, axis=-1, keepdims=True) * (1.0 / SLOT_ROWS)
        comb_ref[rows, :] = jnp.where(member, exponent * (1.0 / summed), 0.0)
        inside = jnp.where(member, logits, MASKED)
        return jnp.maximum(peak, jnp.max(inside.reshape(count // 8, 8, columns), axis=0))

    peak = over_rows(0, tokens, jnp.full((8, columns), MASKED, F32), mixing)
    present = ends > starts
    peak = jnp.where(present, jnp.max(peak, axis=0, keepdims=True), 0.0)

    def exponents(at, count, summed):
        rows = pl.ds(at, count)
        member = members(at, count)
        exponent = jnp.exp(jnp.where(member, logit[rows, :] - peak, 0.0))
        exponent = jnp.where(member, exponent, 0.0)
        disp_ref[rows, :] = exponent
        return summed + fold_rows(exponent)

    summed = over_rows(0, tokens, jnp.zeros((8, columns), F32), exponents)
    summed = jnp.sum(summed, axis=0, keepdims=True) + jnp.where(present, 0.0, 1.0)
    dispatch = disp_ref[...] * (1.0 / summed)
    disp_ref[...] = dispatch
    slots = mm_tn(dispatch.astype(BF16), h2_ref[...])
    grad_result = mm_tn(comb_ref[...].astype(BF16), gy_ref[...])
    for part, matrix in enumerate((slots, grad_result)):
        pack_rows(packf, matrix.reshape(experts, SLOT_ROWS, D))
        pack_ref[:, part * 16 : (part + 1) * 16, :] = packf[...].astype(BF16)


def pack_rows(packf, blocks):
    packf[...] = jnp.zeros_like(packf)
    for c in range(3):
        packf[:, c * IMAGES : (c + 1) * IMAGES, :] = blocks[:, :IMAGES, c * 128 : (c + 1) * 128]


def unpack_rows(packf, wide):
    wide[...] = jnp.zeros_like(wide)
    for c in range(3):
        wide[:, 0:IMAGES, c * 128 : (c + 1) * 128] = packf[:, c * IMAGES : (c + 1) * IMAGES, :]


def forward_local(lengths, patches, main, normal, cotangent, experts):
    tokens = patches.shape[0]
    columns = experts * SLOT_ROWS
    shape = jax.ShapeDtypeStruct
    return pl.pallas_call(
        functools.partial(forward_kernel, experts),
        out_shape=(
            shape((D, 4 * D), BF16),
            shape((columns, D), BF16),
            shape((8, D), F32),
            shape((tokens, D), F32),
            shape((tokens, 128), F32),
            shape((tokens, D), BF16),
            shape((9, tokens + WINDOW_PAD, 128), BF16),
            shape((tokens + WINDOW_PAD, D), BF16),
            shape((tokens + WINDOW_PAD, 128), F32),
            shape((tokens, D), F32),
            shape((tokens, D), BF16),
            shape((tokens, columns), F32),
            shape((tokens, columns), F32),
            shape((tokens, D), BF16),
            shape((experts, 32, 128), BF16),
        ),
        in_specs=[pl.BlockSpec(memory_space=pltpu.SMEM)]
        + whole(3)
        + [pl.BlockSpec(memory_space=pltpu.HBM)],
        out_specs=tuple(whole(15)),
        scratch_shapes=[
            pltpu.VMEM((tokens, columns), F32),
            pltpu.VMEM((experts, 16, 128), F32),
            pltpu.VMEM((2, LONG_WINDOW, LONG_SPAN), F32),
            pltpu.VMEM((2, LONG_WINDOW, LONG_SPAN), BF16),
            pltpu.VMEM((2, LONG_WINDOW, 128), F32),
            pltpu.VMEM((tokens, D), BF16),
            pltpu.SemaphoreType.DMA((1,)),
        ],
        compiler_params=pltpu.CompilerParams(vmem_limit_bytes=vmem_bytes(experts, 24)),
        name="forward_local",
    )(lengths, patches, main, normal, cotangent)


def expert_kernel(experts, pack_ref, in_ref, out_ref, result_ref, gslot_ref, gin_ref, gout_ref,
                  square_ref, inbox, partial, given, outbox, back, packf, packe, widee, sems):
    core = lax.axis_index("batch")
    chip = lax.axis_index("expert")
    barrier = pltpu.get_barrier_semaphore()

    @pl.loop(1, experts)
    def _(j):
        peer = lax.rem(chip + j, experts)
        pl.semaphore_signal(barrier, inc=1, device_id=(core, peer), device_id_type=MESH)

    pl.semaphore_signal(barrier, inc=1, device_id=(1 - core, chip), device_id_type=MESH)
    w_in = in_ref[0].astype(BF16)
    w_out = out_ref[0].astype(BF16)
    for part in range(2):
        inbox[part, core, chip] = pack_ref[chip, part * 16 : (part + 1) * 16, :]
    pl.semaphore_wait(barrier, experts)

    def copy(source, target, sem, device):
        return pltpu.make_async_remote_copy(
            src_ref=source,
            dst_ref=target,
            send_sem=sems.at[sem],
            recv_sem=sems.at[sem + 1],
            device_id=device,
            device_id_type=MESH,
        )

    others = pl.ds(0, experts - 1)
    firsts, pairs, halves, seconds = [], [], [], []
    for part in range(2):
        block = pl.ds(part * 16, 16)

        @pl.loop(1, experts)
        def _(j):
            peer = lax.rem(chip + j, experts)
            copy(
                pack_ref.at[peer, block], inbox.at[part, core, chip], 2 * part, (core, peer)
            ).start()

        firsts.append(
            copy(pack_ref.at[others, block], inbox.at[part, core, others], 2 * part, (core, chip))
        )
        mine = inbox.at[part, core]
        pairs.append(copy(mine, mine, 4 + 2 * part, (1 - core, chip)))
        halves.append(copy(partial.at[part], given.at[part], 8 + 2 * part, (1 - core, chip)))
        seconds.append(
            copy(outbox.at[part, others], back.at[part, others], 12 + 2 * part, (core, chip))
        )

    def spread(part, side):
        packe[...] = inbox[part, side].astype(F32)
        unpack_rows(packe, widee)
        return widee[...].reshape(experts * SLOT_ROWS, D).astype(BF16)

    root = math.sqrt(2.0 / math.pi)

    def forward(side):
        slots = spread(0, side)
        hidden = mm(slots, w_in)
        bent = jnp.tanh(root * (hidden + 0.044715 * (hidden * hidden * hidden)))
        half = 0.5 * (1.0 + bent)
        act = (hidden * half).astype(BF16)
        slope = half + 0.5 * hidden * (1.0 - bent * bent) * (
            root * (1.0 + 3.0 * 0.044715 * (hidden * hidden))
        )
        return slots, act, slope, mm(act, w_out)

    def backward(side, slope):
        grads = spread(1, side)
        grad_hidden = (mm_nt(grads, w_out) * slope).astype(BF16)
        return grads, grad_hidden, mm_nt(grad_hidden, w_in)

    def give_half(part, values):
        pack_rows(packf, values.reshape(experts, SLOT_ROWS, D))
        partial[part] = packf[...].astype(BF16)
        halves[part].start()

    def send_back(part, values):
        pack_rows(packf, values.reshape(experts, SLOT_ROWS, D))
        halves[part].wait_recv()
        outbox[part] = (packf[...] + given[part].astype(F32)).astype(BF16)

        @pl.loop(1, experts)
        def _(j):
            peer = lax.rem(chip + j, experts)
            copy(outbox.at[part, peer], back.at[part, chip], 12 + 2 * part, (core, peer)).start()

        back[part, chip] = outbox[part, chip]

    firsts[0].wait_recv()
    pairs[0].start()
    pairs[0].wait_recv()
    their_slots, their_act, their_slope, their_result = forward(1 - core)
    give_half(0, their_result)
    firsts[1].wait_recv()
    pairs[1].start()
    our_slots, our_act, our_slope, our_result = forward(core)
    send_back(0, our_result)
    pairs[1].wait_recv()
    their_grads, their_hidden, their_back = backward(1 - core, their_slope)
    give_half(1, their_back)
    our_grads, our_hidden, our_back = backward(core, our_slope)
    send_back(1, our_back)
    grad_out = mm_tn(our_act, our_grads) + mm_tn(their_act, their_grads)
    gout_ref[0] = grad_out
    grad_in = mm_tn(our_slots, our_hidden) + mm_tn(their_slots, their_hidden)
    gin_ref[0] = grad_in
    squares = jnp.zeros((1, 128), F32)
    for grad in (grad_out, grad_in):
        columns = jnp.sum(grad * grad, axis=0, keepdims=True)
        for c in range(0, grad.shape[1], 128):
            squares = squares + columns[:, c : c + 128]
    square_ref[...] = squares
    for part, target in enumerate((result_ref, gslot_ref)):
        seconds[part].wait_recv()
        packe[...] = back[part].astype(F32)
        unpack_rows(packe, widee)
        target[...] = widee[...].reshape(experts * SLOT_ROWS, D).astype(BF16)
    for sent in firsts + pairs + halves + seconds:
        sent.wait_send()


def run_experts(packed, expert_in, expert_out, experts):
    shape = jax.ShapeDtypeStruct
    return pl.pallas_call(
        functools.partial(expert_kernel, experts),
        out_shape=(
            shape((experts * SLOT_ROWS, D), BF16),
            shape((experts * SLOT_ROWS, D), BF16),
            shape(expert_in.shape, F32),
            shape(expert_out.shape, F32),
            shape((1, 128), F32),
        ),
        in_specs=whole(3),
        out_specs=tuple(whole(5)),
        scratch_shapes=[
            pltpu.VMEM((2, 2, experts, 16, 128), BF16),
            pltpu.VMEM((2, experts, 16, 128), BF16),
            pltpu.VMEM((2, experts, 16, 128), BF16),
            pltpu.VMEM((2, experts, 16, 128), BF16),
            pltpu.VMEM((2, experts, 16, 128), BF16),
            pltpu.VMEM((experts, 16, 128), F32),
            pltpu.VMEM((experts, 16, 128), F32),
            pltpu.VMEM((experts, SLOT_ROWS, D), F32),
            pltpu.SemaphoreType.DMA((16,)),
        ],
        compiler_params=pltpu.CompilerParams(
            collective_id=1, has_side_effects=True, vmem_limit_bytes=vmem_bytes(experts, 8)
        ),
        name="run_experts",
    )(packed, expert_in, expert_out)


def backward_kernel(experts, len_ref, normal_one, inverse_one, w_ref, phi_ref, norms_ref, normal_two,
                    inverse_two, h1_all, qkv_ref, o_ref, lse_ref, h2_ref, disp_ref, comb_ref, gy_ref,
                    result_ref, gslot_ref, input_ref, gw_ref, gdisp, glog, gx1, branch, go, gqkv,
                    scores, grad_probs, probs, grad_scores, sums, gcomb, wide_rows):
    tokens = h2_ref.shape[0]
    columns = experts * SLOT_ROWS
    tile = tokens // 5
    phi, norms = phi_ref[...], norms_ref[...]
    result = result_ref[...]
    gslots = gslot_ref[...]

    kept = gdisp.shape[0] == tokens

    def place(at):
        return at if kept else at % tile

    inner = jnp.zeros((8, columns), F32)
    for t in range(5):
        rows = pl.ds(t * tile, tile)
        gdisp[pl.ds(place(t * tile), tile), :] = mm_nt(h2_ref[rows, :], gslots)

        def dispatch_inner(at, count, inner):
            products = disp_ref[pl.ds(at, count), :] * gdisp[pl.ds(place(at), count), :]
            return inner + fold_rows(products)

        inner = over_rows(t * tile, (t + 1) * tile, inner, dispatch_inner)
    inner = jnp.sum(inner, axis=0, keepdims=True)
    for t in range(5):
        rows = pl.ds(t * tile, tile)
        here = pl.ds(place(t * tile), tile)
        gcomb[here, :] = mm_nt(gy_ref[rows, :], result)
        if not kept:
            gdisp[here, :] = mm_nt(h2_ref[rows, :], gslots)

        def logit_grads(at, count, carry):
            rows, here = pl.ds(at, count), pl.ds(place(at), count)
            combine = comb_ref[rows, :]
            weighted = combine * gcomb[here, :]
            glog[rows, :] = (
                weighted
                - combine * jnp.sum(weighted, axis=-1, keepdims=True)
                + disp_ref[rows, :] * (gdisp[here, :] - inner)
            ).astype(BF16)
            return carry

        over_rows(t * tile, (t + 1) * tile, 0, logit_grads)
    for t in range(5):
        rows = pl.ds(t * tile, tile)
        gx1[rows, :] = mm(disp_ref[rows, :].astype(BF16), gslots) + mm(glog[rows, :], phi)

    def second_norm(at, count, carry):
        gain, bias = carry
        rows = pl.ds(at, count)
        grad_h2 = gx1[rows, :]
        normal, inverse = normal_two[rows, :], thrice(inverse_two[rows, :])
        grad_x1 = gy_ref[rows, :].astype(F32) + norm_back(grad_h2, normal, inverse, norms[2:3])
        gx1[rows, :] = grad_x1
        branch[rows, :] = grad_x1.astype(BF16)
        return gain + fold_rows(grad_h2 * normal), bias + fold_rows(grad_h2)

    zero = jnp.zeros((8, D), F32)
    gain_two, bias_two = over_rows(0, tokens, (zero, zero), second_norm)
    w_o = w_ref[:, 3 * D :]
    for t in range(5):
        rows = pl.ds(t * tile, tile)
        grad_o = mm_nt(branch[rows, :], w_o).astype(BF16)
        for c in range(PAIRS):
            go[c, rows, :] = grad_o[:, c * 128 : (c + 1) * 128]

    small_rows = gw_ref.shape[2] - 6 * GROUP_ROWS
    row = lax.broadcasted_iota(jnp.int32, (columns, small_rows), 0)
    column = lax.broadcasted_iota(jnp.int32, (columns, small_rows), 1)
    fold = jnp.where(column == row // SLOT_ROWS, 1.0, 0.0).astype(BF16)
    folded = mm(glog[...], fold).astype(BF16)
    gw_ref[0, :, 6 * GROUP_ROWS :, :] = pack_turned(mm_tn(folded, h2_ref[...]))

    def put(side, part, value):
        for g in range(3):
            place = (2 * g + part) * GROUP_ROWS
            gw_ref[side, :, place : place + GROUP_ROWS, :] = value[
                :, g * 128 : (g + 1) * 128
            ].reshape(GROUPS, GROUP_ROWS, 128)

    put(1, 1, mm_tn(o_ref[0:tokens, :], branch[...]))

    gqkv[...] = jnp.zeros_like(gqkv)
    go[:, tokens:, :] = jnp.zeros((PAIRS, WINDOW_PAD, 128), BF16)
    low_lane = lax.broadcasted_iota(jnp.int32, (1, 128), 1) < HEAD_DIM

    head_row = lax.broadcasted_iota(jnp.int32, (8, 128), 0)
    head_lane = lax.broadcasted_iota(jnp.int32, (8, 128), 1)
    heads = jnp.where(head_row == head_lane // HEAD_DIM, 1.0, 0.0).astype(BF16)

    def attend(first, shift, full, window):
        span = round_up(window, 128)
        inside = rows_inside(shift, full, 0, window)
        queries_inside = columns_inside(shift, full, span)
        rows = pl.ds(first, window)
        wide = pl.ds(first, span)
        sums[:, :span] = jnp.transpose(lse_ref[wide, :])

        def score(n):
            p, h = divmod(n, 2)
            mine = low_lane if h == 0 else jnp.logical_not(low_lane)
            keys = jnp.where(mine, qkv_ref[PAIRS + p, rows, :].astype(F32) * SCORE_SCALE, 0.0)
            values = jnp.where(mine, qkv_ref[2 * PAIRS + p, rows, :].astype(F32), 0.0)
            scores[h, :window, :span] = mm_nt(keys.astype(BF16), qkv_ref[p, wide, :])
            grad_probs[h, :window, :span] = mm_nt(values.astype(BF16), go[p, wide, :])

        def split(values):
            low = values.astype(F32)
            halves = (jnp.where(low_lane, low, 0.0), jnp.where(low_lane, 0.0, low))
            return jnp.concatenate(halves, axis=0).astype(BF16)

        def finish(p):
            slopes = [grad_scores[(2 * p + g) % 4, :window, :span] for g in range(2)]
            weights = [probs[(2 * p + g) % 4, :window, :span] for g in range(2)]
            keys = split(qkv_ref[PAIRS + p, rows, :])
            news = (
                jnp.transpose(mm_tn(keys, jnp.concatenate(slopes, axis=0)))[:window] * SCORE_SCALE,
                mm(jnp.concatenate(slopes, axis=1), split(qkv_ref[p, wide, :])) * SCORE_SCALE,
                mm(jnp.concatenate(weights, axis=1), split(go[p, wide, :])),
            )
            for c in range(3):
                old = gqkv[c * PAIRS + p, rows, :].astype(F32)
                gqkv[c * PAIRS + p, rows, :] = jnp.where(inside, news[c], old).astype(BF16)

        score(0)
        for n in range(HEADS):
            p, h = divmod(n, 2)
            if n + 1 < HEADS:
                score(n + 1)
            if h == 0:
                lanes = slice(p * 128, (p + 1) * 128)
                product = go[p, wide, :].astype(F32) * o_ref[wide, lanes].astype(F32)
                upper = product.astype(BF16)
                lower = (product - upper.astype(F32)).astype(BF16)
                inner_rows = mm_nt(heads, upper) + mm_nt(heads, lower)
            logs = jnp.where(queries_inside, sums[n : n + 1, :span], 1e30)
            inner_row = inner_rows[h : h + 1]
            for r in range(0, window, 16):
                part = jnp.exp(scores[h, r : r + 16, :span] - logs)
                if r == 0 or r + 16 > full:
                    part = jnp.where(rows_inside(shift, full, r, 16), part, 0.0)
                probs[n % 4, r : r + 16, :span] = part.astype(BF16)
                slope = part * (grad_probs[h, r : r + 16, :span] - inner_row)
                grad_scores[n % 4, r : r + 16, :span] = slope.astype(BF16)
            if n in (2, 4):
                finish(n // 2 - 1)
        finish(PAIRS - 1)

    over_images(len_ref, tokens, attend)

    w_qkv = w_ref[:, : 3 * D]
    sums_one = (zero, zero)
    for t in range(5):
        rows = pl.ds(t * tile, tile)
        grad_qkv = jnp.concatenate([gqkv[c, rows, :] for c in range(9)], axis=1)
        wide_rows[pl.ds(place(t * tile), tile), :] = mm_nt(grad_qkv, w_qkv)

        def first_norm(at, count, carry):
            gain, bias = carry
            rows = pl.ds(at, count)
            grad_h1 = wide_rows[pl.ds(place(at), count), :]
            normal, inverse = normal_one[rows, :], thrice(inverse_one[rows, :])
            grad_x = gx1[rows, :] + norm_back(grad_h1, normal, inverse, norms[0:1])
            input_ref[rows, :] = grad_x.astype(BF16)
            return gain + fold_rows(grad_h1 * normal), bias + fold_rows(grad_h1)

        sums_one = over_rows(t * tile, (t + 1) * tile, sums_one, first_norm)
    gain_one, bias_one = sums_one
    grad = mm_tn(h1_all[...], jnp.concatenate([gqkv[c] for c in range(9)], axis=1))
    for c, (side, part) in enumerate(((0, 0), (0, 1), (1, 0))):
        put(side, part, grad[:, c * D : (c + 1) * D])
    zeros = jnp.zeros((small_rows - 4, D), F32)
    turned = [jnp.sum(one, axis=0, keepdims=True) for one in (gain_one, bias_one, gain_two, bias_two)]
    turned = jnp.concatenate(turned + [zeros], axis=0)
    gw_ref[1, :, 6 * GROUP_ROWS :, :] = pack_turned(turned)


def backward_local(lengths, first_norm, saved, result, gslots, block, experts):
    tokens = first_norm[0].shape[0]
    columns = experts * SLOT_ROWS
    kept = tokens if experts <= 16 else tokens // 5
    shape = jax.ShapeDtypeStruct
    return pl.pallas_call(
        functools.partial(backward_kernel, experts),
        out_shape=(
            shape((tokens, D), BF16),
            shape((2, GROUPS) + block, F32),
        ),
        in_specs=[pl.BlockSpec(memory_space=pltpu.SMEM)] + whole(17),
        out_specs=tuple(whole(2)),
        scratch_shapes=[
            pltpu.VMEM((kept, columns), F32),
            pltpu.VMEM((tokens, columns), BF16),
            pltpu.VMEM((tokens, D), F32),
            pltpu.VMEM((tokens, D), BF16),
            pltpu.VMEM((PAIRS, tokens + WINDOW_PAD, 128), BF16),
            pltpu.VMEM((9, tokens, 128), BF16),
            pltpu.VMEM((2, LONG_WINDOW, LONG_SPAN), F32),
            pltpu.VMEM((2, LONG_WINDOW, LONG_SPAN), F32),
            pltpu.VMEM((4, LONG_WINDOW, LONG_SPAN), BF16),
            pltpu.VMEM((4, LONG_WINDOW, LONG_SPAN), BF16),
            pltpu.VMEM((128, LONG_SPAN), F32),
            pltpu.VMEM((kept, columns), F32),
            pltpu.VMEM((kept, D), F32),
        ],
        compiler_params=pltpu.CompilerParams(vmem_limit_bytes=vmem_bytes(experts, 28)),
        name="backward_local",
    )(lengths, *first_norm, *saved, result, gslots)


def reduce_kernel(experts, gw_ref, square_ref, x1_ref, comb_ref, result_ref, attn_out, phi_out, norm_out, total_ref, block_ref, own, pair_in,
                  box_one, in_one, box_two, in_two, box_z, in_z, final, scalars, load_sem, sent,
                  pair_recv, recv_one, recv_two, recv_z, swap_sem, norm_recv):
    core, chip, first, second = ring(experts)
    rows = attn_out.shape[0]
    layers = experts // 4
    layer = chip // 4
    column = lax.rem(chip, 4)
    barrier = pltpu.get_barrier_semaphore()

    @pl.loop(1, experts)
    def _(j):
        peer = lax.rem(chip + j, experts)
        pl.semaphore_signal(barrier, inc=1, device_id=(core, peer), device_id_type=MESH)

    pl.semaphore_signal(barrier, inc=1, device_id=(1 - core, chip), device_id_type=MESH)
    load = pltpu.make_async_copy(gw_ref.at[core], own, load_sem.at[0])
    load.start()
    pl.semaphore_wait(barrier, experts)

    def send(source, target, send_sem, recv_sem, device):
        return pltpu.make_async_remote_copy(
            src_ref=source,
            dst_ref=target,
            send_sem=send_sem,
            recv_sem=recv_sem,
            device_id=device,
            device_id_type=MESH,
        )

    def pair_copy(place):
        return send(
            gw_ref.at[1 - core, :, place],
            pair_in.at[:, place],
            sent.at[0],
            pair_recv.at[place],
            (1 - core, chip),
        )

    def to_first(index):
        return send(box_one.at[index], in_one.at[index], sent.at[1], recv_one.at[index], (core, first))

    def to_second(index):
        return send(box_two.at[index], in_two.at[index], sent.at[2], recv_two.at[index], (core, second))

    def layer_at(d):
        return lax.rem(layer + 1 + d, layers)

    far = 3 - column

    both, one, two = far, lax.rem(first, 4), lax.rem(second, 4)

    for place in (both, two, one, column):
        pair_copy(place).start()

    load.wait()

    for batch, place in ((0, both), (1, one)):
        pair_copy(place).wait_recv()

        @pl.loop(0, layers)
        def _(d):
            index = batch * layers + layer_at(d)
            total = own[layer_at(d), place] + pair_in[layer_at(d), place]
            box_one[index] = total.astype(BF16)
            to_first(index).start()

    tile = x1_ref.shape[0] // 5
    for t in range(5):
        part = pl.ds(t * tile, tile)
        mixed = mm(comb_ref[part, :].astype(BF16), result_ref[...])
        block_ref[part, :] = (x1_ref[part, :] + mixed).astype(BF16)
    pair_copy(two).wait_recv()

    @pl.loop(0, layers)
    def _(d):
        index = layer_at(d)
        total = own[index, two] + pair_in[index, two]
        to_first(index).wait_recv()
        box_two[index] = (total + in_one[index].astype(F32)).astype(BF16)
        to_second(index).start()

    pair_copy(column).wait_recv()

    def to_layer(index):
        return send(
            box_z.at[index], in_z.at[layer], sent.at[3], recv_z.at[layer], (core, index * 4 + column)
        )

    def column_sum(index):
        total = own[index, column] + pair_in[index, column]
        to_first(layers + index).wait_recv()
        total = total + in_one[layers + index].astype(F32)
        to_second(index).wait_recv()
        return total + in_two[index].astype(F32)

    @pl.loop(0, layers - 1)
    def _(d):
        index = layer_at(d)
        box_z[index] = column_sum(index).astype(BF16)
        to_layer(index).start()

    final[core] = column_sum(layer)

    @pl.loop(1, layers)
    def _(d):
        index = lax.rem(layer - d + layers, layers)
        send(
            box_z.at[index], in_z.at[index], sent.at[3], recv_z.at[index], (core, index * 4 + column)
        ).wait_recv()
        final[core] += in_z[index].astype(F32)

    def swap(side):
        return send(final.at[side], final.at[side], swap_sem.at[0], swap_sem.at[1], (1 - core, chip))

    mine = final[core]
    swap(core).start()

    scalars[experts + core] = square_ref[...] + jnp.sum(mine * mine, axis=0, keepdims=True)

    def norm_pair(side):
        mine = scalars.at[experts + side]
        return send(mine, mine, swap_sem.at[2], swap_sem.at[3], (1 - core, chip))

    norm_pair(core).start()
    norm_pair(1 - core).wait_recv()
    scalars[chip] = scalars[experts] + scalars[experts + 1]

    @pl.loop(1, experts)
    def _(j):
        mine = scalars.at[chip]
        send(mine, mine, sent.at[4], norm_recv.at[0], (core, lax.rem(chip + j, experts))).start()

    swap(1 - core).wait_recv()
    for side in range(2):
        for part in range(2):
            for g in range(3):
                lanes = (side * 2 + part) * D + g * 128
                place = (2 * g + part) * rows
                attn_out[:, lanes : lanes + 128] = final[side, place : place + rows, :]
    phi_out[...] = final[0, 6 * rows : 6 * rows + experts, 0:rows]
    norm_out[...] = final[1, 6 * rows : 6 * rows + 4, 0:rows]

    others = scalars.at[pl.ds(0, experts - 1)]
    norms = send(others, others, sent.at[4], norm_recv.at[0], (1 - core, chip))
    norms.wait_recv()
    lanes = jnp.sum(scalars[0:experts], axis=0)
    total = jnp.sqrt(jnp.sum(lanes, axis=-1, keepdims=True))
    total_ref[...] = jnp.broadcast_to(total, (1, 128))
    swap(core).wait_send()
    norm_pair(core).wait_send()

    for source, sem in (
        (gw_ref.at[1 - core], 0),
        (box_one, 1),
        (box_two, 2),
        (box_z.at[pl.ds(0, layers - 1)], 3),
    ):
        send(source, source, sent.at[sem], sent.at[sem], (1 - core, chip)).wait_send()
    norms.wait_send()


def reduce_grads(grads, squares, x1, combine, result, experts):
    rows = D // experts
    layers = experts // 4
    block = grads.shape[2:]
    shape = jax.ShapeDtypeStruct
    dma = pltpu.SemaphoreType.DMA
    return pl.pallas_call(
        functools.partial(reduce_kernel, experts),
        out_shape=(
            shape((rows, 4 * D), F32),
            shape((experts, rows), F32),
            shape((4, rows), F32),
            shape((1, 128), F32),
            shape(x1.shape, BF16),
        ),
        in_specs=[pl.BlockSpec(memory_space=pl.ANY)] + whole(4),
        out_specs=tuple(whole(5)),
        scratch_shapes=[
            pltpu.VMEM((layers, 4) + block, F32),
            pltpu.VMEM((layers, 4) + block, F32),
            pltpu.VMEM((2 * layers,) + block, BF16),
            pltpu.VMEM((2 * layers,) + block, BF16),
            pltpu.VMEM((layers,) + block, BF16),
            pltpu.VMEM((layers,) + block, BF16),
            pltpu.VMEM((layers,) + block, BF16),
            pltpu.VMEM((layers,) + block, BF16),
            pltpu.VMEM((2,) + block, F32),
            pltpu.VMEM((experts + 2, 1, 128), F32),
            dma((1,)),
            dma((5,)),
            dma((4,)),
            dma((2 * layers,)),
            dma((layers,)),
            dma((layers,)),
            dma((4,)),
            dma((1,)),
        ],
        compiler_params=pltpu.CompilerParams(
            collective_id=2, has_side_effects=True, vmem_limit_bytes=vmem_bytes(experts, 16)
        ),
        name="reduce_grads",
    )(grads.reshape((2, layers, 4) + block), squares, x1, combine, result)


def adam_update(weight, first_moment, second_moment, gradient, factor, learning_rate, decay_rate):
    clipped = gradient * factor
    first_new = BETA_FIRST * first_moment + (1.0 - BETA_FIRST) * clipped
    second_new = BETA_SECOND * second_moment + (1.0 - BETA_SECOND) * clipped * clipped
    step_rate = learning_rate / (1.0 - BETA_FIRST**STEP)
    root = jnp.sqrt(second_new * (1.0 / (1.0 - BETA_SECOND**STEP)))
    weight_new = weight * (1.0 - learning_rate * decay_rate) - step_rate * (
        first_new / (root + ADAM_EPS)
    )
    return (weight_new, first_new, second_new)


RATES = (
    (1.0 / math.sqrt(D), WEIGHT_DECAY),
    (0.25 / math.sqrt(D), WEIGHT_DECAY),
    (0.8, 0.0),
    (4.0 / math.sqrt(D), WEIGHT_DECAY),
    (8.0 / math.sqrt(FF), WEIGHT_DECAY),
)
UPDATE_STEPS = 4


def update_kernel(block_ref, norm_ref, *refs):
    inputs, block_out, outputs, news, sems = refs[:20], refs[20], refs[21:36], refs[36:51], refs[51]
    grad_norm = norm_ref[...]
    factor = (CLIP_NORM / jnp.maximum(grad_norm, CLIP_NORM))[0:1, 0:1]
    copies = []

    def start(source, target):
        copies.append(pltpu.make_async_copy(source, target, sems.at[len(copies)]))
        copies[-1].start()

    for t in range(UPDATE_STEPS):
        for k in (3, 4):
            rate, decay = RATES[k]
            rows = inputs[4 * k].shape[1] // UPDATE_STEPS
            part = (0, pl.ds(t * rows, rows))
            weight, first, second, grad = (ref[part] for ref in inputs[4 * k : 4 * k + 4])
            made = adam_update(weight, first, second, grad, factor, rate, decay)
            for c in range(3):
                news[3 * k + c][part] = made[c]
                start(news[3 * k + c].at[part], outputs[3 * k + c].at[part])
        if t == 0:
            start(block_ref, block_out)
    for k in range(3):
        rate, decay = RATES[k]
        weight, first, second, grad = (ref[...] for ref in inputs[4 * k : 4 * k + 4])
        made = adam_update(weight, first, second, grad, factor, rate, decay)
        for c in range(3):
            news[3 * k + c][...] = made[c]
            start(news[3 * k + c], outputs[3 * k + c])
    for copy in copies:
        copy.wait()


def update(block_output, norm_tile, groups):
    shapes = [group[0].shape for group in groups for _ in range(3)]
    block_shape = jax.ShapeDtypeStruct(block_output.shape, BF16)
    return pl.pallas_call(
        update_kernel,
        out_shape=(block_shape,) + tuple(jax.ShapeDtypeStruct(shape, F32) for shape in shapes),
        in_specs=whole(22),
        out_specs=(pl.BlockSpec(memory_space=pl.ANY),) * 16,
        scratch_shapes=[pltpu.VMEM(shape, F32) for shape in shapes]
        + [pltpu.SemaphoreType.DMA((10 + 6 * UPDATE_STEPS,))],
        compiler_params=pltpu.CompilerParams(vmem_limit_bytes=24 * 1024 * 1024),
        name="update",
    )(block_output, norm_tile, *[array for group in groups for array in group])


def in_hbm(array):
    return pltpu.with_memory_space_constraint(array, pltpu.HBM)


def pad_to(array, shape):
    return jnp.pad(array, [(0, full - size) for size, full in zip(array.shape, shape)])


def regroup_weights(blocks, experts):
    rows = D // experts
    if rows == GROUP_ROWS:
        return blocks
    main = blocks[:, :, : 6 * rows].reshape(experts, 2, 3, 2, rows, 128).transpose(1, 2, 3, 0, 4, 5)
    main = main.reshape(2, 3, 2, GROUPS, GROUP_ROWS, 128).transpose(3, 0, 1, 2, 4, 5)
    main = main.reshape(GROUPS, 2, 6 * GROUP_ROWS, 128)
    small_rows = max(experts, 16)
    small = blocks[:, :, 6 * rows :, :rows]
    small = pad_to(small[:, :, :small_rows], (experts, 2, small_rows, rows))
    small = small.transpose(1, 2, 0, 3).reshape(2, small_rows, GROUPS, GROUP_ROWS)
    small = pad_to(small.transpose(2, 0, 1, 3), (GROUPS, 2, small_rows, 128))
    return jnp.concatenate([main, small], axis=2)


def regroup_grads(groups, experts):
    rows = D // experts
    if rows == GROUP_ROWS:
        return groups
    main = groups[:, :, : 6 * GROUP_ROWS].reshape(2, GROUPS, 3, 2, GROUP_ROWS, 128)
    main = main.transpose(0, 2, 3, 1, 4, 5).reshape(2, 3, 2, experts, rows, 128)
    main = main.transpose(0, 3, 1, 2, 4, 5).reshape(2, experts, 6 * rows, 128)
    small = groups[:, :, 6 * GROUP_ROWS :, :GROUP_ROWS]
    small_rows = min(small.shape[2], block_rows(experts) - 6 * rows)
    small = small[:, :, :small_rows].transpose(0, 2, 1, 3).reshape(2, small_rows, experts, rows)
    small = pad_to(small.transpose(0, 2, 1, 3), (2, experts, small_rows, 128))
    both = jnp.concatenate([main, small], axis=2)
    return pad_to(both, (2, experts, block_rows(experts), 128))


def local(
    patches,
    slot_len,
    attn_weight,
    attn_first,
    attn_second,
    phi_weight,
    phi_first,
    phi_second,
    norm_params,
    norm_first,
    norm_second,
    expert_in,
    in_first,
    in_second,
    expert_out,
    out_first,
    out_second,
    cotangent,
):
    experts = lax.axis_size("expert")
    weights, *first_norm = gather_weights(
        in_hbm(attn_weight), in_hbm(phi_weight.T), in_hbm(norm_params), in_hbm(patches), experts
    )
    weights = regroup_weights(weights, experts)
    *saved, packed = forward_local(
        slot_len, patches, weights, first_norm[0], in_hbm(cotangent), experts
    )
    x1, combine = saved.pop(9), saved[11]
    result, gslots, grad_in, grad_out, squares = run_experts(packed, expert_in, expert_out, experts)
    input_grad, grads = backward_local(
        slot_len, first_norm, saved, result, gslots, weights.shape[2:], experts
    )
    grads = regroup_grads(grads, experts)
    attn_part, phi_part, norm_part, norm_tile, block_output = reduce_grads(
        grads, squares, x1, combine, result, experts
    )
    block_output, *news = update(
        block_output,
        norm_tile,
        (
            (attn_weight, attn_first, attn_second, attn_part),
            (phi_weight.T, phi_first.T, phi_second.T, phi_part),
            (norm_params, norm_first, norm_second, norm_part),
            (expert_in, in_first, in_second, grad_in),
            (expert_out, out_first, out_second, grad_out),
        ),
    )
    attn_new, attn_first_new, attn_second_new = news[0:3]
    phi_new, phi_first_new, phi_second_new = (new.T for new in news[3:6])
    norm_new, norm_first_new, norm_second_new = news[6:9]
    in_new, in_first_new, in_second_new = news[9:12]
    out_new, out_first_new, out_second_new = news[12:15]
    grad_norm = norm_tile[0, 0]
    return (
        block_output,
        input_grad,
        grad_norm,
        attn_new,
        attn_first_new,
        attn_second_new,
        phi_new,
        phi_first_new,
        phi_second_new,
        norm_new,
        norm_first_new,
        norm_second_new,
        in_new,
        in_first_new,
        in_second_new,
        out_new,
        out_first_new,
        out_second_new,
    )


def solution(mesh):
    in_specs = (
        P(("batch", "expert"), None),
        P(("batch", "expert"), None),
        P("expert", None),
        P("expert", None),
        P("expert", None),
        P("expert", None),
        P("expert", None),
        P("expert", None),
        P(None, "expert"),
        P(None, "expert"),
        P(None, "expert"),
        P("expert", None, "batch"),
        P("expert", None, "batch"),
        P("expert", None, "batch"),
        P("expert", "batch", None),
        P("expert", "batch", None),
        P("expert", "batch", None),
        P(("batch", "expert"), None),
    )
    out_specs = (
        P(("batch", "expert"), None),
        P(("batch", "expert"), None),
        P(),
        P("expert", None),
        P("expert", None),
        P("expert", None),
        P("expert", None),
        P("expert", None),
        P("expert", None),
        P(None, "expert"),
        P(None, "expert"),
        P(None, "expert"),
        P("expert", None, "batch"),
        P("expert", None, "batch"),
        P("expert", None, "batch"),
        P("expert", "batch", None),
        P("expert", "batch", None),
        P("expert", "batch", None),
    )
    return jax.shard_map(local, mesh=mesh, in_specs=in_specs, out_specs=out_specs, check_vma=False)
```

```python
import functools
import math

import jax
import jax.numpy as jnp
from jax import lax
from jax.experimental import pallas as pl
from jax.experimental.pallas import tpu as pltpu
from jax.sharding import PartitionSpec as P

D = 384
HEADS = 6
HEAD_DIM = 64
FF = 1536
STEP = 3
SHORT_LEN = 196
LONG_LEN = 576
IMAGES = 5
SLOT_ROWS = 8
PAIRS = 3
GROUPS = 16
GROUP_ROWS = D // GROUPS
CHUNK = 112
LONG_WINDOW = 592
LONG_SPAN = 640
WINDOW_PAD = 48

NORM_EPS = 1e-06
CLIP_NORM = 1.0
BETA_FIRST = 0.5
BETA_SECOND = 0.5
ADAM_EPS = 1e-08
WEIGHT_DECAY = 0.05
MASKED = -1e30
SCORE_SCALE = HEAD_DIM ** (-0.5)

MESH = pl.DeviceIdType.MESH
F32 = jnp.float32
BF16 = jnp.bfloat16


def vmem_bytes(experts, mebibytes):
    return (mebibytes if experts <= 16 else 60) * 1024 * 1024


def whole(count):
    return [pl.BlockSpec(memory_space=pltpu.VMEM)] * count


def round_up(value, unit):
    return -(-value // unit) * unit


def mm(left, right):
    return jnp.dot(left, right, preferred_element_type=F32)


def mm_nt(left, right):
    return lax.dot_general(left, right, (((1,), (1,)), ((), ())), preferred_element_type=F32)


def mm_tn(left, right):
    return lax.dot_general(left, right, (((0,), (0,)), ((), ())), preferred_element_type=F32)


def block_rows(experts):
    rows = D // experts
    return round_up(6 * rows + max(experts, 4), 16)


def ring(experts):
    core = lax.axis_index("batch")
    chip = lax.axis_index("expert")
    first = chip ^ (1 + core)
    second = chip ^ (2 - core)
    return core, chip, first, second


def gather_kernel(experts, attn_hbm, phi_hbm, norm_hbm, patch_hbm, out, normal_ref, inverse_ref, patch_ref, stage, attn_ref, phi_ref, norm_ref, load_sem,
                  sent, recv):
    core, chip, first, second = ring(experts)
    rows = attn_ref.shape[0]
    half = pl.multiple_of(core * (2 * D), 128)
    loads = [
        pltpu.make_async_copy(attn_hbm.at[:, pl.ds(half, 2 * D)], attn_ref, load_sem.at[0]),
        pltpu.make_async_copy(phi_hbm, phi_ref, load_sem.at[1]),
        pltpu.make_async_copy(norm_hbm, norm_ref, load_sem.at[2]),
    ]
    for load in loads:
        load.start()
    load_patches = pltpu.make_async_copy(patch_hbm, patch_ref, load_sem.at[3])
    load_patches.start()
    column = lax.rem(chip, 4)
    layers = experts // 4
    layer = chip // 4
    barrier = pltpu.get_barrier_semaphore()

    @pl.loop(1, layers)
    def _(d):
        peer = lax.rem(layer + d, layers) * 4 + column
        pl.semaphore_signal(barrier, inc=1, device_id=(core, peer), device_id_type=MESH)

    pl.semaphore_signal(barrier, inc=1, device_id=(core, first), device_id_type=MESH)
    pl.semaphore_signal(barrier, inc=1, device_id=(core, second), device_id_type=MESH)
    pl.semaphore_signal(barrier, inc=1, device_id=(1 - core, chip), device_id_type=MESH)
    stage[...] = jnp.zeros_like(stage)
    for load in loads:
        load.wait()
    for part in range(2):
        for g in range(3):
            lanes = part * D + g * 128
            place = (2 * g + part) * rows
            stage[place : place + rows, :] = attn_ref[:, lanes : lanes + 128]

    @pl.when(core == 0)
    def _():
        stage[6 * rows : 6 * rows + experts, 0:rows] = phi_ref[...]

    @pl.when(core == 1)
    def _():
        stage[6 * rows : 6 * rows + 4, 0:rows] = norm_ref[...]

    out[chip, core] = stage[...].astype(BF16)
    pl.semaphore_wait(barrier, layers + 2)

    def copy(source, target, send_sem, recv_sem, device):
        return pltpu.make_async_remote_copy(
            src_ref=source,
            dst_ref=target,
            send_sem=send_sem,
            recv_sem=recv_sem,
            device_id=device,
            device_id_type=MESH,
        )

    def along(block, peer):
        mine = out.at[block, core]
        return copy(mine, mine, sent.at[0], recv.at[block], (core, peer))

    def to_pair(block):
        mine = out.at[block, core]
        return copy(mine, mine, sent.at[1], sent.at[2], (1 - core, chip))

    @pl.loop(1, layers)
    def _(d):
        along(chip, lax.rem(layer + d, layers) * 4 + column).start()

    along(chip, first).start()
    along(chip, second).start()
    to_pair(chip).start()

    load_patches.wait()

    def statistics(at, count, carry):
        rows = pl.ds(at, count)
        normal, inverse = normed(patch_ref[rows, :].astype(F32))
        normal_ref[rows, :] = normal
        inverse_ref[rows, :] = jnp.broadcast_to(inverse, (count, 128))
        return carry

    over_rows(0, patch_ref.shape[0], 0, statistics)

    @pl.loop(1, layers)
    def _(d):
        block = lax.rem(layer - d + layers, layers) * 4 + column
        along(block, first).wait_recv()
        along(block, first).start()
        along(block, second).start()
        to_pair(block).start()

    @pl.loop(0, layers)
    def _(d):
        block = lax.rem(layer - d + layers, layers) * 4 + lax.rem(first, 4)
        along(block, first).wait_recv()
        along(block, second).start()
        to_pair(block).start()

    @pl.loop(0, 2 * layers)
    def _(d):
        other = jnp.where(lax.rem(d, 2) == 0, lax.rem(second, 4), lax.rem(3 - column, 4))
        block = lax.rem(layer - d // 2 + layers, layers) * 4 + other
        along(block, first).wait_recv()
        to_pair(block).start()

    sides = out.at[pl.ds(0, experts - 1), core]
    copy(sides, sides, sent.at[0], sent.at[0], (1 - core, chip)).wait_send()
    copy(out.at[:, core], out.at[:, 1 - core], sent.at[1], sent.at[2], (1 - core, chip)).wait()


def gather_weights(attn_weight, phi_turned, norm_params, patches, experts):
    rows = block_rows(experts)
    tokens = patches.shape[0]
    dma = pltpu.SemaphoreType.DMA
    return pl.pallas_call(
        functools.partial(gather_kernel, experts),
        out_shape=(
            jax.ShapeDtypeStruct((experts, 2, rows, 128), BF16),
            jax.ShapeDtypeStruct((tokens, D), F32),
            jax.ShapeDtypeStruct((tokens, 128), F32),
        ),
        in_specs=[pl.BlockSpec(memory_space=pltpu.HBM)] * 4,
        out_specs=tuple(whole(3)),
        scratch_shapes=[
            pltpu.VMEM((tokens, D), BF16),
            pltpu.VMEM((rows, 128), F32),
            pltpu.VMEM((attn_weight.shape[0], 2 * D), F32),
            pltpu.VMEM(phi_turned.shape, F32),
            pltpu.VMEM(norm_params.shape, F32),
            dma((4,)),
            dma((3,)),
            dma((experts,)),
        ],
        compiler_params=pltpu.CompilerParams(
            collective_id=0, has_side_effects=True, vmem_limit_bytes=vmem_bytes(experts, 10)
        ),
        name="gather_weights",
    )(attn_weight, phi_turned, norm_params, patches)


def unpack_weight(main_ref, side, part):
    blocks = main_ref[:, side].astype(F32)
    columns = []
    for g in range(3):
        place = (2 * g + part) * GROUP_ROWS
        columns.append(blocks[:, place : place + GROUP_ROWS, :].reshape(D, 128))
    return jnp.concatenate(columns, axis=1).astype(BF16)


def group_lanes():
    lane = lax.broadcasted_iota(jnp.int32, (128, D), 0)
    column = lax.broadcasted_iota(jnp.int32, (128, D), 1)
    return jnp.where(column % GROUP_ROWS == lane, 1.0, 0.0).astype(BF16)


def unpack_turned(main_ref, side, rows):
    first = 6 * GROUP_ROWS
    blocks = main_ref[:, side].astype(F32)[:, first : first + rows, :]
    spread = mm(blocks.reshape(GROUPS * rows, 128).astype(BF16), group_lanes())
    spread = spread.reshape(GROUPS, rows, D)
    group = lax.broadcasted_iota(jnp.int32, (GROUPS, 1, D), 0)
    column = lax.broadcasted_iota(jnp.int32, (GROUPS, 1, D), 2)
    return jnp.sum(jnp.where(column // GROUP_ROWS == group, spread, 0.0), axis=0)


def pack_turned(values):
    rows = values.shape[0]
    group = lax.broadcasted_iota(jnp.int32, (GROUPS, 1, D), 0)
    column = lax.broadcasted_iota(jnp.int32, (GROUPS, 1, D), 2)
    spread = jnp.where(column // GROUP_ROWS == group, values[None], 0.0)
    spread = spread.reshape(GROUPS * rows, D).astype(BF16)
    return mm_nt(spread, group_lanes()).reshape(GROUPS, rows, 128)


def unpack_small(main_ref, experts):
    turned = unpack_turned(main_ref, 0, max(experts, 16)).astype(BF16)
    row = lax.broadcasted_iota(jnp.int32, (experts * SLOT_ROWS, turned.shape[0]), 0)
    column = lax.broadcasted_iota(jnp.int32, (experts * SLOT_ROWS, turned.shape[0]), 1)
    spread = jnp.where(column == row // SLOT_ROWS, 1.0, 0.0).astype(BF16)
    return mm(spread, turned).astype(BF16), unpack_turned(main_ref, 1, 8)


def slot_bounds(len_ref, columns):
    image = lax.broadcasted_iota(jnp.int32, (1, columns), 1) % SLOT_ROWS
    starts = jnp.zeros((1, columns), jnp.int32)
    ends = jnp.zeros((1, columns), jnp.int32)
    start = jnp.int32(0)
    for k in range(IMAGES):
        end = start + len_ref[0, k]
        starts = jnp.where(image == k, start, starts)
        ends = jnp.where(image == k, end, ends)
        start = end
    return starts, ends, start


def normed(values):
    centred = values - jnp.mean(values, axis=-1, keepdims=True)
    variance = jnp.mean(centred * centred, axis=-1, keepdims=True)
    inverse = lax.rsqrt(variance + NORM_EPS)
    return centred * inverse, inverse


def norm_back(grad_shaped, normal, inverse, scaling):
    grad_normal = grad_shaped * scaling
    return inverse * (
        grad_normal
        - jnp.mean(grad_normal, axis=-1, keepdims=True)
        - normal * jnp.mean(grad_normal * normal, axis=-1, keepdims=True)
    )


def over_rows(start, stop, carry, body):
    for at in range(start, stop, CHUNK):
        carry = body(at, min(CHUNK, stop - at), carry)
    return carry


def thrice(values):
    return jnp.concatenate([values] * 3, axis=1)


def fold_rows(values):
    return jnp.sum(values.reshape(values.shape[0] // 8, 8, values.shape[1]), axis=0)


def over_images(len_ref, tokens, body):
    def step(k, start):
        length = len_ref[0, k]
        for full in (SHORT_LEN, LONG_LEN):

            @pl.when(length == full)
            def _():
                window = round_up(full + 12, 16)
                first = jnp.minimum((start // 16) * 16, tokens - window)
                body(pl.multiple_of(first, 16), start - first, full, window)

        return start + length

    lax.fori_loop(0, IMAGES, step, jnp.int32(0))


def rows_inside(shift, full, first, count):
    row = first + lax.broadcasted_iota(jnp.int32, (count, 1), 0)
    return (row >= shift) & (row < shift + full)


def columns_inside(shift, full, count):
    column = lax.broadcasted_iota(jnp.int32, (1, count), 1)
    return (column >= shift) & (column < shift + full)


def forward_kernel(experts, len_ref, patch_ref, main_ref, norm_ref, cot_hbm, w_ref, phi_ref, norms_ref,
                   normal_ref, inverse_ref, h1_all, qkv_ref, o_ref, lse_ref, x1_ref, h2_ref, disp_ref,
                   comb_ref, gy_ref, pack_ref, logit, packf, scores,
                   probs, peaks, cot_ref, load_sem):
    load = pltpu.make_async_copy(cot_hbm, cot_ref, load_sem.at[0])
    load.start()
    tokens = patch_ref.shape[0]
    columns = experts * SLOT_ROWS
    tile = tokens // 5
    phi, norms = unpack_small(main_ref, experts)
    starts, ends, total = slot_bounds(len_ref, columns)
    norms_ref[...] = norms
    phi_ref[...] = phi
    for k in range(4):
        w_ref[:, k * D : (k + 1) * D] = unpack_weight(main_ref, k // 2, k % 2)
    w_qkv = w_ref[:, : 3 * D]

    def first_norm(at, count, carry):
        rows = pl.ds(at, count)
        h1_all[rows, :] = (norm_ref[rows, :] * norms[0:1] + norms[1:2]).astype(BF16)
        return carry

    for t in range(5):
        over_rows(t * tile, (t + 1) * tile, 0, first_norm)
        rows = pl.ds(t * tile, tile)
        qkv = mm(h1_all[rows, :], w_qkv).astype(BF16)
        for c in range(9):
            qkv_ref[c, rows, :] = qkv[:, c * 128 : (c + 1) * 128]
    qkv_ref[:, tokens:, :] = jnp.zeros((9, WINDOW_PAD, 128), BF16)
    o_ref[...] = jnp.zeros_like(o_ref)
    lse_ref[...] = jnp.zeros_like(lse_ref)
    low_lane = lax.broadcasted_iota(jnp.int32, (1, 128), 1) < HEAD_DIM
    lane = lax.broadcasted_iota(jnp.int32, (1, 128), 1)

    def attend(first, shift, full, window):
        span = round_up(window, 128)
        bias = jnp.where(columns_inside(shift, full, span), 0.0, MASKED)
        inside = rows_inside(shift, full, 0, window)
        rows = pl.ds(first, window)
        wide = pl.ds(first, span)

        ones = jnp.ones((span, 128), BF16)

        def score(n):
            p, h = divmod(n, 2)
            mine = low_lane if h == 0 else jnp.logical_not(low_lane)
            query = jnp.where(mine, qkv_ref[p, rows, :].astype(F32) * SCORE_SCALE, 0.0)
            keys = qkv_ref[PAIRS + p, wide, :]
            scores[h, :window, :span] = mm_nt(query.astype(BF16), keys)

        score(0)
        outs = []
        for n in range(HEADS):
            p, h = divmod(n, 2)
            if n + 1 < HEADS:
                score(n + 1)
            for r in range(0, window, 16):
                part = scores[h, r : r + 16, :span] + bias
                peak = jnp.max(part, axis=-1, keepdims=True)
                probs[h, r : r + 16, :span] = jnp.exp(part - peak).astype(BF16)
                peaks[h, r : r + 16, :] = jnp.broadcast_to(peak, (16, 128))
            values = jnp.concatenate([qkv_ref[2 * PAIRS + p, wide, :], ones], axis=1)
            both = mm(probs[h, :window, :span], values)
            summed = both[:, 128:]
            outs.append(both[:, :128] * (1.0 / summed))
            logs = peaks[h, :window, :] + jnp.log(summed)
            lse_ref[rows, :] = jnp.where(inside & (lane == n), logs, lse_ref[rows, :])
            if h == 1:
                lanes = slice(p * 128, (p + 1) * 128)
                old = o_ref[rows, lanes].astype(F32)
                merged = jnp.where(inside, jnp.where(low_lane, outs[n - 1], outs[n]), old)
                o_ref[rows, lanes] = merged.astype(BF16)

    over_images(len_ref, tokens, attend)

    load.wait()
    w_o = w_ref[:, 3 * D :]
    def project(t):
        rows = pl.ds(t * tile, tile)
        x1_ref[rows, :] = mm(o_ref[rows, :], w_o)

    def second_norm(at, count, carry):
        rows = pl.ds(at, count)
        x1 = patch_ref[rows, :].astype(F32) + x1_ref[rows, :]
        normal, inverse = normed(x1)
        normal_ref[rows, :] = normal
        inverse_ref[rows, :] = jnp.broadcast_to(inverse, (count, 128))
        h2_ref[rows, :] = (normal * norms[2:3] + norms[3:4]).astype(BF16)
        valid = at + lax.broadcasted_iota(jnp.int32, (count, 1), 0) < total
        x1_ref[rows, :] = jnp.where(valid, x1, 0.0)
        gy_ref[rows, :] = jnp.where(valid, cot_ref[rows, :].astype(F32), 0.0).astype(BF16)
        return carry

    project(0)
    for t in range(5):
        if t < 4:
            project(t + 1)
        over_rows(t * tile, (t + 1) * tile, 0, second_norm)
        rows = pl.ds(t * tile, tile)
        logit[rows, :] = mm_nt(h2_ref[rows, :], phi)

    def members(at, count):
        position = at + lax.broadcasted_iota(jnp.int32, (count, columns), 0)
        return (position >= starts) & (position < ends)

    def mixing(at, count, peak):
        rows = pl.ds(at, count)
        logits = logit[rows, :]
        member = members(at, count)
        exponent = jnp.exp(logits - jnp.max(logits, axis=-1, keepdims=True))
        summed = jnp.sum(exponent, axis=-1, keepdims=True) * (1.0 / SLOT_ROWS)
        comb_ref[rows, :] = jnp.where(member, exponent * (1.0 / summed), 0.0)
        inside = jnp.where(member, logits, MASKED)
        return jnp.maximum(peak, jnp.max(inside.reshape(count // 8, 8, columns), axis=0))

    peak = over_rows(0, tokens, jnp.full((8, columns), MASKED, F32), mixing)
    present = ends > starts
    peak = jnp.where(present, jnp.max(peak, axis=0, keepdims=True), 0.0)

    def exponents(at, count, summed):
        rows = pl.ds(at, count)
        member = members(at, count)
        exponent = jnp.exp(jnp.where(member, logit[rows, :] - peak, 0.0))
        exponent = jnp.where(member, exponent, 0.0)
        disp_ref[rows, :] = exponent
        return summed + fold_rows(exponent)

    summed = over_rows(0, tokens, jnp.zeros((8, columns), F32), exponents)
    summed = jnp.sum(summed, axis=0, keepdims=True) + jnp.where(present, 0.0, 1.0)
    dispatch = disp_ref[...] * (1.0 / summed)
    disp_ref[...] = dispatch
    slots = mm_tn(dispatch.astype(BF16), h2_ref[...])
    grad_result = mm_tn(comb_ref[...].astype(BF16), gy_ref[...])
    for part, matrix in enumerate((slots, grad_result)):
        pack_rows(packf, matrix.reshape(experts, SLOT_ROWS, D))
        pack_ref[:, part * 16 : (part + 1) * 16, :] = packf[...].astype(BF16)


def pack_rows(packf, blocks):
    packf[...] = jnp.zeros_like(packf)
    for c in range(3):
        packf[:, c * IMAGES : (c + 1) * IMAGES, :] = blocks[:, :IMAGES, c * 128 : (c + 1) * 128]


def unpack_rows(packf, wide):
    wide[...] = jnp.zeros_like(wide)
    for c in range(3):
        wide[:, 0:IMAGES, c * 128 : (c + 1) * 128] = packf[:, c * IMAGES : (c + 1) * IMAGES, :]


def forward_local(lengths, patches, main, normal, cotangent, experts):
    tokens = patches.shape[0]
    columns = experts * SLOT_ROWS
    shape = jax.ShapeDtypeStruct
    return pl.pallas_call(
        functools.partial(forward_kernel, experts),
        out_shape=(
            shape((D, 4 * D), BF16),
            shape((columns, D), BF16),
            shape((8, D), F32),
            shape((tokens, D), F32),
            shape((tokens, 128), F32),
            shape((tokens, D), BF16),
            shape((9, tokens + WINDOW_PAD, 128), BF16),
            shape((tokens + WINDOW_PAD, D), BF16),
            shape((tokens + WINDOW_PAD, 128), F32),
            shape((tokens, D), F32),
            shape((tokens, D), BF16),
            shape((tokens, columns), F32),
            shape((tokens, columns), F32),
            shape((tokens, D), BF16),
            shape((experts, 32, 128), BF16),
        ),
        in_specs=[pl.BlockSpec(memory_space=pltpu.SMEM)]
        + whole(3)
        + [pl.BlockSpec(memory_space=pltpu.HBM)],
        out_specs=tuple(whole(15)),
        scratch_shapes=[
            pltpu.VMEM((tokens, columns), F32),
            pltpu.VMEM((experts, 16, 128), F32),
            pltpu.VMEM((2, LONG_WINDOW, LONG_SPAN), F32),
            pltpu.VMEM((2, LONG_WINDOW, LONG_SPAN), BF16),
            pltpu.VMEM((2, LONG_WINDOW, 128), F32),
            pltpu.VMEM((tokens, D), BF16),
            pltpu.SemaphoreType.DMA((1,)),
        ],
        compiler_params=pltpu.CompilerParams(vmem_limit_bytes=vmem_bytes(experts, 24)),
        name="forward_local",
    )(lengths, patches, main, normal, cotangent)


def expert_kernel(experts, pack_ref, in_ref, out_ref, result_ref, gslot_ref, gin_ref, gout_ref,
                  square_ref, inbox, partial, given, outbox, back, packf, packe, widee, sems):
    core = lax.axis_index("batch")
    chip = lax.axis_index("expert")
    barrier = pltpu.get_barrier_semaphore()

    @pl.loop(1, experts)
    def _(j):
        peer = lax.rem(chip + j, experts)
        pl.semaphore_signal(barrier, inc=1, device_id=(core, peer), device_id_type=MESH)

    pl.semaphore_signal(barrier, inc=1, device_id=(1 - core, chip), device_id_type=MESH)
    w_in = in_ref[0].astype(BF16)
    w_out = out_ref[0].astype(BF16)
    for part in range(2):
        inbox[part, core, chip] = pack_ref[chip, part * 16 : (part + 1) * 16, :]
    pl.semaphore_wait(barrier, experts)

    def copy(source, target, sem, device):
        return pltpu.make_async_remote_copy(
            src_ref=source,
            dst_ref=target,
            send_sem=sems.at[sem],
            recv_sem=sems.at[sem + 1],
            device_id=device,
            device_id_type=MESH,
        )

    others = pl.ds(0, experts - 1)
    firsts, pairs, halves, seconds = [], [], [], []
    for part in range(2):
        block = pl.ds(part * 16, 16)

        @pl.loop(1, experts)
        def _(j):
            peer = lax.rem(chip + j, experts)
            copy(
                pack_ref.at[peer, block], inbox.at[part, core, chip], 2 * part, (core, peer)
            ).start()

        firsts.append(
            copy(pack_ref.at[others, block], inbox.at[part, core, others], 2 * part, (core, chip))
        )
        mine = inbox.at[part, core]
        pairs.append(copy(mine, mine, 4 + 2 * part, (1 - core, chip)))
        halves.append(copy(partial.at[part], given.at[part], 8 + 2 * part, (1 - core, chip)))
        seconds.append(
            copy(outbox.at[part, others], back.at[part, others], 12 + 2 * part, (core, chip))
        )

    def spread(part, side):
        packe[...] = inbox[part, side].astype(F32)
        unpack_rows(packe, widee)
        return widee[...].reshape(experts * SLOT_ROWS, D).astype(BF16)

    root = math.sqrt(2.0 / math.pi)

    def forward(side):
        slots = spread(0, side)
        hidden = mm(slots, w_in)
        bent = jnp.tanh(root * (hidden + 0.044715 * (hidden * hidden * hidden)))
        half = 0.5 * (1.0 + bent)
        act = (hidden * half).astype(BF16)
        slope = half + 0.5 * hidden * (1.0 - bent * bent) * (
            root * (1.0 + 3.0 * 0.044715 * (hidden * hidden))
        )
        return slots, act, slope, mm(act, w_out)

    def backward(side, slope):
        grads = spread(1, side)
        grad_hidden = (mm_nt(grads, w_out) * slope).astype(BF16)
        return grads, grad_hidden, mm_nt(grad_hidden, w_in)

    def give_half(part, values):
        pack_rows(packf, values.reshape(experts, SLOT_ROWS, D))
        partial[part] = packf[...].astype(BF16)
        halves[part].start()

    def send_back(part, values):
        pack_rows(packf, values.reshape(experts, SLOT_ROWS, D))
        halves[part].wait_recv()
        outbox[part] = (packf[...] + given[part].astype(F32)).astype(BF16)

        @pl.loop(1, experts)
        def _(j):
            peer = lax.rem(chip + j, experts)
            copy(outbox.at[part, peer], back.at[part, chip], 12 + 2 * part, (core, peer)).start()

        back[part, chip] = outbox[part, chip]

    firsts[0].wait_recv()
    pairs[0].start()
    pairs[0].wait_recv()
    their_slots, their_act, their_slope, their_result = forward(1 - core)
    give_half(0, their_result)
    firsts[1].wait_recv()
    pairs[1].start()
    our_slots, our_act, our_slope, our_result = forward(core)
    send_back(0, our_result)
    pairs[1].wait_recv()
    their_grads, their_hidden, their_back = backward(1 - core, their_slope)
    give_half(1, their_back)
    our_grads, our_hidden, our_back = backward(core, our_slope)
    send_back(1, our_back)
    grad_out = mm_tn(our_act, our_grads) + mm_tn(their_act, their_grads)
    gout_ref[0] = grad_out
    grad_in = mm_tn(our_slots, our_hidden) + mm_tn(their_slots, their_hidden)
    gin_ref[0] = grad_in
    squares = jnp.zeros((1, 128), F32)
    for grad in (grad_out, grad_in):
        columns = jnp.sum(grad * grad, axis=0, keepdims=True)
        for c in range(0, grad.shape[1], 128):
            squares = squares + columns[:, c : c + 128]
    square_ref[...] = squares
    for part, target in enumerate((result_ref, gslot_ref)):
        seconds[part].wait_recv()
        packe[...] = back[part].astype(F32)
        unpack_rows(packe, widee)
        target[...] = widee[...].reshape(experts * SLOT_ROWS, D).astype(BF16)
    for sent in firsts + pairs + halves + seconds:
        sent.wait_send()


def run_experts(packed, expert_in, expert_out, experts):
    shape = jax.ShapeDtypeStruct
    return pl.pallas_call(
        functools.partial(expert_kernel, experts),
        out_shape=(
            shape((experts * SLOT_ROWS, D), BF16),
            shape((experts * SLOT_ROWS, D), BF16),
            shape(expert_in.shape, F32),
            shape(expert_out.shape, F32),
            shape((1, 128), F32),
        ),
        in_specs=whole(3),
        out_specs=tuple(whole(5)),
        scratch_shapes=[
            pltpu.VMEM((2, 2, experts, 16, 128), BF16),
            pltpu.VMEM((2, experts, 16, 128), BF16),
            pltpu.VMEM((2, experts, 16, 128), BF16),
            pltpu.VMEM((2, experts, 16, 128), BF16),
            pltpu.VMEM((2, experts, 16, 128), BF16),
            pltpu.VMEM((experts, 16, 128), F32),
            pltpu.VMEM((experts, 16, 128), F32),
            pltpu.VMEM((experts, SLOT_ROWS, D), F32),
            pltpu.SemaphoreType.DMA((16,)),
        ],
        compiler_params=pltpu.CompilerParams(
            collective_id=1, has_side_effects=True, vmem_limit_bytes=vmem_bytes(experts, 8)
        ),
        name="run_experts",
    )(packed, expert_in, expert_out)


def backward_kernel(experts, len_ref, normal_one, inverse_one, w_ref, phi_ref, norms_ref, normal_two,
                    inverse_two, h1_all, qkv_ref, o_ref, lse_ref, h2_ref, disp_ref, comb_ref, gy_ref,
                    result_ref, gslot_ref, input_ref, gw_ref, gdisp, glog, gx1, branch, go, gqkv,
                    scores, grad_probs, probs, grad_scores, sums, gcomb, wide_rows):
    tokens = h2_ref.shape[0]
    columns = experts * SLOT_ROWS
    tile = tokens // 5
    phi, norms = phi_ref[...], norms_ref[...]
    result = result_ref[...]
    gslots = gslot_ref[...]

    kept = gdisp.shape[0] == tokens

    def place(at):
        return at if kept else at % tile

    inner = jnp.zeros((8, columns), F32)
    for t in range(5):
        rows = pl.ds(t * tile, tile)
        gdisp[pl.ds(place(t * tile), tile), :] = mm_nt(h2_ref[rows, :], gslots)

        def dispatch_inner(at, count, inner):
            products = disp_ref[pl.ds(at, count), :] * gdisp[pl.ds(place(at), count), :]
            return inner + fold_rows(products)

        inner = over_rows(t * tile, (t + 1) * tile, inner, dispatch_inner)
    inner = jnp.sum(inner, axis=0, keepdims=True)
    for t in range(5):
        rows = pl.ds(t * tile, tile)
        here = pl.ds(place(t * tile), tile)
        gcomb[here, :] = mm_nt(gy_ref[rows, :], result)
        if not kept:
            gdisp[here, :] = mm_nt(h2_ref[rows, :], gslots)

        def logit_grads(at, count, carry):
            rows, here = pl.ds(at, count), pl.ds(place(at), count)
            combine = comb_ref[rows, :]
            weighted = combine * gcomb[here, :]
            glog[rows, :] = (
                weighted
                - combine * jnp.sum(weighted, axis=-1, keepdims=True)
                + disp_ref[rows, :] * (gdisp[here, :] - inner)
            ).astype(BF16)
            return carry

        over_rows(t * tile, (t + 1) * tile, 0, logit_grads)
    for t in range(5):
        rows = pl.ds(t * tile, tile)
        gx1[rows, :] = mm(disp_ref[rows, :].astype(BF16), gslots) + mm(glog[rows, :], phi)

    def second_norm(at, count, carry):
        gain, bias = carry
        rows = pl.ds(at, count)
        grad_h2 = gx1[rows, :]
        normal, inverse = normal_two[rows, :], thrice(inverse_two[rows, :])
        grad_x1 = gy_ref[rows, :].astype(F32) + norm_back(grad_h2, normal, inverse, norms[2:3])
        gx1[rows, :] = grad_x1
        branch[rows, :] = grad_x1.astype(BF16)
        return gain + fold_rows(grad_h2 * normal), bias + fold_rows(grad_h2)

    zero = jnp.zeros((8, D), F32)
    w_o = w_ref[:, 3 * D :]
    sums_two = (zero, zero)
    for t in range(5):
        sums_two = over_rows(t * tile, (t + 1) * tile, sums_two, second_norm)
        rows = pl.ds(t * tile, tile)
        grad_o = mm_nt(branch[rows, :], w_o).astype(BF16)
        for c in range(PAIRS):
            go[c, rows, :] = grad_o[:, c * 128 : (c + 1) * 128]
    gain_two, bias_two = sums_two

    small_rows = gw_ref.shape[2] - 6 * GROUP_ROWS
    row = lax.broadcasted_iota(jnp.int32, (columns, small_rows), 0)
    column = lax.broadcasted_iota(jnp.int32, (columns, small_rows), 1)
    fold = jnp.where(column == row // SLOT_ROWS, 1.0, 0.0).astype(BF16)
    folded = mm(glog[...], fold).astype(BF16)
    gw_ref[0, :, 6 * GROUP_ROWS :, :] = pack_turned(mm_tn(folded, h2_ref[...]))

    def put(side, part, value):
        for g in range(3):
            place = (2 * g + part) * GROUP_ROWS
            gw_ref[side, :, place : place + GROUP_ROWS, :] = value[
                :, g * 128 : (g + 1) * 128
            ].reshape(GROUPS, GROUP_ROWS, 128)

    put(1, 1, mm_tn(o_ref[0:tokens, :], branch[...]))

    gqkv[...] = jnp.zeros_like(gqkv)
    go[:, tokens:, :] = jnp.zeros((PAIRS, WINDOW_PAD, 128), BF16)
    low_lane = lax.broadcasted_iota(jnp.int32, (1, 128), 1) < HEAD_DIM

    head_row = lax.broadcasted_iota(jnp.int32, (8, 128), 0)
    head_lane = lax.broadcasted_iota(jnp.int32, (8, 128), 1)
    heads = jnp.where(head_row == head_lane // HEAD_DIM, 1.0, 0.0).astype(BF16)

    def attend(first, shift, full, window):
        span = round_up(window, 128)
        inside = rows_inside(shift, full, 0, window)
        queries_inside = columns_inside(shift, full, span)
        rows = pl.ds(first, window)
        wide = pl.ds(first, span)
        sums[:, :span] = jnp.transpose(lse_ref[wide, :])

        def score(n):
            p, h = divmod(n, 2)
            mine = low_lane if h == 0 else jnp.logical_not(low_lane)
            keys = jnp.where(mine, qkv_ref[PAIRS + p, rows, :].astype(F32) * SCORE_SCALE, 0.0)
            values = jnp.where(mine, qkv_ref[2 * PAIRS + p, rows, :].astype(F32), 0.0)
            scores[h, :window, :span] = mm_nt(keys.astype(BF16), qkv_ref[p, wide, :])
            grad_probs[h, :window, :span] = mm_nt(values.astype(BF16), go[p, wide, :])

        def split(values):
            low = values.astype(F32)
            halves = (jnp.where(low_lane, low, 0.0), jnp.where(low_lane, 0.0, low))
            return jnp.concatenate(halves, axis=0).astype(BF16)

        def finish(p):
            slopes = [grad_scores[(2 * p + g) % 4, :window, :span] for g in range(2)]
            weights = [probs[(2 * p + g) % 4, :window, :span] for g in range(2)]
            keys = split(qkv_ref[PAIRS + p, rows, :])
            news = (
                jnp.transpose(mm_tn(keys, jnp.concatenate(slopes, axis=0)))[:window] * SCORE_SCALE,
                mm(jnp.concatenate(slopes, axis=1), split(qkv_ref[p, wide, :])) * SCORE_SCALE,
                mm(jnp.concatenate(weights, axis=1), split(go[p, wide, :])),
            )
            for c in range(3):
                old = gqkv[c * PAIRS + p, rows, :].astype(F32)
                gqkv[c * PAIRS + p, rows, :] = jnp.where(inside, news[c], old).astype(BF16)

        score(0)
        for n in range(HEADS):
            p, h = divmod(n, 2)
            if n + 1 < HEADS:
                score(n + 1)
            if h == 0:
                lanes = slice(p * 128, (p + 1) * 128)
                product = go[p, wide, :].astype(F32) * o_ref[wide, lanes].astype(F32)
                upper = product.astype(BF16)
                lower = (product - upper.astype(F32)).astype(BF16)
                inner_rows = mm_nt(heads, upper) + mm_nt(heads, lower)
            logs = jnp.where(queries_inside, sums[n : n + 1, :span], 1e30)
            inner_row = inner_rows[h : h + 1]
            for r in range(0, window, 16):
                part = jnp.exp(scores[h, r : r + 16, :span] - logs)
                if r == 0 or r + 16 > full:
                    part = jnp.where(rows_inside(shift, full, r, 16), part, 0.0)
                probs[n % 4, r : r + 16, :span] = part.astype(BF16)
                slope = part * (grad_probs[h, r : r + 16, :span] - inner_row)
                grad_scores[n % 4, r : r + 16, :span] = slope.astype(BF16)
            if n in (2, 4):
                finish(n // 2 - 1)
        finish(PAIRS - 1)

    over_images(len_ref, tokens, attend)

    w_qkv = w_ref[:, : 3 * D]
    sums_one = (zero, zero)
    for t in range(5):
        rows = pl.ds(t * tile, tile)
        grad_qkv = jnp.concatenate([gqkv[c, rows, :] for c in range(9)], axis=1)
        wide_rows[pl.ds(place(t * tile), tile), :] = mm_nt(grad_qkv, w_qkv)

        def first_norm(at, count, carry):
            gain, bias = carry
            rows = pl.ds(at, count)
            grad_h1 = wide_rows[pl.ds(place(at), count), :]
            normal, inverse = normal_one[rows, :], thrice(inverse_one[rows, :])
            grad_x = gx1[rows, :] + norm_back(grad_h1, normal, inverse, norms[0:1])
            input_ref[rows, :] = grad_x.astype(BF16)
            return gain + fold_rows(grad_h1 * normal), bias + fold_rows(grad_h1)

        sums_one = over_rows(t * tile, (t + 1) * tile, sums_one, first_norm)
    gain_one, bias_one = sums_one
    grad = mm_tn(h1_all[...], jnp.concatenate([gqkv[c] for c in range(9)], axis=1))
    for c, (side, part) in enumerate(((0, 0), (0, 1), (1, 0))):
        put(side, part, grad[:, c * D : (c + 1) * D])
    zeros = jnp.zeros((small_rows - 4, D), F32)
    turned = [jnp.sum(one, axis=0, keepdims=True) for one in (gain_one, bias_one, gain_two, bias_two)]
    turned = jnp.concatenate(turned + [zeros], axis=0)
    gw_ref[1, :, 6 * GROUP_ROWS :, :] = pack_turned(turned)


def backward_local(lengths, first_norm, saved, result, gslots, block, experts):
    tokens = first_norm[0].shape[0]
    columns = experts * SLOT_ROWS
    kept = tokens if experts <= 16 else tokens // 5
    shape = jax.ShapeDtypeStruct
    return pl.pallas_call(
        functools.partial(backward_kernel, experts),
        out_shape=(
            shape((tokens, D), BF16),
            shape((2, GROUPS) + block, F32),
        ),
        in_specs=[pl.BlockSpec(memory_space=pltpu.SMEM)] + whole(17),
        out_specs=tuple(whole(2)),
        scratch_shapes=[
            pltpu.VMEM((kept, columns), F32),
            pltpu.VMEM((tokens, columns), BF16),
            pltpu.VMEM((tokens, D), F32),
            pltpu.VMEM((tokens, D), BF16),
            pltpu.VMEM((PAIRS, tokens + WINDOW_PAD, 128), BF16),
            pltpu.VMEM((9, tokens, 128), BF16),
            pltpu.VMEM((2, LONG_WINDOW, LONG_SPAN), F32),
            pltpu.VMEM((2, LONG_WINDOW, LONG_SPAN), F32),
            pltpu.VMEM((4, LONG_WINDOW, LONG_SPAN), BF16),
            pltpu.VMEM((4, LONG_WINDOW, LONG_SPAN), BF16),
            pltpu.VMEM((128, LONG_SPAN), F32),
            pltpu.VMEM((kept, columns), F32),
            pltpu.VMEM((kept, D), F32),
        ],
        compiler_params=pltpu.CompilerParams(vmem_limit_bytes=vmem_bytes(experts, 28)),
        name="backward_local",
    )(lengths, *first_norm, *saved, result, gslots)


def reduce_kernel(experts, gw_ref, square_ref, x1_ref, comb_ref, result_ref, attn_out, phi_out, norm_out, total_ref, block_ref, own, pair_in,
                  box_one, in_one, box_two, in_two, box_z, in_z, final, scalars, load_sem, sent,
                  pair_recv, recv_one, recv_two, recv_z, swap_sem, norm_recv):
    core, chip, first, second = ring(experts)
    rows = attn_out.shape[0]
    layers = experts // 4
    layer = chip // 4
    column = lax.rem(chip, 4)
    barrier = pltpu.get_barrier_semaphore()

    @pl.loop(1, experts)
    def _(j):
        peer = lax.rem(chip + j, experts)
        pl.semaphore_signal(barrier, inc=1, device_id=(core, peer), device_id_type=MESH)

    pl.semaphore_signal(barrier, inc=1, device_id=(1 - core, chip), device_id_type=MESH)
    load = pltpu.make_async_copy(gw_ref.at[core], own, load_sem.at[0])
    load.start()
    pl.semaphore_wait(barrier, experts)

    def send(source, target, send_sem, recv_sem, device):
        return pltpu.make_async_remote_copy(
            src_ref=source,
            dst_ref=target,
            send_sem=send_sem,
            recv_sem=recv_sem,
            device_id=device,
            device_id_type=MESH,
        )

    def pair_copy(place):
        return send(
            gw_ref.at[1 - core, :, place],
            pair_in.at[:, place],
            sent.at[0],
            pair_recv.at[place],
            (1 - core, chip),
        )

    def to_first(index):
        return send(box_one.at[index], in_one.at[index], sent.at[1], recv_one.at[index], (core, first))

    def to_second(index):
        return send(box_two.at[index], in_two.at[index], sent.at[2], recv_two.at[index], (core, second))

    def layer_at(d):
        return lax.rem(layer + 1 + d, layers)

    far = 3 - column

    both, one, two = far, lax.rem(first, 4), lax.rem(second, 4)

    for place in (both, two, one, column):
        pair_copy(place).start()

    load.wait()

    for batch, place in ((0, both), (1, one)):
        pair_copy(place).wait_recv()

        @pl.loop(0, layers)
        def _(d):
            index = batch * layers + layer_at(d)
            total = own[layer_at(d), place] + pair_in[layer_at(d), place]
            box_one[index] = total.astype(BF16)
            to_first(index).start()

    tile = x1_ref.shape[0] // 5
    for t in range(5):
        part = pl.ds(t * tile, tile)
        mixed = mm(comb_ref[part, :].astype(BF16), result_ref[...])
        block_ref[part, :] = (x1_ref[part, :] + mixed).astype(BF16)
    pair_copy(two).wait_recv()

    @pl.loop(0, layers)
    def _(d):
        index = layer_at(d)
        total = own[index, two] + pair_in[index, two]
        to_first(index).wait_recv()
        box_two[index] = (total + in_one[index].astype(F32)).astype(BF16)
        to_second(index).start()

    pair_copy(column).wait_recv()

    def to_layer(index):
        return send(
            box_z.at[index], in_z.at[layer], sent.at[3], recv_z.at[layer], (core, index * 4 + column)
        )

    def column_sum(index):
        total = own[index, column] + pair_in[index, column]
        to_first(layers + index).wait_recv()
        total = total + in_one[layers + index].astype(F32)
        to_second(index).wait_recv()
        return total + in_two[index].astype(F32)

    @pl.loop(0, layers - 1)
    def _(d):
        index = layer_at(d)
        box_z[index] = column_sum(index).astype(BF16)
        to_layer(index).start()

    final[core] = column_sum(layer)

    @pl.loop(1, layers)
    def _(d):
        index = lax.rem(layer - d + layers, layers)
        send(
            box_z.at[index], in_z.at[index], sent.at[3], recv_z.at[index], (core, index * 4 + column)
        ).wait_recv()
        final[core] += in_z[index].astype(F32)

    def swap(side):
        return send(final.at[side], final.at[side], swap_sem.at[0], swap_sem.at[1], (1 - core, chip))

    mine = final[core]
    swap(core).start()

    scalars[experts + core] = square_ref[...] + jnp.sum(mine * mine, axis=0, keepdims=True)

    def norm_pair(side):
        mine = scalars.at[experts + side]
        return send(mine, mine, swap_sem.at[2], swap_sem.at[3], (1 - core, chip))

    norm_pair(core).start()
    norm_pair(1 - core).wait_recv()
    scalars[chip] = scalars[experts] + scalars[experts + 1]

    @pl.loop(1, experts)
    def _(j):
        mine = scalars.at[chip]
        send(mine, mine, sent.at[4], norm_recv.at[0], (core, lax.rem(chip + j, experts))).start()

    swap(1 - core).wait_recv()
    for side in range(2):
        for part in range(2):
            for g in range(3):
                lanes = (side * 2 + part) * D + g * 128
                place = (2 * g + part) * rows
                attn_out[:, lanes : lanes + 128] = final[side, place : place + rows, :]
    phi_out[...] = final[0, 6 * rows : 6 * rows + experts, 0:rows]
    norm_out[...] = final[1, 6 * rows : 6 * rows + 4, 0:rows]

    others = scalars.at[pl.ds(0, experts - 1)]
    norms = send(others, others, sent.at[4], norm_recv.at[0], (1 - core, chip))
    norms.wait_recv()
    lanes = jnp.sum(scalars[0:experts], axis=0)
    total = jnp.sqrt(jnp.sum(lanes, axis=-1, keepdims=True))
    total_ref[...] = jnp.broadcast_to(total, (1, 128))
    swap(core).wait_send()
    norm_pair(core).wait_send()

    for source, sem in (
        (gw_ref.at[1 - core], 0),
        (box_one, 1),
        (box_two, 2),
        (box_z.at[pl.ds(0, layers - 1)], 3),
    ):
        send(source, source, sent.at[sem], sent.at[sem], (1 - core, chip)).wait_send()
    norms.wait_send()


def reduce_grads(grads, squares, x1, combine, result, experts):
    rows = D // experts
    layers = experts // 4
    block = grads.shape[2:]
    shape = jax.ShapeDtypeStruct
    dma = pltpu.SemaphoreType.DMA
    return pl.pallas_call(
        functools.partial(reduce_kernel, experts),
        out_shape=(
            shape((rows, 4 * D), F32),
            shape((experts, rows), F32),
            shape((4, rows), F32),
            shape((1, 128), F32),
            shape(x1.shape, BF16),
        ),
        in_specs=[pl.BlockSpec(memory_space=pl.ANY)] + whole(4),
        out_specs=tuple(whole(5)),
        scratch_shapes=[
            pltpu.VMEM((layers, 4) + block, F32),
            pltpu.VMEM((layers, 4) + block, F32),
            pltpu.VMEM((2 * layers,) + block, BF16),
            pltpu.VMEM((2 * layers,) + block, BF16),
            pltpu.VMEM((layers,) + block, BF16),
            pltpu.VMEM((layers,) + block, BF16),
            pltpu.VMEM((layers,) + block, BF16),
            pltpu.VMEM((layers,) + block, BF16),
            pltpu.VMEM((2,) + block, F32),
            pltpu.VMEM((experts + 2, 1, 128), F32),
            dma((1,)),
            dma((5,)),
            dma((4,)),
            dma((2 * layers,)),
            dma((layers,)),
            dma((layers,)),
            dma((4,)),
            dma((1,)),
        ],
        compiler_params=pltpu.CompilerParams(
            collective_id=2, has_side_effects=True, vmem_limit_bytes=vmem_bytes(experts, 16)
        ),
        name="reduce_grads",
    )(grads.reshape((2, layers, 4) + block), squares, x1, combine, result)


def adam_update(weight, first_moment, second_moment, gradient, factor, learning_rate, decay_rate):
    clipped = gradient * factor
    first_new = BETA_FIRST * first_moment + (1.0 - BETA_FIRST) * clipped
    second_new = BETA_SECOND * second_moment + (1.0 - BETA_SECOND) * clipped * clipped
    step_rate = learning_rate / (1.0 - BETA_FIRST**STEP)
    root = jnp.sqrt(second_new * (1.0 / (1.0 - BETA_SECOND**STEP)))
    weight_new = weight * (1.0 - learning_rate * decay_rate) - step_rate * (
        first_new / (root + ADAM_EPS)
    )
    return (weight_new, first_new, second_new)


RATES = (
    (1.0 / math.sqrt(D), WEIGHT_DECAY),
    (0.25 / math.sqrt(D), WEIGHT_DECAY),
    (0.8, 0.0),
    (4.0 / math.sqrt(D), WEIGHT_DECAY),
    (8.0 / math.sqrt(FF), WEIGHT_DECAY),
)
UPDATE_STEPS = 4


def update_kernel(block_ref, norm_ref, *refs):
    inputs, block_out, outputs, news, sems = refs[:20], refs[20], refs[21:36], refs[36:51], refs[51]
    grad_norm = norm_ref[...]
    factor = (CLIP_NORM / jnp.maximum(grad_norm, CLIP_NORM))[0:1, 0:1]
    copies = []

    def start(source, target):
        copies.append(pltpu.make_async_copy(source, target, sems.at[len(copies)]))
        copies[-1].start()

    for t in range(UPDATE_STEPS):
        for k in (3, 4):
            rate, decay = RATES[k]
            rows = inputs[4 * k].shape[1] // UPDATE_STEPS
            part = (0, pl.ds(t * rows, rows))
            weight, first, second, grad = (ref[part] for ref in inputs[4 * k : 4 * k + 4])
            made = adam_update(weight, first, second, grad, factor, rate, decay)
            for c in range(3):
                news[3 * k + c][part] = made[c]
                start(news[3 * k + c].at[part], outputs[3 * k + c].at[part])
        if t == 0:
            start(block_ref, block_out)
    for k in range(3):
        rate, decay = RATES[k]
        weight, first, second, grad = (ref[...] for ref in inputs[4 * k : 4 * k + 4])
        made = adam_update(weight, first, second, grad, factor, rate, decay)
        for c in range(3):
            news[3 * k + c][...] = made[c]
            start(news[3 * k + c], outputs[3 * k + c])
    for copy in copies:
        copy.wait()


def update(block_output, norm_tile, groups):
    shapes = [group[0].shape for group in groups for _ in range(3)]
    block_shape = jax.ShapeDtypeStruct(block_output.shape, BF16)
    return pl.pallas_call(
        update_kernel,
        out_shape=(block_shape,) + tuple(jax.ShapeDtypeStruct(shape, F32) for shape in shapes),
        in_specs=whole(22),
        out_specs=(pl.BlockSpec(memory_space=pl.ANY),) * 16,
        scratch_shapes=[pltpu.VMEM(shape, F32) for shape in shapes]
        + [pltpu.SemaphoreType.DMA((10 + 6 * UPDATE_STEPS,))],
        compiler_params=pltpu.CompilerParams(vmem_limit_bytes=24 * 1024 * 1024),
        name="update",
    )(block_output, norm_tile, *[array for group in groups for array in group])


def in_hbm(array):
    return pltpu.with_memory_space_constraint(array, pltpu.HBM)


def pad_to(array, shape):
    return jnp.pad(array, [(0, full - size) for size, full in zip(array.shape, shape)])


def regroup_weights(blocks, experts):
    rows = D // experts
    if rows == GROUP_ROWS:
        return blocks
    main = blocks[:, :, : 6 * rows].reshape(experts, 2, 3, 2, rows, 128).transpose(1, 2, 3, 0, 4, 5)
    main = main.reshape(2, 3, 2, GROUPS, GROUP_ROWS, 128).transpose(3, 0, 1, 2, 4, 5)
    main = main.reshape(GROUPS, 2, 6 * GROUP_ROWS, 128)
    small_rows = max(experts, 16)
    small = blocks[:, :, 6 * rows :, :rows]
    small = pad_to(small[:, :, :small_rows], (experts, 2, small_rows, rows))
    small = small.transpose(1, 2, 0, 3).reshape(2, small_rows, GROUPS, GROUP_ROWS)
    small = pad_to(small.transpose(2, 0, 1, 3), (GROUPS, 2, small_rows, 128))
    return jnp.concatenate([main, small], axis=2)


def regroup_grads(groups, experts):
    rows = D // experts
    if rows == GROUP_ROWS:
        return groups
    main = groups[:, :, : 6 * GROUP_ROWS].reshape(2, GROUPS, 3, 2, GROUP_ROWS, 128)
    main = main.transpose(0, 2, 3, 1, 4, 5).reshape(2, 3, 2, experts, rows, 128)
    main = main.transpose(0, 3, 1, 2, 4, 5).reshape(2, experts, 6 * rows, 128)
    small = groups[:, :, 6 * GROUP_ROWS :, :GROUP_ROWS]
    small_rows = min(small.shape[2], block_rows(experts) - 6 * rows)
    small = small[:, :, :small_rows].transpose(0, 2, 1, 3).reshape(2, small_rows, experts, rows)
    small = pad_to(small.transpose(0, 2, 1, 3), (2, experts, small_rows, 128))
    both = jnp.concatenate([main, small], axis=2)
    return pad_to(both, (2, experts, block_rows(experts), 128))


def local(
    patches,
    slot_len,
    attn_weight,
    attn_first,
    attn_second,
    phi_weight,
    phi_first,
    phi_second,
    norm_params,
    norm_first,
    norm_second,
    expert_in,
    in_first,
    in_second,
    expert_out,
    out_first,
    out_second,
    cotangent,
):
    experts = lax.axis_size("expert")
    weights, *first_norm = gather_weights(
        in_hbm(attn_weight), in_hbm(phi_weight.T), in_hbm(norm_params), in_hbm(patches), experts
    )
    weights = regroup_weights(weights, experts)
    *saved, packed = forward_local(
        slot_len, patches, weights, first_norm[0], in_hbm(cotangent), experts
    )
    x1, combine = saved.pop(9), saved[11]
    result, gslots, grad_in, grad_out, squares = run_experts(packed, expert_in, expert_out, experts)
    input_grad, grads = backward_local(
        slot_len, first_norm, saved, result, gslots, weights.shape[2:], experts
    )
    grads = regroup_grads(grads, experts)
    attn_part, phi_part, norm_part, norm_tile, block_output = reduce_grads(
        grads, squares, x1, combine, result, experts
    )
    block_output, *news = update(
        block_output,
        norm_tile,
        (
            (attn_weight, attn_first, attn_second, attn_part),
            (phi_weight.T, phi_first.T, phi_second.T, phi_part),
            (norm_params, norm_first, norm_second, norm_part),
            (expert_in, in_first, in_second, grad_in),
            (expert_out, out_first, out_second, grad_out),
        ),
    )
    attn_new, attn_first_new, attn_second_new = news[0:3]
    phi_new, phi_first_new, phi_second_new = (new.T for new in news[3:6])
    norm_new, norm_first_new, norm_second_new = news[6:9]
    in_new, in_first_new, in_second_new = news[9:12]
    out_new, out_first_new, out_second_new = news[12:15]
    grad_norm = norm_tile[0, 0]
    return (
        block_output,
        input_grad,
        grad_norm,
        attn_new,
        attn_first_new,
        attn_second_new,
        phi_new,
        phi_first_new,
        phi_second_new,
        norm_new,
        norm_first_new,
        norm_second_new,
        in_new,
        in_first_new,
        in_second_new,
        out_new,
        out_first_new,
        out_second_new,
    )


def solution(mesh):
    in_specs = (
        P(("batch", "expert"), None),
        P(("batch", "expert"), None),
        P("expert", None),
        P("expert", None),
        P("expert", None),
        P("expert", None),
        P("expert", None),
        P("expert", None),
        P(None, "expert"),
        P(None, "expert"),
        P(None, "expert"),
        P("expert", None, "batch"),
        P("expert", None, "batch"),
        P("expert", None, "batch"),
        P("expert", "batch", None),
        P("expert", "batch", None),
        P("expert", "batch", None),
        P(("batch", "expert"), None),
    )
    out_specs = (
        P(("batch", "expert"), None),
        P(("batch", "expert"), None),
        P(),
        P("expert", None),
        P("expert", None),
        P("expert", None),
        P("expert", None),
        P("expert", None),
        P("expert", None),
        P(None, "expert"),
        P(None, "expert"),
        P(None, "expert"),
        P("expert", None, "batch"),
        P("expert", None, "batch"),
        P("expert", None, "batch"),
        P("expert", "batch", None),
        P("expert", "batch", None),
        P("expert", "batch", None),
    )
    return jax.shard_map(local, mesh=mesh, in_specs=in_specs, out_specs=out_specs, check_vma=False)
```

```python
import functools
import math

import jax
import jax.numpy as jnp
from jax import lax
from jax.experimental import pallas as pl
from jax.experimental.pallas import tpu as pltpu
from jax.sharding import PartitionSpec as P

D = 384
HEADS = 6
HEAD_DIM = 64
FF = 1536
STEP = 3
SHORT_LEN = 196
LONG_LEN = 576
IMAGES = 5
SLOT_ROWS = 8
PAIRS = 3
GROUPS = 16
GROUP_ROWS = D // GROUPS
CHUNK = 112
LONG_WINDOW = 592
LONG_SPAN = 640
WINDOW_PAD = 48

NORM_EPS = 1e-06
CLIP_NORM = 1.0
BETA_FIRST = 0.5
BETA_SECOND = 0.5
ADAM_EPS = 1e-08
WEIGHT_DECAY = 0.05
MASKED = -1e30
SCORE_SCALE = HEAD_DIM ** (-0.5)

MESH = pl.DeviceIdType.MESH
F32 = jnp.float32
BF16 = jnp.bfloat16


def vmem_bytes(experts, mebibytes):
    return (mebibytes if experts <= 16 else 60) * 1024 * 1024


def whole(count):
    return [pl.BlockSpec(memory_space=pltpu.VMEM)] * count


def round_up(value, unit):
    return -(-value // unit) * unit


def mm(left, right):
    return jnp.dot(left, right, preferred_element_type=F32)


def mm_nt(left, right):
    return lax.dot_general(left, right, (((1,), (1,)), ((), ())), preferred_element_type=F32)


def mm_tn(left, right):
    return lax.dot_general(left, right, (((0,), (0,)), ((), ())), preferred_element_type=F32)


def block_rows(experts):
    rows = D // experts
    return round_up(6 * rows + max(experts, 4), 16)


def ring(experts):
    core = lax.axis_index("batch")
    chip = lax.axis_index("expert")
    first = chip ^ (1 + core)
    second = chip ^ (2 - core)
    return core, chip, first, second


def gather_kernel(experts, attn_hbm, phi_hbm, norm_hbm, patch_hbm, out, normal_ref, inverse_ref, patch_ref, stage, attn_ref, phi_ref, norm_ref, load_sem,
                  sent, recv):
    core, chip, first, second = ring(experts)
    rows = attn_ref.shape[0]
    half = pl.multiple_of(core * (2 * D), 128)
    loads = [
        pltpu.make_async_copy(attn_hbm.at[:, pl.ds(half, 2 * D)], attn_ref, load_sem.at[0]),
        pltpu.make_async_copy(phi_hbm, phi_ref, load_sem.at[1]),
        pltpu.make_async_copy(norm_hbm, norm_ref, load_sem.at[2]),
    ]
    for load in loads:
        load.start()
    load_patches = pltpu.make_async_copy(patch_hbm, patch_ref, load_sem.at[3])
    load_patches.start()
    column = lax.rem(chip, 4)
    layers = experts // 4
    layer = chip // 4
    barrier = pltpu.get_barrier_semaphore()

    @pl.loop(1, layers)
    def _(d):
        peer = lax.rem(layer + d, layers) * 4 + column
        pl.semaphore_signal(barrier, inc=1, device_id=(core, peer), device_id_type=MESH)

    pl.semaphore_signal(barrier, inc=1, device_id=(core, first), device_id_type=MESH)
    pl.semaphore_signal(barrier, inc=1, device_id=(core, second), device_id_type=MESH)
    pl.semaphore_signal(barrier, inc=1, device_id=(1 - core, chip), device_id_type=MESH)
    stage[...] = jnp.zeros_like(stage)
    for load in loads:
        load.wait()
    for part in range(2):
        for g in range(3):
            lanes = part * D + g * 128
            place = (2 * g + part) * rows
            stage[place : place + rows, :] = attn_ref[:, lanes : lanes + 128]

    @pl.when(core == 0)
    def _():
        stage[6 * rows : 6 * rows + experts, 0:rows] = phi_ref[...]

    @pl.when(core == 1)
    def _():
        stage[6 * rows : 6 * rows + 4, 0:rows] = norm_ref[...]

    out[chip, core] = stage[...].astype(BF16)
    pl.semaphore_wait(barrier, layers + 2)

    def copy(source, target, send_sem, recv_sem, device):
        return pltpu.make_async_remote_copy(
            src_ref=source,
            dst_ref=target,
            send_sem=send_sem,
            recv_sem=recv_sem,
            device_id=device,
            device_id_type=MESH,
        )

    def along(block, peer):
        mine = out.at[block, core]
        return copy(mine, mine, sent.at[0], recv.at[block], (core, peer))

    def to_pair(block):
        mine = out.at[block, core]
        return copy(mine, mine, sent.at[1], sent.at[2], (1 - core, chip))

    @pl.loop(1, layers)
    def _(d):
        along(chip, lax.rem(layer + d, layers) * 4 + column).start()

    along(chip, first).start()
    along(chip, second).start()
    to_pair(chip).start()

    load_patches.wait()

    def statistics(at, count, carry):
        rows = pl.ds(at, count)
        normal, inverse = normed(patch_ref[rows, :].astype(F32))
        normal_ref[rows, :] = normal
        inverse_ref[rows, :] = jnp.broadcast_to(inverse, (count, 128))
        return carry

    over_rows(0, patch_ref.shape[0], 0, statistics)

    @pl.loop(1, layers)
    def _(d):
        block = lax.rem(layer - d + layers, layers) * 4 + column
        along(block, first).wait_recv()
        along(block, first).start()
        along(block, second).start()
        to_pair(block).start()

    @pl.loop(0, layers)
    def _(d):
        block = lax.rem(layer - d + layers, layers) * 4 + lax.rem(first, 4)
        along(block, first).wait_recv()
        along(block, second).start()
        to_pair(block).start()

    @pl.loop(0, 2 * layers)
    def _(d):
        other = jnp.where(lax.rem(d, 2) == 0, lax.rem(second, 4), lax.rem(3 - column, 4))
        block = lax.rem(layer - d // 2 + layers, layers) * 4 + other
        along(block, first).wait_recv()
        to_pair(block).start()

    sides = out.at[pl.ds(0, experts - 1), core]
    copy(sides, sides, sent.at[0], sent.at[0], (1 - core, chip)).wait_send()
    copy(out.at[:, core], out.at[:, 1 - core], sent.at[1], sent.at[2], (1 - core, chip)).wait()


def gather_weights(attn_weight, phi_turned, norm_params, patches, experts):
    rows = block_rows(experts)
    tokens = patches.shape[0]
    dma = pltpu.SemaphoreType.DMA
    return pl.pallas_call(
        functools.partial(gather_kernel, experts),
        out_shape=(
            jax.ShapeDtypeStruct((experts, 2, rows, 128), BF16),
            jax.ShapeDtypeStruct((tokens, D), F32),
            jax.ShapeDtypeStruct((tokens, 128), F32),
        ),
        in_specs=[pl.BlockSpec(memory_space=pltpu.HBM)] * 4,
        out_specs=tuple(whole(3)),
        scratch_shapes=[
            pltpu.VMEM((tokens, D), BF16),
            pltpu.VMEM((rows, 128), F32),
            pltpu.VMEM((attn_weight.shape[0], 2 * D), F32),
            pltpu.VMEM(phi_turned.shape, F32),
            pltpu.VMEM(norm_params.shape, F32),
            dma((4,)),
            dma((3,)),
            dma((experts,)),
        ],
        compiler_params=pltpu.CompilerParams(
            collective_id=0, has_side_effects=True, vmem_limit_bytes=vmem_bytes(experts, 10)
        ),
        name="gather_weights",
    )(attn_weight, phi_turned, norm_params, patches)


def unpack_weight(main_ref, side, part):
    blocks = main_ref[:, side].astype(F32)
    columns = []
    for g in range(3):
        place = (2 * g + part) * GROUP_ROWS
        columns.append(blocks[:, place : place + GROUP_ROWS, :].reshape(D, 128))
    return jnp.concatenate(columns, axis=1).astype(BF16)


def group_lanes():
    lane = lax.broadcasted_iota(jnp.int32, (128, D), 0)
    column = lax.broadcasted_iota(jnp.int32, (128, D), 1)
    return jnp.where(column % GROUP_ROWS == lane, 1.0, 0.0).astype(BF16)


def unpack_turned(main_ref, side, rows):
    first = 6 * GROUP_ROWS
    blocks = main_ref[:, side].astype(F32)[:, first : first + rows, :]
    spread = mm(blocks.reshape(GROUPS * rows, 128).astype(BF16), group_lanes())
    spread = spread.reshape(GROUPS, rows, D)
    group = lax.broadcasted_iota(jnp.int32, (GROUPS, 1, D), 0)
    column = lax.broadcasted_iota(jnp.int32, (GROUPS, 1, D), 2)
    return jnp.sum(jnp.where(column // GROUP_ROWS == group, spread, 0.0), axis=0)


def pack_turned(values):
    rows = values.shape[0]
    group = lax.broadcasted_iota(jnp.int32, (GROUPS, 1, D), 0)
    column = lax.broadcasted_iota(jnp.int32, (GROUPS, 1, D), 2)
    spread = jnp.where(column // GROUP_ROWS == group, values[None], 0.0)
    spread = spread.reshape(GROUPS * rows, D).astype(BF16)
    return mm_nt(spread, group_lanes()).reshape(GROUPS, rows, 128)


def unpack_small(main_ref, experts):
    turned = unpack_turned(main_ref, 0, max(experts, 16)).astype(BF16)
    row = lax.broadcasted_iota(jnp.int32, (experts * SLOT_ROWS, turned.shape[0]), 0)
    column = lax.broadcasted_iota(jnp.int32, (experts * SLOT_ROWS, turned.shape[0]), 1)
    spread = jnp.where(column == row // SLOT_ROWS, 1.0, 0.0).astype(BF16)
    return mm(spread, turned).astype(BF16), unpack_turned(main_ref, 1, 8)


def slot_bounds(len_ref, columns):
    image = lax.broadcasted_iota(jnp.int32, (1, columns), 1) % SLOT_ROWS
    starts = jnp.zeros((1, columns), jnp.int32)
    ends = jnp.zeros((1, columns), jnp.int32)
    start = jnp.int32(0)
    for k in range(IMAGES):
        end = start + len_ref[0, k]
        starts = jnp.where(image == k, start, starts)
        ends = jnp.where(image == k, end, ends)
        start = end
    return starts, ends, start


def normed(values):
    centred = values - jnp.mean(values, axis=-1, keepdims=True)
    variance = jnp.mean(centred * centred, axis=-1, keepdims=True)
    inverse = lax.rsqrt(variance + NORM_EPS)
    return centred * inverse, inverse


def norm_back(grad_shaped, normal, inverse, scaling):
    grad_normal = grad_shaped * scaling
    return inverse * (
        grad_normal
        - jnp.mean(grad_normal, axis=-1, keepdims=True)
        - normal * jnp.mean(grad_normal * normal, axis=-1, keepdims=True)
    )


def over_rows(start, stop, carry, body):
    for at in range(start, stop, CHUNK):
        carry = body(at, min(CHUNK, stop - at), carry)
    return carry


def thrice(values):
    return jnp.concatenate([values] * 3, axis=1)


def fold_rows(values):
    return jnp.sum(values.reshape(values.shape[0] // 8, 8, values.shape[1]), axis=0)


def over_images(len_ref, tokens, body):
    def step(k, start):
        length = len_ref[0, k]
        for full in (SHORT_LEN, LONG_LEN):

            @pl.when(length == full)
            def _():
                window = round_up(full + 12, 16)
                first = jnp.minimum((start // 16) * 16, tokens - window)
                body(pl.multiple_of(first, 16), start - first, full, window)

        return start + length

    lax.fori_loop(0, IMAGES, step, jnp.int32(0))


def rows_inside(shift, full, first, count):
    row = first + lax.broadcasted_iota(jnp.int32, (count, 1), 0)
    return (row >= shift) & (row < shift + full)


def columns_inside(shift, full, count):
    column = lax.broadcasted_iota(jnp.int32, (1, count), 1)
    return (column >= shift) & (column < shift + full)


def forward_kernel(experts, len_ref, patch_ref, main_ref, norm_ref, cot_hbm, w_ref, phi_ref, norms_ref,
                   normal_ref, inverse_ref, h1_all, qkv_ref, o_ref, lse_ref, x1_ref, h2_ref, disp_ref,
                   comb_ref, gy_ref, pack_ref, logit, packf, scores,
                   probs, peaks, cot_ref, load_sem):
    load = pltpu.make_async_copy(cot_hbm, cot_ref, load_sem.at[0])
    load.start()
    tokens = patch_ref.shape[0]
    columns = experts * SLOT_ROWS
    tile = tokens // 5
    phi, norms = unpack_small(main_ref, experts)
    starts, ends, total = slot_bounds(len_ref, columns)
    norms_ref[...] = norms
    phi_ref[...] = phi
    for k in range(4):
        w_ref[:, k * D : (k + 1) * D] = unpack_weight(main_ref, k // 2, k % 2)
    w_qkv = w_ref[:, : 3 * D]

    def first_norm(at, count, carry):
        rows = pl.ds(at, count)
        h1_all[rows, :] = (norm_ref[rows, :] * norms[0:1] + norms[1:2]).astype(BF16)
        return carry

    for t in range(5):
        over_rows(t * tile, (t + 1) * tile, 0, first_norm)
        rows = pl.ds(t * tile, tile)
        qkv = mm(h1_all[rows, :], w_qkv).astype(BF16)
        for c in range(9):
            qkv_ref[c, rows, :] = qkv[:, c * 128 : (c + 1) * 128]
    qkv_ref[:, tokens:, :] = jnp.zeros((9, WINDOW_PAD, 128), BF16)
    o_ref[...] = jnp.zeros_like(o_ref)
    lse_ref[...] = jnp.zeros_like(lse_ref)
    low_lane = lax.broadcasted_iota(jnp.int32, (1, 128), 1) < HEAD_DIM
    lane = lax.broadcasted_iota(jnp.int32, (1, 128), 1)

    def attend(first, shift, full, window):
        span = round_up(window, 128)
        bias = jnp.where(columns_inside(shift, full, span), 0.0, MASKED)
        inside = rows_inside(shift, full, 0, window)
        rows = pl.ds(first, window)
        wide = pl.ds(first, span)

        ones = jnp.ones((span, 128), BF16)

        def score(n):
            p, h = divmod(n, 2)
            mine = low_lane if h == 0 else jnp.logical_not(low_lane)
            query = jnp.where(mine, qkv_ref[p, rows, :].astype(F32) * SCORE_SCALE, 0.0)
            keys = qkv_ref[PAIRS + p, wide, :]
            scores[h, :window, :span] = mm_nt(query.astype(BF16), keys)

        score(0)
        outs = []
        for n in range(HEADS):
            p, h = divmod(n, 2)
            if n + 1 < HEADS:
                score(n + 1)
            for r in range(0, window, 16):
                part = scores[h, r : r + 16, :span] + bias
                peak = jnp.max(part, axis=-1, keepdims=True)
                probs[h, r : r + 16, :span] = jnp.exp(part - peak).astype(BF16)
                peaks[h, r : r + 16, :] = jnp.broadcast_to(peak, (16, 128))
            values = jnp.concatenate([qkv_ref[2 * PAIRS + p, wide, :], ones], axis=1)
            both = mm(probs[h, :window, :span], values)
            summed = both[:, 128:]
            outs.append(both[:, :128] * (1.0 / summed))
            logs = peaks[h, :window, :] + jnp.log(summed)
            lse_ref[rows, :] = jnp.where(inside & (lane == n), logs, lse_ref[rows, :])
            if h == 1:
                lanes = slice(p * 128, (p + 1) * 128)
                old = o_ref[rows, lanes].astype(F32)
                merged = jnp.where(inside, jnp.where(low_lane, outs[n - 1], outs[n]), old)
                o_ref[rows, lanes] = merged.astype(BF16)

    over_images(len_ref, tokens, attend)

    load.wait()
    w_o = w_ref[:, 3 * D :]
    def project(t):
        rows = pl.ds(t * tile, tile)
        x1_ref[rows, :] = mm(o_ref[rows, :], w_o)

    def second_norm(at, count, carry):
        rows = pl.ds(at, count)
        x1 = patch_ref[rows, :].astype(F32) + x1_ref[rows, :]
        normal, inverse = normed(x1)
        normal_ref[rows, :] = normal
        inverse_ref[rows, :] = jnp.broadcast_to(inverse, (count, 128))
        h2_ref[rows, :] = (normal * norms[2:3] + norms[3:4]).astype(BF16)
        valid = at + lax.broadcasted_iota(jnp.int32, (count, 1), 0) < total
        x1_ref[rows, :] = jnp.where(valid, x1, 0.0)
        gy_ref[rows, :] = jnp.where(valid, cot_ref[rows, :].astype(F32), 0.0).astype(BF16)
        return carry

    project(0)
    for t in range(5):
        if t < 4:
            project(t + 1)
        over_rows(t * tile, (t + 1) * tile, 0, second_norm)
        rows = pl.ds(t * tile, tile)
        logit[rows, :] = mm_nt(h2_ref[rows, :], phi)

    def members(at, count):
        position = at + lax.broadcasted_iota(jnp.int32, (count, columns), 0)
        return (position >= starts) & (position < ends)

    def mixing(at, count, peak):
        rows = pl.ds(at, count)
        logits = logit[rows, :]
        member = members(at, count)
        exponent = jnp.exp(logits - jnp.max(logits, axis=-1, keepdims=True))
        summed = jnp.sum(exponent, axis=-1, keepdims=True) * (1.0 / SLOT_ROWS)
        comb_ref[rows, :] = jnp.where(member, exponent * (1.0 / summed), 0.0)
        inside = jnp.where(member, logits, MASKED)
        return jnp.maximum(peak, jnp.max(inside.reshape(count // 8, 8, columns), axis=0))

    peak = over_rows(0, tokens, jnp.full((8, columns), MASKED, F32), mixing)
    present = ends > starts
    peak = jnp.where(present, jnp.max(peak, axis=0, keepdims=True), 0.0)

    def exponents(at, count, summed):
        rows = pl.ds(at, count)
        member = members(at, count)
        exponent = jnp.exp(jnp.where(member, logit[rows, :] - peak, 0.0))
        exponent = jnp.where(member, exponent, 0.0)
        disp_ref[rows, :] = exponent
        return summed + fold_rows(exponent)

    summed = over_rows(0, tokens, jnp.zeros((8, columns), F32), exponents)
    summed = jnp.sum(summed, axis=0, keepdims=True) + jnp.where(present, 0.0, 1.0)
    dispatch = disp_ref[...] * (1.0 / summed)
    disp_ref[...] = dispatch
    slots = mm_tn(dispatch.astype(BF16), h2_ref[...])
    grad_result = mm_tn(comb_ref[...].astype(BF16), gy_ref[...])
    for part, matrix in enumerate((slots, grad_result)):
        pack_rows(packf, matrix.reshape(experts, SLOT_ROWS, D))
        pack_ref[:, part * 16 : (part + 1) * 16, :] = packf[...].astype(BF16)


def pack_rows(packf, blocks):
    packf[...] = jnp.zeros_like(packf)
    for c in range(3):
        packf[:, c * IMAGES : (c + 1) * IMAGES, :] = blocks[:, :IMAGES, c * 128 : (c + 1) * 128]


def unpack_rows(packf, wide):
    wide[...] = jnp.zeros_like(wide)
    for c in range(3):
        wide[:, 0:IMAGES, c * 128 : (c + 1) * 128] = packf[:, c * IMAGES : (c + 1) * IMAGES, :]


def forward_local(lengths, patches, main, normal, cotangent, experts):
    tokens = patches.shape[0]
    columns = experts * SLOT_ROWS
    shape = jax.ShapeDtypeStruct
    return pl.pallas_call(
        functools.partial(forward_kernel, experts),
        out_shape=(
            shape((D, 4 * D), BF16),
            shape((columns, D), BF16),
            shape((8, D), F32),
            shape((tokens, D), F32),
            shape((tokens, 128), F32),
            shape((tokens, D), BF16),
            shape((9, tokens + WINDOW_PAD, 128), BF16),
            shape((tokens + WINDOW_PAD, D), BF16),
            shape((tokens + WINDOW_PAD, 128), F32),
            shape((tokens, D), F32),
            shape((tokens, D), BF16),
            shape((tokens, columns), F32),
            shape((tokens, columns), F32),
            shape((tokens, D), BF16),
            shape((experts, 32, 128), BF16),
        ),
        in_specs=[pl.BlockSpec(memory_space=pltpu.SMEM)]
        + whole(3)
        + [pl.BlockSpec(memory_space=pltpu.HBM)],
        out_specs=tuple(whole(15)),
        scratch_shapes=[
            pltpu.VMEM((tokens, columns), F32),
            pltpu.VMEM((experts, 16, 128), F32),
            pltpu.VMEM((2, LONG_WINDOW, LONG_SPAN), F32),
            pltpu.VMEM((2, LONG_WINDOW, LONG_SPAN), BF16),
            pltpu.VMEM((2, LONG_WINDOW, 128), F32),
            pltpu.VMEM((tokens, D), BF16),
            pltpu.SemaphoreType.DMA((1,)),
        ],
        compiler_params=pltpu.CompilerParams(vmem_limit_bytes=vmem_bytes(experts, 24)),
        name="forward_local",
    )(lengths, patches, main, normal, cotangent)


def expert_kernel(experts, pack_ref, in_ref, out_ref, result_ref, gslot_ref, gin_ref, gout_ref,
                  square_ref, inbox, partial, given, outbox, back, packf, packe, widee, sems):
    core = lax.axis_index("batch")
    chip = lax.axis_index("expert")
    barrier = pltpu.get_barrier_semaphore()

    @pl.loop(1, experts)
    def _(j):
        peer = lax.rem(chip + j, experts)
        pl.semaphore_signal(barrier, inc=1, device_id=(core, peer), device_id_type=MESH)

    pl.semaphore_signal(barrier, inc=1, device_id=(1 - core, chip), device_id_type=MESH)
    w_in = in_ref[0].astype(BF16)
    w_out = out_ref[0].astype(BF16)
    for part in range(2):
        inbox[part, core, chip] = pack_ref[chip, part * 16 : (part + 1) * 16, :]
    pl.semaphore_wait(barrier, experts)

    def copy(source, target, sem, device):
        return pltpu.make_async_remote_copy(
            src_ref=source,
            dst_ref=target,
            send_sem=sems.at[sem],
            recv_sem=sems.at[sem + 1],
            device_id=device,
            device_id_type=MESH,
        )

    others = pl.ds(0, experts - 1)
    firsts, pairs, halves, seconds = [], [], [], []
    for part in range(2):
        block = pl.ds(part * 16, 16)

        @pl.loop(1, experts)
        def _(j):
            peer = lax.rem(chip + j, experts)
            copy(
                pack_ref.at[peer, block], inbox.at[part, core, chip], 2 * part, (core, peer)
            ).start()

        firsts.append(
            copy(pack_ref.at[others, block], inbox.at[part, core, others], 2 * part, (core, chip))
        )
        mine = inbox.at[part, core]
        pairs.append(copy(mine, mine, 4 + 2 * part, (1 - core, chip)))
        halves.append(copy(partial.at[part], given.at[part], 8 + 2 * part, (1 - core, chip)))
        seconds.append(
            copy(outbox.at[part, others], back.at[part, others], 12 + 2 * part, (core, chip))
        )

    def spread(part, side):
        packe[...] = inbox[part, side].astype(F32)
        unpack_rows(packe, widee)
        return widee[...].reshape(experts * SLOT_ROWS, D).astype(BF16)

    root = math.sqrt(2.0 / math.pi)

    def forward(side):
        slots = spread(0, side)
        hidden = mm(slots, w_in)
        bent = jnp.tanh(root * (hidden + 0.044715 * (hidden * hidden * hidden)))
        half = 0.5 * (1.0 + bent)
        act = (hidden * half).astype(BF16)
        slope = half + 0.5 * hidden * (1.0 - bent * bent) * (
            root * (1.0 + 3.0 * 0.044715 * (hidden * hidden))
        )
        return slots, act, slope, mm(act, w_out)

    def backward(side, slope):
        grads = spread(1, side)
        grad_hidden = (mm_nt(grads, w_out) * slope).astype(BF16)
        return grads, grad_hidden, mm_nt(grad_hidden, w_in)

    def give_half(part, values):
        pack_rows(packf, values.reshape(experts, SLOT_ROWS, D))
        partial[part] = packf[...].astype(BF16)
        halves[part].start()

    def send_back(part, values):
        pack_rows(packf, values.reshape(experts, SLOT_ROWS, D))
        halves[part].wait_recv()
        outbox[part] = (packf[...] + given[part].astype(F32)).astype(BF16)

        @pl.loop(1, experts)
        def _(j):
            peer = lax.rem(chip + j, experts)
            copy(outbox.at[part, peer], back.at[part, chip], 12 + 2 * part, (core, peer)).start()

        back[part, chip] = outbox[part, chip]

    firsts[0].wait_recv()
    pairs[0].start()
    pairs[0].wait_recv()
    their_slots, their_act, their_slope, their_result = forward(1 - core)
    give_half(0, their_result)
    firsts[1].wait_recv()
    pairs[1].start()
    our_slots, our_act, our_slope, our_result = forward(core)
    send_back(0, our_result)
    pairs[1].wait_recv()
    their_grads, their_hidden, their_back = backward(1 - core, their_slope)
    give_half(1, their_back)
    our_grads, our_hidden, our_back = backward(core, our_slope)
    send_back(1, our_back)
    grad_out = mm_tn(our_act, our_grads) + mm_tn(their_act, their_grads)
    gout_ref[0] = grad_out
    grad_in = mm_tn(our_slots, our_hidden) + mm_tn(their_slots, their_hidden)
    gin_ref[0] = grad_in
    squares = jnp.zeros((1, 128), F32)
    for grad in (grad_out, grad_in):
        columns = jnp.sum(grad * grad, axis=0, keepdims=True)
        for c in range(0, grad.shape[1], 128):
            squares = squares + columns[:, c : c + 128]
    square_ref[...] = squares
    for part, target in enumerate((result_ref, gslot_ref)):
        seconds[part].wait_recv()
        packe[...] = back[part].astype(F32)
        unpack_rows(packe, widee)
        target[...] = widee[...].reshape(experts * SLOT_ROWS, D).astype(BF16)
    for sent in firsts + pairs + halves + seconds:
        sent.wait_send()


def run_experts(packed, expert_in, expert_out, experts):
    shape = jax.ShapeDtypeStruct
    return pl.pallas_call(
        functools.partial(expert_kernel, experts),
        out_shape=(
            shape((experts * SLOT_ROWS, D), BF16),
            shape((experts * SLOT_ROWS, D), BF16),
            shape(expert_in.shape, F32),
            shape(expert_out.shape, F32),
            shape((1, 128), F32),
        ),
        in_specs=whole(3),
        out_specs=tuple(whole(5)),
        scratch_shapes=[
            pltpu.VMEM((2, 2, experts, 16, 128), BF16),
            pltpu.VMEM((2, experts, 16, 128), BF16),
            pltpu.VMEM((2, experts, 16, 128), BF16),
            pltpu.VMEM((2, experts, 16, 128), BF16),
            pltpu.VMEM((2, experts, 16, 128), BF16),
            pltpu.VMEM((experts, 16, 128), F32),
            pltpu.VMEM((experts, 16, 128), F32),
            pltpu.VMEM((experts, SLOT_ROWS, D), F32),
            pltpu.SemaphoreType.DMA((16,)),
        ],
        compiler_params=pltpu.CompilerParams(
            collective_id=1, has_side_effects=True, vmem_limit_bytes=vmem_bytes(experts, 8)
        ),
        name="run_experts",
    )(packed, expert_in, expert_out)


def backward_kernel(experts, len_ref, normal_one, inverse_one, w_ref, phi_ref, norms_ref, normal_two,
                    inverse_two, h1_all, qkv_ref, o_ref, lse_ref, h2_ref, disp_ref, comb_ref, gy_ref,
                    result_ref, gslot_ref, input_ref, gw_ref, gdisp, glog, gx1, branch, go, gqkv,
                    scores, grad_probs, probs, grad_scores, sums, gcomb, wide_rows):
    tokens = h2_ref.shape[0]
    columns = experts * SLOT_ROWS
    tile = tokens // 5
    phi, norms = phi_ref[...], norms_ref[...]
    result = result_ref[...]
    gslots = gslot_ref[...]

    kept = gdisp.shape[0] == tokens

    def place(at):
        return at if kept else at % tile

    inner = jnp.zeros((8, columns), F32)
    for t in range(5):
        rows = pl.ds(t * tile, tile)
        gdisp[pl.ds(place(t * tile), tile), :] = mm_nt(h2_ref[rows, :], gslots)

        def dispatch_inner(at, count, inner):
            products = disp_ref[pl.ds(at, count), :] * gdisp[pl.ds(place(at), count), :]
            return inner + fold_rows(products)

        inner = over_rows(t * tile, (t + 1) * tile, inner, dispatch_inner)
    inner = jnp.sum(inner, axis=0, keepdims=True)
    for t in range(5):
        rows = pl.ds(t * tile, tile)
        here = pl.ds(place(t * tile), tile)
        gcomb[here, :] = mm_nt(gy_ref[rows, :], result)
        if not kept:
            gdisp[here, :] = mm_nt(h2_ref[rows, :], gslots)

        def logit_grads(at, count, carry):
            rows, here = pl.ds(at, count), pl.ds(place(at), count)
            combine = comb_ref[rows, :]
            weighted = combine * gcomb[here, :]
            glog[rows, :] = (
                weighted
                - combine * jnp.sum(weighted, axis=-1, keepdims=True)
                + disp_ref[rows, :] * (gdisp[here, :] - inner)
            ).astype(BF16)
            return carry

        over_rows(t * tile, (t + 1) * tile, 0, logit_grads)
    for t in range(5):
        rows = pl.ds(t * tile, tile)
        gx1[rows, :] = mm(disp_ref[rows, :].astype(BF16), gslots) + mm(glog[rows, :], phi)

    def second_norm(at, count, carry):
        gain, bias = carry
        rows = pl.ds(at, count)
        grad_h2 = gx1[rows, :]
        normal, inverse = normal_two[rows, :], thrice(inverse_two[rows, :])
        grad_x1 = gy_ref[rows, :].astype(F32) + norm_back(grad_h2, normal, inverse, norms[2:3])
        gx1[rows, :] = grad_x1
        branch[rows, :] = grad_x1.astype(BF16)
        return gain + fold_rows(grad_h2 * normal), bias + fold_rows(grad_h2)

    zero = jnp.zeros((8, D), F32)
    w_o = w_ref[:, 3 * D :]
    sums_two = (zero, zero)
    for t in range(5):
        sums_two = over_rows(t * tile, (t + 1) * tile, sums_two, second_norm)
        rows = pl.ds(t * tile, tile)
        grad_o = mm_nt(branch[rows, :], w_o).astype(BF16)
        for c in range(PAIRS):
            go[c, rows, :] = grad_o[:, c * 128 : (c + 1) * 128]
    gain_two, bias_two = sums_two

    small_rows = gw_ref.shape[2] - 6 * GROUP_ROWS
    row = lax.broadcasted_iota(jnp.int32, (columns, small_rows), 0)
    column = lax.broadcasted_iota(jnp.int32, (columns, small_rows), 1)
    fold = jnp.where(column == row // SLOT_ROWS, 1.0, 0.0).astype(BF16)
    folded = mm(glog[...], fold).astype(BF16)
    gw_ref[0, :, 6 * GROUP_ROWS :, :] = pack_turned(mm_tn(folded, h2_ref[...]))

    def put(side, part, value):
        for g in range(3):
            place = (2 * g + part) * GROUP_ROWS
            gw_ref[side, :, place : place + GROUP_ROWS, :] = value[
                :, g * 128 : (g + 1) * 128
            ].reshape(GROUPS, GROUP_ROWS, 128)

    put(1, 1, mm_tn(o_ref[0:tokens, :], branch[...]))

    gqkv[...] = jnp.zeros_like(gqkv)
    go[:, tokens:, :] = jnp.zeros((PAIRS, WINDOW_PAD, 128), BF16)
    low_lane = lax.broadcasted_iota(jnp.int32, (1, 128), 1) < HEAD_DIM

    head_row = lax.broadcasted_iota(jnp.int32, (8, 128), 0)
    head_lane = lax.broadcasted_iota(jnp.int32, (8, 128), 1)
    heads = jnp.where(head_row == head_lane // HEAD_DIM, 1.0, 0.0).astype(BF16)

    def attend(first, shift, full, window):
        span = round_up(window, 128)
        inside = rows_inside(shift, full, 0, window)
        queries_inside = columns_inside(shift, full, span)
        rows = pl.ds(first, window)
        wide = pl.ds(first, span)
        sums[:, :span] = jnp.transpose(lse_ref[wide, :])

        def score(n):
            p, h = divmod(n, 2)
            mine = low_lane if h == 0 else jnp.logical_not(low_lane)
            keys = jnp.where(mine, qkv_ref[PAIRS + p, rows, :].astype(F32) * SCORE_SCALE, 0.0)
            values = jnp.where(mine, qkv_ref[2 * PAIRS + p, rows, :].astype(F32), 0.0)
            scores[h, :window, :span] = mm_nt(keys.astype(BF16), qkv_ref[p, wide, :])
            grad_probs[h, :window, :span] = mm_nt(values.astype(BF16), go[p, wide, :])

        def split(values):
            low = values.astype(F32)
            halves = (jnp.where(low_lane, low, 0.0), jnp.where(low_lane, 0.0, low))
            return jnp.concatenate(halves, axis=0).astype(BF16)

        def finish(p):
            slopes = [grad_scores[(2 * p + g) % 4, :window, :span] for g in range(2)]
            weights = [probs[(2 * p + g) % 4, :window, :span] for g in range(2)]
            keys = split(qkv_ref[PAIRS + p, rows, :])
            news = (
                jnp.transpose(mm_tn(keys, jnp.concatenate(slopes, axis=0)))[:window] * SCORE_SCALE,
                mm(jnp.concatenate(slopes, axis=1), split(qkv_ref[p, wide, :])) * SCORE_SCALE,
                mm(jnp.concatenate(weights, axis=1), split(go[p, wide, :])),
            )
            for c in range(3):
                old = gqkv[c * PAIRS + p, rows, :].astype(F32)
                gqkv[c * PAIRS + p, rows, :] = jnp.where(inside, news[c], old).astype(BF16)

        score(0)
        for n in range(HEADS):
            p, h = divmod(n, 2)
            if n + 1 < HEADS:
                score(n + 1)
            if h == 0:
                lanes = slice(p * 128, (p + 1) * 128)
                product = go[p, wide, :].astype(F32) * o_ref[wide, lanes].astype(F32)
                upper = product.astype(BF16)
                lower = (product - upper.astype(F32)).astype(BF16)
                inner_rows = mm_nt(heads, upper) + mm_nt(heads, lower)
            logs = jnp.where(queries_inside, sums[n : n + 1, :span], 1e30)
            inner_row = inner_rows[h : h + 1]
            for r in range(0, window, 16):
                part = jnp.exp(scores[h, r : r + 16, :span] - logs)
                if r == 0 or r + 16 > full:
                    part = jnp.where(rows_inside(shift, full, r, 16), part, 0.0)
                probs[n % 4, r : r + 16, :span] = part.astype(BF16)
                slope = part * (grad_probs[h, r : r + 16, :span] - inner_row)
                grad_scores[n % 4, r : r + 16, :span] = slope.astype(BF16)
            if n in (2, 4):
                finish(n // 2 - 1)
        finish(PAIRS - 1)

    over_images(len_ref, tokens, attend)

    w_qkv = w_ref[:, : 3 * D]
    sums_one = (zero, zero)
    for t in range(5):
        rows = pl.ds(t * tile, tile)
        grad_qkv = jnp.concatenate([gqkv[c, rows, :] for c in range(9)], axis=1)
        wide_rows[pl.ds(place(t * tile), tile), :] = mm_nt(grad_qkv, w_qkv)

        def first_norm(at, count, carry):
            gain, bias = carry
            rows = pl.ds(at, count)
            grad_h1 = wide_rows[pl.ds(place(at), count), :]
            normal, inverse = normal_one[rows, :], thrice(inverse_one[rows, :])
            grad_x = gx1[rows, :] + norm_back(grad_h1, normal, inverse, norms[0:1])
            input_ref[rows, :] = grad_x.astype(BF16)
            return gain + fold_rows(grad_h1 * normal), bias + fold_rows(grad_h1)

        sums_one = over_rows(t * tile, (t + 1) * tile, sums_one, first_norm)
    gain_one, bias_one = sums_one
    grad = mm_tn(h1_all[...], jnp.concatenate([gqkv[c] for c in range(9)], axis=1))
    for c, (side, part) in enumerate(((0, 0), (0, 1), (1, 0))):
        put(side, part, grad[:, c * D : (c + 1) * D])
    zeros = jnp.zeros((small_rows - 4, D), F32)
    turned = [jnp.sum(one, axis=0, keepdims=True) for one in (gain_one, bias_one, gain_two, bias_two)]
    turned = jnp.concatenate(turned + [zeros], axis=0)
    gw_ref[1, :, 6 * GROUP_ROWS :, :] = pack_turned(turned)


def backward_local(lengths, first_norm, saved, result, gslots, block, experts):
    tokens = first_norm[0].shape[0]
    columns = experts * SLOT_ROWS
    kept = tokens if experts <= 16 else tokens // 5
    shape = jax.ShapeDtypeStruct
    return pl.pallas_call(
        functools.partial(backward_kernel, experts),
        out_shape=(
            shape((tokens, D), BF16),
            shape((2, GROUPS) + block, F32),
        ),
        in_specs=[pl.BlockSpec(memory_space=pltpu.SMEM)] + whole(17),
        out_specs=tuple(whole(2)),
        scratch_shapes=[
            pltpu.VMEM((kept, columns), F32),
            pltpu.VMEM((tokens, columns), BF16),
            pltpu.VMEM((tokens, D), F32),
            pltpu.VMEM((tokens, D), BF16),
            pltpu.VMEM((PAIRS, tokens + WINDOW_PAD, 128), BF16),
            pltpu.VMEM((9, tokens, 128), BF16),
            pltpu.VMEM((2, LONG_WINDOW, LONG_SPAN), F32),
            pltpu.VMEM((2, LONG_WINDOW, LONG_SPAN), F32),
            pltpu.VMEM((4, LONG_WINDOW, LONG_SPAN), BF16),
            pltpu.VMEM((4, LONG_WINDOW, LONG_SPAN), BF16),
            pltpu.VMEM((128, LONG_SPAN), F32),
            pltpu.VMEM((kept, columns), F32),
            pltpu.VMEM((kept, D), F32),
        ],
        compiler_params=pltpu.CompilerParams(vmem_limit_bytes=vmem_bytes(experts, 28)),
        name="backward_local",
    )(lengths, *first_norm, *saved, result, gslots)


def reduce_kernel(experts, gw_ref, square_ref, x1_ref, comb_ref, result_ref, attn_out, phi_out, norm_out, total_ref, block_ref, own, pair_in,
                  box_one, in_one, box_two, in_two, box_z, in_z, final, scalars, load_sem, sent,
                  pair_recv, recv_one, recv_two, recv_z, swap_sem, norm_recv):
    core, chip, first, second = ring(experts)
    rows = attn_out.shape[0]
    layers = experts // 4
    layer = chip // 4
    column = lax.rem(chip, 4)
    barrier = pltpu.get_barrier_semaphore()

    @pl.loop(1, experts)
    def _(j):
        peer = lax.rem(chip + j, experts)
        pl.semaphore_signal(barrier, inc=1, device_id=(core, peer), device_id_type=MESH)

    pl.semaphore_signal(barrier, inc=1, device_id=(1 - core, chip), device_id_type=MESH)
    load = pltpu.make_async_copy(gw_ref.at[core], own, load_sem.at[0])
    load.start()
    pl.semaphore_wait(barrier, experts)

    def send(source, target, send_sem, recv_sem, device):
        return pltpu.make_async_remote_copy(
            src_ref=source,
            dst_ref=target,
            send_sem=send_sem,
            recv_sem=recv_sem,
            device_id=device,
            device_id_type=MESH,
        )

    def pair_copy(place):
        return send(
            gw_ref.at[1 - core, :, place],
            pair_in.at[:, place],
            sent.at[0],
            pair_recv.at[place],
            (1 - core, chip),
        )

    def to_first(index):
        return send(box_one.at[index], in_one.at[index], sent.at[1], recv_one.at[index], (core, first))

    def to_second(index):
        return send(box_two.at[index], in_two.at[index], sent.at[2], recv_two.at[index], (core, second))

    def layer_at(d):
        return lax.rem(layer + 1 + d, layers)

    far = 3 - column

    both, one, two = far, lax.rem(first, 4), lax.rem(second, 4)

    for place in (both, two, one, column):
        pair_copy(place).start()

    load.wait()

    for batch, place in ((0, both), (1, one)):
        pair_copy(place).wait_recv()

        @pl.loop(0, layers)
        def _(d):
            index = batch * layers + layer_at(d)
            total = own[layer_at(d), place] + pair_in[layer_at(d), place]
            box_one[index] = total.astype(BF16)
            to_first(index).start()

    tile = x1_ref.shape[0] // 5
    for t in range(5):
        part = pl.ds(t * tile, tile)
        mixed = mm(comb_ref[part, :].astype(BF16), result_ref[...])
        block_ref[part, :] = (x1_ref[part, :] + mixed).astype(BF16)
    pair_copy(two).wait_recv()

    @pl.loop(0, layers)
    def _(d):
        index = layer_at(d)
        total = own[index, two] + pair_in[index, two]
        to_first(index).wait_recv()
        box_two[index] = (total + in_one[index].astype(F32)).astype(BF16)
        to_second(index).start()

    pair_copy(column).wait_recv()

    def to_layer(index):
        return send(
            box_z.at[index], in_z.at[layer], sent.at[3], recv_z.at[layer], (core, index * 4 + column)
        )

    def column_sum(index):
        total = own[index, column] + pair_in[index, column]
        to_first(layers + index).wait_recv()
        total = total + in_one[layers + index].astype(F32)
        to_second(index).wait_recv()
        return total + in_two[index].astype(F32)

    @pl.loop(0, layers - 1)
    def _(d):
        index = layer_at(d)
        box_z[index] = column_sum(index).astype(BF16)
        to_layer(index).start()

    final[core] = column_sum(layer)

    @pl.loop(1, layers)
    def _(d):
        index = lax.rem(layer - d + layers, layers)
        send(
            box_z.at[index], in_z.at[index], sent.at[3], recv_z.at[index], (core, index * 4 + column)
        ).wait_recv()
        final[core] += in_z[index].astype(F32)

    def swap(side):
        return send(final.at[side], final.at[side], swap_sem.at[0], swap_sem.at[1], (1 - core, chip))

    mine = final[core]
    swap(core).start()

    scalars[experts + core] = square_ref[...] + jnp.sum(mine * mine, axis=0, keepdims=True)

    def norm_pair(side):
        mine = scalars.at[experts + side]
        return send(mine, mine, swap_sem.at[2], swap_sem.at[3], (1 - core, chip))

    norm_pair(core).start()
    norm_pair(1 - core).wait_recv()
    scalars[chip] = scalars[experts] + scalars[experts + 1]

    @pl.loop(1, experts)
    def _(j):
        mine = scalars.at[chip]
        send(mine, mine, sent.at[4], norm_recv.at[0], (core, lax.rem(chip + j, experts))).start()

    swap(1 - core).wait_recv()
    for side in range(2):
        for part in range(2):
            for g in range(3):
                lanes = (side * 2 + part) * D + g * 128
                place = (2 * g + part) * rows
                attn_out[:, lanes : lanes + 128] = final[side, place : place + rows, :]
    phi_out[...] = final[0, 6 * rows : 6 * rows + experts, 0:rows]
    norm_out[...] = final[1, 6 * rows : 6 * rows + 4, 0:rows]

    others = scalars.at[pl.ds(0, experts - 1)]
    norms = send(others, others, sent.at[4], norm_recv.at[0], (1 - core, chip))
    norms.wait_recv()
    lanes = jnp.sum(scalars[0:experts], axis=0)
    total = jnp.sqrt(jnp.sum(lanes, axis=-1, keepdims=True))
    total_ref[...] = jnp.broadcast_to(total, (1, 128))
    swap(core).wait_send()
    norm_pair(core).wait_send()

    for source, sem in (
        (gw_ref.at[1 - core], 0),
        (box_one, 1),
        (box_two, 2),
        (box_z.at[pl.ds(0, layers - 1)], 3),
    ):
        send(source, source, sent.at[sem], sent.at[sem], (1 - core, chip)).wait_send()
    norms.wait_send()


def reduce_grads(grads, squares, x1, combine, result, experts):
    rows = D // experts
    layers = experts // 4
    block = grads.shape[2:]
    shape = jax.ShapeDtypeStruct
    dma = pltpu.SemaphoreType.DMA
    return pl.pallas_call(
        functools.partial(reduce_kernel, experts),
        out_shape=(
            shape((rows, 4 * D), F32),
            shape((experts, rows), F32),
            shape((4, rows), F32),
            shape((1, 128), F32),
            shape(x1.shape, BF16),
        ),
        in_specs=[pl.BlockSpec(memory_space=pl.ANY)] + whole(4),
        out_specs=tuple(whole(5)),
        scratch_shapes=[
            pltpu.VMEM((layers, 4) + block, F32),
            pltpu.VMEM((layers, 4) + block, F32),
            pltpu.VMEM((2 * layers,) + block, BF16),
            pltpu.VMEM((2 * layers,) + block, BF16),
            pltpu.VMEM((layers,) + block, BF16),
            pltpu.VMEM((layers,) + block, BF16),
            pltpu.VMEM((layers,) + block, BF16),
            pltpu.VMEM((layers,) + block, BF16),
            pltpu.VMEM((2,) + block, F32),
            pltpu.VMEM((experts + 2, 1, 128), F32),
            dma((1,)),
            dma((5,)),
            dma((4,)),
            dma((2 * layers,)),
            dma((layers,)),
            dma((layers,)),
            dma((4,)),
            dma((1,)),
        ],
        compiler_params=pltpu.CompilerParams(
            collective_id=2, has_side_effects=True, vmem_limit_bytes=vmem_bytes(experts, 16)
        ),
        name="reduce_grads",
    )(grads.reshape((2, layers, 4) + block), squares, x1, combine, result)


def adam_update(weight, first_moment, second_moment, gradient, factor, learning_rate, decay_rate):
    clipped = gradient * factor
    first_new = BETA_FIRST * first_moment + (1.0 - BETA_FIRST) * clipped
    second_new = BETA_SECOND * second_moment + (1.0 - BETA_SECOND) * clipped * clipped
    step_rate = learning_rate / (1.0 - BETA_FIRST**STEP)
    root = jnp.sqrt(second_new * (1.0 / (1.0 - BETA_SECOND**STEP)))
    weight_new = weight * (1.0 - learning_rate * decay_rate) - step_rate * (
        first_new / (root + ADAM_EPS)
    )
    return (weight_new, first_new, second_new)


RATES = (
    (1.0 / math.sqrt(D), WEIGHT_DECAY),
    (0.25 / math.sqrt(D), WEIGHT_DECAY),
    (0.8, 0.0),
    (4.0 / math.sqrt(D), WEIGHT_DECAY),
    (8.0 / math.sqrt(FF), WEIGHT_DECAY),
)
UPDATE_STEPS = 8


def update_kernel(block_ref, norm_ref, *refs):
    inputs, block_out, outputs, news, sems = refs[:20], refs[20], refs[21:36], refs[36:51], refs[51]
    grad_norm = norm_ref[...]
    factor = (CLIP_NORM / jnp.maximum(grad_norm, CLIP_NORM))[0:1, 0:1]
    copies = []

    def start(source, target):
        copies.append(pltpu.make_async_copy(source, target, sems.at[len(copies)]))
        copies[-1].start()

    start(block_ref, block_out)
    for t in range(UPDATE_STEPS):
        for k in (3, 4):
            rate, decay = RATES[k]
            rows = inputs[4 * k].shape[1] // UPDATE_STEPS
            part = (0, pl.ds(t * rows, rows))
            weight, first, second, grad = (ref[part] for ref in inputs[4 * k : 4 * k + 4])
            made = adam_update(weight, first, second, grad, factor, rate, decay)
            for c in range(3):
                news[3 * k + c][part] = made[c]
                start(news[3 * k + c].at[part], outputs[3 * k + c].at[part])
    for k in range(3):
        rate, decay = RATES[k]
        weight, first, second, grad = (ref[...] for ref in inputs[4 * k : 4 * k + 4])
        made = adam_update(weight, first, second, grad, factor, rate, decay)
        for c in range(3):
            news[3 * k + c][...] = made[c]
            start(news[3 * k + c], outputs[3 * k + c])
    for copy in copies:
        copy.wait()


def update(block_output, norm_tile, groups):
    shapes = [group[0].shape for group in groups for _ in range(3)]
    block_shape = jax.ShapeDtypeStruct(block_output.shape, BF16)
    return pl.pallas_call(
        update_kernel,
        out_shape=(block_shape,) + tuple(jax.ShapeDtypeStruct(shape, F32) for shape in shapes),
        in_specs=whole(22),
        out_specs=(pl.BlockSpec(memory_space=pl.ANY),) * 16,
        scratch_shapes=[pltpu.VMEM(shape, F32) for shape in shapes]
        + [pltpu.SemaphoreType.DMA((10 + 6 * UPDATE_STEPS,))],
        compiler_params=pltpu.CompilerParams(vmem_limit_bytes=24 * 1024 * 1024),
        name="update",
    )(block_output, norm_tile, *[array for group in groups for array in group])


def in_hbm(array):
    return pltpu.with_memory_space_constraint(array, pltpu.HBM)


def pad_to(array, shape):
    return jnp.pad(array, [(0, full - size) for size, full in zip(array.shape, shape)])


def regroup_weights(blocks, experts):
    rows = D // experts
    if rows == GROUP_ROWS:
        return blocks
    main = blocks[:, :, : 6 * rows].reshape(experts, 2, 3, 2, rows, 128).transpose(1, 2, 3, 0, 4, 5)
    main = main.reshape(2, 3, 2, GROUPS, GROUP_ROWS, 128).transpose(3, 0, 1, 2, 4, 5)
    main = main.reshape(GROUPS, 2, 6 * GROUP_ROWS, 128)
    small_rows = max(experts, 16)
    small = blocks[:, :, 6 * rows :, :rows]
    small = pad_to(small[:, :, :small_rows], (experts, 2, small_rows, rows))
    small = small.transpose(1, 2, 0, 3).reshape(2, small_rows, GROUPS, GROUP_ROWS)
    small = pad_to(small.transpose(2, 0, 1, 3), (GROUPS, 2, small_rows, 128))
    return jnp.concatenate([main, small], axis=2)


def regroup_grads(groups, experts):
    rows = D // experts
    if rows == GROUP_ROWS:
        return groups
    main = groups[:, :, : 6 * GROUP_ROWS].reshape(2, GROUPS, 3, 2, GROUP_ROWS, 128)
    main = main.transpose(0, 2, 3, 1, 4, 5).reshape(2, 3, 2, experts, rows, 128)
    main = main.transpose(0, 3, 1, 2, 4, 5).reshape(2, experts, 6 * rows, 128)
    small = groups[:, :, 6 * GROUP_ROWS :, :GROUP_ROWS]
    small_rows = min(small.shape[2], block_rows(experts) - 6 * rows)
    small = small[:, :, :small_rows].transpose(0, 2, 1, 3).reshape(2, small_rows, experts, rows)
    small = pad_to(small.transpose(0, 2, 1, 3), (2, experts, small_rows, 128))
    both = jnp.concatenate([main, small], axis=2)
    return pad_to(both, (2, experts, block_rows(experts), 128))


def local(
    patches,
    slot_len,
    attn_weight,
    attn_first,
    attn_second,
    phi_weight,
    phi_first,
    phi_second,
    norm_params,
    norm_first,
    norm_second,
    expert_in,
    in_first,
    in_second,
    expert_out,
    out_first,
    out_second,
    cotangent,
):
    experts = lax.axis_size("expert")
    weights, *first_norm = gather_weights(
        in_hbm(attn_weight), in_hbm(phi_weight.T), in_hbm(norm_params), in_hbm(patches), experts
    )
    weights = regroup_weights(weights, experts)
    *saved, packed = forward_local(
        slot_len, patches, weights, first_norm[0], in_hbm(cotangent), experts
    )
    x1, combine = saved.pop(9), saved[11]
    result, gslots, grad_in, grad_out, squares = run_experts(packed, expert_in, expert_out, experts)
    input_grad, grads = backward_local(
        slot_len, first_norm, saved, result, gslots, weights.shape[2:], experts
    )
    grads = regroup_grads(grads, experts)
    attn_part, phi_part, norm_part, norm_tile, block_output = reduce_grads(
        grads, squares, x1, combine, result, experts
    )
    block_output, *news = update(
        block_output,
        norm_tile,
        (
            (attn_weight, attn_first, attn_second, attn_part),
            (phi_weight.T, phi_first.T, phi_second.T, phi_part),
            (norm_params, norm_first, norm_second, norm_part),
            (expert_in, in_first, in_second, grad_in),
            (expert_out, out_first, out_second, grad_out),
        ),
    )
    attn_new, attn_first_new, attn_second_new = news[0:3]
    phi_new, phi_first_new, phi_second_new = (new.T for new in news[3:6])
    norm_new, norm_first_new, norm_second_new = news[6:9]
    in_new, in_first_new, in_second_new = news[9:12]
    out_new, out_first_new, out_second_new = news[12:15]
    grad_norm = norm_tile[0, 0]
    return (
        block_output,
        input_grad,
        grad_norm,
        attn_new,
        attn_first_new,
        attn_second_new,
        phi_new,
        phi_first_new,
        phi_second_new,
        norm_new,
        norm_first_new,
        norm_second_new,
        in_new,
        in_first_new,
        in_second_new,
        out_new,
        out_first_new,
        out_second_new,
    )


def solution(mesh):
    in_specs = (
        P(("batch", "expert"), None),
        P(("batch", "expert"), None),
        P("expert", None),
        P("expert", None),
        P("expert", None),
        P("expert", None),
        P("expert", None),
        P("expert", None),
        P(None, "expert"),
        P(None, "expert"),
        P(None, "expert"),
        P("expert", None, "batch"),
        P("expert", None, "batch"),
        P("expert", None, "batch"),
        P("expert", "batch", None),
        P("expert", "batch", None),
        P("expert", "batch", None),
        P(("batch", "expert"), None),
    )
    out_specs = (
        P(("batch", "expert"), None),
        P(("batch", "expert"), None),
        P(),
        P("expert", None),
        P("expert", None),
        P("expert", None),
        P("expert", None),
        P("expert", None),
        P("expert", None),
        P(None, "expert"),
        P(None, "expert"),
        P(None, "expert"),
        P("expert", None, "batch"),
        P("expert", None, "batch"),
        P("expert", None, "batch"),
        P("expert", "batch", None),
        P("expert", "batch", None),
        P("expert", "batch", None),
    )
    return jax.shard_map(local, mesh=mesh, in_specs=in_specs, out_specs=out_specs, check_vma=False)
```
